32 devices in a mesh: fsdp: 8 (over y, x, core), inner: 4 (over z).
Axes of the slice: x: 2, y: 2, z: 4, core: 2. Of those that a mesh axis runs over, the one named last changes fastest.
Arguments:
- tokens: bfloat16 [32768, 1024], P(('fsdp', 'inner')), may hold values from -6 to 6
- doc_starts: int32 [32768], P(('fsdp', 'inner')), may hold values 0 or 1
- w_qkv: bfloat16 [1024, 3072], P('fsdp', 'inner'), may hold values from -0.1875 to 0.1875
- w_dense: bfloat16 [1024, 1024], P('fsdp', 'inner'), may hold values from -0.75 to 0.75
- w_up: bfloat16 [1024, 4096], P('fsdp', 'inner'), may hold values from -0.1875 to 0.1875
- w_down: bfloat16 [4096, 1024], P('fsdp', 'inner'), may hold values from -0.09375 to 0.09375
- norm1_gain: float32 [1024], P('fsdp'), may hold values from 0.5 to 1.5
- norm1_bias: float32 [1024], P('fsdp'), may hold values from -3 to 3
- norm2_gain: float32 [1024], P('fsdp'), may hold values from 0.5 to 1.5
- norm2_bias: float32 [1024], P('fsdp'), may hold values from -3 to 3
- feature_weight: float32 [1024], P('fsdp'), may hold values from 0.25 to 4
- cotangent: bfloat16 [32768, 1024], P(('fsdp', 'inner')), may hold values from -6 to 6
Outputs:
- output: bfloat16 [32768, 1024], P(('fsdp', 'inner'))
- input_grad: float32 [32768, 1024], P(('fsdp', 'inner'))
- grad_qkv: float32 [1024, 3072], P('fsdp', 'inner')
- grad_dense: float32 [1024, 1024], P('fsdp', 'inner')
- grad_up: float32 [1024, 4096], P('fsdp', 'inner')
- grad_down: float32 [4096, 1024], P('fsdp', 'inner')
- grad_gain_one: float32 [1024], P('fsdp')
- grad_bias_one: float32 [1024], P('fsdp')
- grad_gain_two: float32 [1024], P('fsdp')
- grad_bias_two: float32 [1024], P('fsdp')
- grad_feature: float32 [1024], P('fsdp')
The draws below stay inside these ranges and needn't reach their ends.
All inputs are finite; a program needn't handle non-finite values. No bound on the sum of `doc_starts` on one device may be relied on, other than what follows from the above.
Results may differ from the reference program's by a relative error of at most 0.025.
Values may be sent and summed in bfloat16 or wider, within the bound.
A program may use at most 256 MiB of HBM per device.

```python
import math
import jax
import jax.numpy as jnp
from jax import lax

D = 1024
HEADS = 16
HEAD = 64
ROT = 16
FF = 4096
FEATS = 64
BLOCK = 64
SEQ_LEN = 1024
TOKENS = 32768


def place_ends(values, rng, least, top_value):
    shape = values.shape
    spot = [jax.random.randint(jax.random.fold_in(rng, axis), (), 0, shape[axis]) for axis in range(len(shape))]
    values = values.at[tuple(spot)].set(least)
    longest = shape.index(max(shape))
    spot[longest] = (spot[longest] + 1) % shape[longest]
    return values.at[tuple(spot)].set(top_value)


def spiked(values, rng, source, target, parts, factor):
    def block_of(position):
        return (jnp.arange(values.shape[position]) // (values.shape[position] // parts)).reshape((-1,) + (1,) * (values.ndim - 1 - position))

    first = jax.random.permutation(rng, parts)[block_of(target)]
    second = (block_of(target) + parts // 2) % parts
    return jnp.where((block_of(source) == first) | (block_of(source) == second), factor * values, values)


def block_scale(stream_key, extent, cuts, smallest, largest):
    level = 1.0
    for axis_at, shards_of in cuts:
        draws = jax.random.uniform(jax.random.fold_in(jax.random.fold_in(stream_key, 6), axis_at), (shards_of,), jnp.float32, smallest / len(cuts), largest / len(cuts))
        level = level * jnp.repeat(jnp.exp(draws), extent[axis_at] // shards_of).reshape((-1,) + (1,) * (len(extent) - 1 - axis_at))
    return level


def gaussian(key, extent, deviation, reach, cuts=(), kind=jnp.bfloat16):
    factor_of = block_scale(key, extent, cuts, -0.22, 0.18) if cuts else 1.0
    values = jax.random.normal(key, extent, jnp.float32) * deviation * factor_of
    return jnp.minimum(jnp.maximum(values, -reach), reach).astype(kind)


def gaussian_with(stream_key, extent, deviation, bound, shards, heavy, held_as=jnp.bfloat16):
    entries = deviation * jax.random.normal(stream_key, extent, jnp.float32)
    if shards:
        entries = entries * block_scale(stream_key, extent, shards, -0.22, 0.18)
    return jnp.clip(spiked(entries, jax.random.fold_in(stream_key, 3), *heavy), -bound, bound).astype(held_as)


def setup_inputs(seed: int = 0) -> dict:
    keys = jax.random.split(jax.random.key(seed), 13)
    return {
        "tokens": gaussian(keys[0], (TOKENS, D), 1.0, 6.0, ((0, 32),)),
        "doc_starts": place_ends((jax.random.randint(keys[1], (TOKENS,), 0, 256) < 1).astype(jnp.int32), jax.random.fold_in(keys[1], 1), 0, 1),
        "w_qkv": gaussian(keys[2], (D, 3 * D), D ** -0.5, 0.1875, ((0, 8), (1, 4))),
        "w_dense": gaussian(keys[3], (D, D), (D // 16) ** -0.5, 0.75, ((0, 8), (1, 4))),
        "w_up": gaussian(keys[4], (D, FF), D ** -0.5, 0.1875, ((0, 8), (1, 4))),
        "w_down": gaussian(keys[5], (FF, D), FF ** -0.5, 0.09375, ((0, 8), (1, 4))),
        "norm1_gain": jnp.clip(1.0 + 0.1 * jax.random.normal(keys[6], (D,), jnp.float32), 0.5, 1.5),
        "norm1_bias": gaussian(keys[7], (D,), 0.5, 3.0, ((0, 8),), jnp.float32),
        "norm2_gain": jnp.clip(1.0 + 0.1 * jax.random.normal(keys[8], (D,), jnp.float32), 0.5, 1.5),
        "norm2_bias": gaussian(keys[9], (D,), 0.5, 3.0, ((0, 8),), jnp.float32),
        "feature_weight": jnp.clip(jnp.exp(math.log(4.0) - 2.7725887 * jax.random.uniform(keys[10], (HEADS * FEATS,), jnp.float32) ** block_scale(keys[10], (HEADS * FEATS,), ((0, 8),), -0.2, 0.2)), 0.25, 4.0),
        "cotangent": gaussian_with(keys[11], (TOKENS, D), 1.0, 6.0, ((0, 32),), (0, 1, 32, 2.75)),
    }


@jax.custom_vjp
def low(v):
    return lax.optimization_barrier(v.astype(jnp.bfloat16)).astype(jnp.float32)

@jax.custom_vjp
def low_back(v):
    return v

def low_keep(v):
    return (low(v), None)

def low_pass(kept, grad):
    return (grad,)

def back_keep(v):
    return (v, None)

def back_low(kept, grad):
    return (low(grad),)
low.defvjp(low_keep, low_pass)
low_back.defvjp(back_keep, back_low)
PRECISION_BEST = lax.Precision.HIGHEST

def layer_norm(values, gain, bias):
    center = values - lax.optimization_barrier(jnp.mean(values, axis=-1, keepdims=True))
    spread = lax.optimization_barrier(jnp.mean(center * center, axis=-1, keepdims=True))
    return center * lax.rsqrt(spread + 1e-05) * gain + bias

def rotary_tables():
    places = jnp.arange(SEQ_LEN, dtype=jnp.float32)
    powers = jnp.arange(0, ROT, 2, dtype=jnp.float32) / ROT
    freqs = 1.0 / 10000.0 ** powers
    angles = places[:, None] * freqs[None, :]
    cosine_pos = jnp.concatenate([jnp.cos(angles), jnp.cos(angles)], axis=-1)
    sine_pos = jnp.concatenate([jnp.sin(angles), jnp.sin(angles)], axis=-1)
    return (cosine_pos, sine_pos)

def feature_tables():
    order_k = jnp.arange(HEAD, dtype=jnp.int32)[:, None]
    order_i = jnp.arange(HEAD, dtype=jnp.int32)[None, :]
    waves = jnp.cos(math.pi * (order_i.astype(jnp.float32) + 0.5) * order_k.astype(jnp.float32) / HEAD)
    cosine = jnp.where(order_k == 0, math.sqrt(1.0 / HEAD), math.sqrt(2.0 / HEAD)) * waves
    points = jnp.arange(FEATS, dtype=jnp.int32)[None, :]
    lattice = (points * (2 * order_k + 1) + order_k) % FEATS
    levels = (lattice.astype(jnp.float32) + 0.5) / FEATS
    normals = math.sqrt(2.0) * lax.erf_inv(2.0 * levels - 1.0)
    return jnp.dot(cosine.T, normals, precision=PRECISION_BEST) / math.sqrt(HEAD)

def rotary(heads_in, cosine_pos, sine_pos):
    turning = heads_in[..., :ROT]
    resting = heads_in[..., ROT:]
    middle_split = ROT // 2
    swapped = jnp.concatenate([-turning[..., middle_split:], turning[..., :middle_split]], axis=-1)
    turned = turning * cosine_pos[:, None, :] + swapped * sine_pos[:, None, :]
    return jnp.concatenate([turned, resting], axis=-1)

def attend(query_feat, key_feat, values, doc):
    blocks = SEQ_LEN // BLOCK
    query_blocks = query_feat.reshape(blocks, BLOCK, HEADS, FEATS)
    key_blocks = key_feat.reshape(blocks, BLOCK, HEADS, FEATS)
    value_blocks = values.reshape(blocks, BLOCK, HEADS, HEAD)
    doc_blocks = doc.reshape(blocks, BLOCK)
    causal_mask = jnp.arange(BLOCK)[:, None] >= jnp.arange(BLOCK)[None, :]

    def advance(carry, piece):
        running_key_state, key_total, state_doc = carry
        query_slice, key_slice, value_portion, doc_part = piece
        doc_last = doc_part[BLOCK - 1]
        permitted_mask = ((doc_part[:, None] == doc_part[None, :]) & causal_mask).astype(jnp.float32)
        attention_scores = jnp.einsum('esz,jsz->sej', query_slice, key_slice, precision=PRECISION_BEST) * permitted_mask[None]
        carried = (doc_part == state_doc).astype(jnp.float32)
        numerator = jnp.einsum('hqk,khe->qhe', attention_scores, value_portion, precision=PRECISION_BEST)
        numerator = numerator + carried[:, None, None] * jnp.einsum('qhf,hfe->qhe', query_slice, running_key_state, precision=PRECISION_BEST)
        denominator = lax.optimization_barrier(jnp.sum(attention_scores, axis=2)).T
        denominator = denominator + carried[:, None] * jnp.einsum('qhf,hf->qh', query_slice, key_total, precision=PRECISION_BEST)
        result = numerator / denominator[:, :, None]
        remains_visible = (state_doc == doc_last).astype(jnp.float32)
        trailing_keys = key_slice * (doc_part == doc_last).astype(jnp.float32)[:, None, None]
        running_key_state = remains_visible * running_key_state + jnp.einsum('bcm,bcn->cmn', trailing_keys, value_portion, precision=PRECISION_BEST)
        key_total = remains_visible * key_total + lax.optimization_barrier(jnp.sum(trailing_keys, axis=0))
        return ((running_key_state, key_total, doc_last.astype(jnp.int32)), result)
    start_state = (jnp.zeros((HEADS, FEATS, HEAD), jnp.float32), jnp.zeros((HEADS, FEATS), jnp.float32), jnp.array(-1, dtype=jnp.int32))
    unused_state, results = lax.scan(jax.checkpoint(advance), start_state, (query_blocks, key_blocks, value_blocks, doc_blocks))
    return results.reshape(SEQ_LEN, HEADS, HEAD)

def attention_core(projected, feature_weight, doc, cosine_pos, sine_pos, mixing_matrix):
    rows_here = projected.shape[0]
    seq_count = rows_here // SEQ_LEN
    queries = projected[:, :D].reshape(seq_count, SEQ_LEN, HEADS, HEAD)
    keys_all = projected[:, D:2 * D].reshape(seq_count, SEQ_LEN, HEADS, HEAD)
    values_all = projected[:, 2 * D:].reshape(seq_count, SEQ_LEN, HEADS, HEAD)
    weights_hf = feature_weight.reshape(HEADS, FEATS)
    query_feat = low(weights_hf * jnp.exp(jnp.einsum('slhe,ef->slhf', rotary(queries, cosine_pos, sine_pos), mixing_matrix, precision=PRECISION_BEST)))
    key_feat = low(weights_hf * jnp.exp(jnp.einsum('slhe,ef->slhf', rotary(keys_all, cosine_pos, sine_pos), mixing_matrix, precision=PRECISION_BEST)))
    values_low = low(values_all)
    attended = jax.vmap(attend)(query_feat, key_feat, values_low, doc)
    return attended.reshape(rows_here, D)

def block_forward(inputs, doc, tables, w_qkv, w_dense, w_up, w_down, norm1_gain, norm1_bias, norm2_gain, norm2_bias, feature_weight):
    cosine_pos, sine_pos, mixing_matrix = tables
    attn_in = low(layer_norm(inputs, norm1_gain, norm1_bias))
    mlp_in = low(layer_norm(inputs, norm2_gain, norm2_bias))
    projected = low_back(jnp.dot(attn_in, w_qkv, precision=PRECISION_BEST))
    attended = attention_core(projected, feature_weight, doc, cosine_pos, sine_pos, mixing_matrix)
    mixed_low = low(low_back(attended))
    attn_branch = jnp.dot(mixed_low, w_dense, precision=PRECISION_BEST)
    hidden_pre = low_back(jnp.dot(mlp_in, w_up, precision=PRECISION_BEST))
    hidden_low = low(jax.nn.gelu(hidden_pre, approximate=False))
    mlp_branch = jnp.dot(hidden_low, w_down, precision=PRECISION_BEST)
    return inputs + attn_branch + mlp_branch

def reference(tokens, doc_starts, w_qkv, w_dense, w_up, w_down, norm1_gain, norm1_bias, norm2_gain, norm2_bias, feature_weight, cotangent):
    params = (w_qkv.astype(jnp.float32), w_dense.astype(jnp.float32), w_up.astype(jnp.float32), w_down.astype(jnp.float32), norm1_gain.astype(jnp.float32), norm1_bias.astype(jnp.float32), norm2_gain.astype(jnp.float32), norm2_bias.astype(jnp.float32), feature_weight.astype(jnp.float32))
    cosine_pos, sine_pos = rotary_tables()
    tables = (cosine_pos, sine_pos, feature_tables())
    seqs_total = TOKENS // SEQ_LEN
    group_seqs = 4 if seqs_total % 4 == 0 else 1
    count_of_groups = seqs_total // group_seqs
    group_rows = group_seqs * SEQ_LEN
    token_groups = tokens.reshape(count_of_groups, group_rows, D)
    start_groups = doc_starts.reshape(count_of_groups, group_seqs, SEQ_LEN)
    cot_groups = cotangent.reshape(count_of_groups, group_rows, D)

    def one_group(summed, group_item):
        token_part, start_part, cot_part = group_item
        doc = jnp.cumsum(start_part, axis=1).astype(jnp.int32)

        def forward_here(inputs, *weights):
            return block_forward(inputs, doc, tables, *weights)
        result, pullback = jax.vjp(forward_here, token_part.astype(jnp.float32), *params)
        gradients = pullback(cot_part.astype(jnp.float32))
        summed = tuple((total + piece for total, piece in zip(summed, gradients[1:])))
        return (summed, (result.astype(jnp.bfloat16), gradients[0]))
    start_sums = tuple((jnp.zeros_like(weight) for weight in params))
    summed, (outputs, input_grads) = lax.scan(one_group, start_sums, (token_groups, start_groups, cot_groups))
    return (outputs.reshape(TOKENS, D), input_grads.reshape(TOKENS, D), summed[0], summed[1], summed[2], summed[3], summed[4], summed[5], summed[6], summed[7], summed[8])
```

```python
from functools import partial
import math
from statistics import NormalDist

import jax
import jax.numpy as jnp
import numpy as np
from jax import lax
from jax.experimental import pallas as pl
from jax.experimental.pallas import tpu as pltpu
from jax.sharding import PartitionSpec as P

MESH = pl.DeviceIdType.MESH
BF16 = jnp.bfloat16
F32 = jnp.float32


HEAD = 64
ROT = 16
FEATS = 64
SEQ_LEN = 1024

class Place:
    def __init__(self, nf, nz):
        self.nf, self.nz = nf, nz
        self.nbits = (nf // 2).bit_length() - 1
        self.f = lax.axis_index("fsdp")
        self.z = lax.axis_index("inner")
        self.core = lax.rem(self.f, 2)
        self.bits = [lax.rem(lax.div(self.f, 2 << b), 2) for b in range(self.nbits)]

    def partner(self):
        return (self.f + 1 - 2 * self.core, self.z)

    def across(self, b):
        return (self.f + (1 - 2 * self.bits[b]) * (2 << b), self.z)

    def along(self, step):
        return (self.f, self.z + step)

    def slot(self, done, flip=None):
        index = []
        for b in reversed(range(self.nbits)):
            if b in done:
                index.append(slice(None))
            elif b == flip:
                index.append(1 - self.bits[b])
            else:
                index.append(self.bits[b])
        return tuple(index)

    def columns(self, buf, zsel):
        if zsel is None:
            return slice(None)
        width = buf.shape[-1] // self.nz
        return pl.ds(pl.multiple_of(zsel * width, width), width)

    def greet(self, far=False):
        bar = pltpu.get_barrier_semaphore()
        z, nz = self.z, self.nz
        fixed = [self.partner()] + [self.across(b) for b in range(self.nbits)]
        for peer in fixed:
            pl.semaphore_signal(bar, inc=1, device_id=peer, device_id_type=MESH)

        @pl.when(z > 0)
        def _():
            pl.semaphore_signal(bar, inc=1, device_id=self.along(-1), device_id_type=MESH)

        @pl.when(z < nz - 1)
        def _():
            pl.semaphore_signal(bar, inc=1, device_id=self.along(1), device_id_type=MESH)

        count = len(fixed)
        if far and nz > 2:
            step = 2
            while step < nz:
                pl.semaphore_signal(
                    bar, inc=1, device_id=self.fold(step), device_id_type=MESH
                )
                count += 1
                step *= 2
        inner = (z > 0).astype(jnp.int32) + (z < nz - 1).astype(jnp.int32)
        pl.semaphore_wait(bar, count + inner)

    def fold(self, step):
        bit = lax.rem(lax.div(self.z, step), 2)
        return (self.f, self.z + (1 - 2 * bit) * step)


class Sems:
    def __init__(self, send, recv):
        self.send, self.recv, self.count = send, recv, 0

    def take(self):
        self.count += 1
        return self.count - 1

    def copy(self, src, dst, i, peer):
        return pltpu.make_async_remote_copy(
            src_ref=src,
            dst_ref=dst,
            send_sem=self.send.at[i],
            recv_sem=self.recv.at[i],
            device_id=peer,
            device_id_type=MESH,
        )


def shares(rows):
    units = rows // 16
    last = units // 4
    first = (units - last + 1) // 2
    sizes = [first * 16, (units - last - first) * 16, last * 16]
    starts = [0, sizes[0], sizes[0] + sizes[1]]
    return list(zip(starts, sizes))


def orders(nbits):
    up, down = list(range(nbits)), list(reversed(range(nbits)))
    return [["z"] + up, ["z"] + down, up + ["z"]]


def copies_of(nz, nbits):
    return nbits + 2 * (nz - 1)


def gather_stream(at, sems, buf, start, size, order):
    rows = pl.ds(start, size)
    rounds = []
    done, zdone = (), False

    def along(k, done):
        ids = (sems.take(), sems.take())

        def right(zsel):
            ref = buf.at[at.slot(done) + (rows, at.columns(buf, zsel))]
            return sems.copy(ref, ref, ids[0], at.along(1))

        def left(zsel):
            ref = buf.at[at.slot(done) + (rows, at.columns(buf, zsel))]
            return sems.copy(ref, ref, ids[1], at.along(-1))

        z, nz = at.z, at.nz
        goes_right = (z < nz - 1) & (z - k + 1 >= 0)
        goes_left = (z > 0) & (z + k - 1 <= nz - 1)

        def send():
            pl.when(goes_right)(lambda: right(z - k + 1).start())
            pl.when(goes_left)(lambda: left(z + k - 1).start())

        def arrive():
            pl.when(z - k >= 0)(lambda: right(z - k).wait_recv())
            pl.when(z + k <= nz - 1)(lambda: left(z + k).wait_recv())

        def leave():
            pl.when(goes_right)(lambda: right(z - k + 1).wait_send())
            pl.when(goes_left)(lambda: left(z + k - 1).wait_send())

        return send, arrive, leave

    def across(b, done, zsel):
        i = sems.take()
        mine = buf.at[at.slot(done) + (rows, at.columns(buf, zsel))]
        theirs = buf.at[at.slot(done, flip=b) + (rows, at.columns(buf, zsel))]
        out = sems.copy(mine, mine, i, at.across(b))
        back = sems.copy(theirs, theirs, i, at.across(b))
        return out.start, back.wait_recv, out.wait_send

    for dim in order:
        if dim == "z":
            rounds += [along(k, done) for k in range(1, at.nz)]
            zdone = True
        else:
            rounds.append(across(dim, done, None if zdone else at.z))
            done = done + (dim,)
    return rounds


def scatter_stream(at, sems, acc, holds, start, size, order):
    rows = pl.ds(start, size)
    rounds = []
    left_bits, zleft = set(range(at.nbits)), True

    def along(k, remaining, hold):
        ids = (sems.take(), sems.take())
        z, nz = at.z, at.nz

        def part(zsel):
            return acc.at[at.slot(remaining) + (rows, at.columns(acc, zsel))]

        def right(zsel):
            return sems.copy(part(zsel), hold.at[2 * k - 2], ids[0], at.along(1))

        def left(zsel):
            return sems.copy(part(zsel), hold.at[2 * k - 1], ids[1], at.along(-1))

        goes_right = z + k <= nz - 1
        goes_left = z - k >= 0

        def send():
            pl.when(goes_right)(lambda: right(z + k).start())
            pl.when(goes_left)(lambda: left(z - k).start())

        def arrive():
            @pl.when((z >= 1) & (z - 1 + k <= nz - 1))
            def _():
                right(z - 1 + k).wait_recv()
                ref = part(z - 1 + k)
                ref[...] += hold[2 * k - 2]

            @pl.when((z <= nz - 2) & (z + 1 - k >= 0))
            def _():
                left(z + 1 - k).wait_recv()
                ref = part(z + 1 - k)
                ref[...] += hold[2 * k - 1]

        def leave():
            pl.when(goes_right)(lambda: right(z + k).wait_send())
            pl.when(goes_left)(lambda: left(z - k).wait_send())

        return send, arrive, leave

    def across(b, remaining, zsel, hold):
        i = sems.take()
        out = sems.copy(
            acc.at[at.slot(remaining, flip=b) + (rows, at.columns(acc, zsel))], hold, i, at.across(b)
        )

        def arrive():
            out.wait_recv()
            ref = acc.at[at.slot(remaining) + (rows, at.columns(acc, zsel))]
            ref[...] += hold[...]

        return out.start, arrive, out.wait_send

    holds = iter(holds)
    for dim in reversed(order):
        if dim == "z":
            hold = next(holds)
            rounds += [along(k, tuple(left_bits), hold) for k in range(at.nz - 1, 0, -1)]
            zleft = False
        else:
            left_bits = left_bits - {dim}
            rounds.append(across(dim, tuple(left_bits), None if zleft else at.z, next(holds)))
    return rounds


def hold_shapes(nz, nbits, size, width, order):
    shapes, bits, zleft = [], nbits, True
    for dim in reversed(order):
        if dim == "z":
            shapes.append((2 * (nz - 1),) + (2,) * bits + (size, width // nz))
            zleft = False
        else:
            bits -= 1
            shapes.append((2,) * bits + (size, width if zleft else width // nz))
    return shapes


def gather_kernel(nf, nz, tok, cot, doc, vec, wq, wd, wu, ww,
                  tok2, cot2, doc2, vecs, bq, bd, bu, bw, send, recv, local):
    at = Place(nf, nz)
    sems = Sems(send, recv)
    c, o = at.core, 1 - at.core
    me = at.slot(())
    col = lambda b: at.columns(b, at.z)
    at.greet()
    nlocal = [0]

    def put(src, dst):
        cp = pltpu.make_async_copy(src, dst, local.at[nlocal[0]])
        nlocal[0] += 1
        cp.start()
        return cp

    def swap(src, dst, arrives):
        i = sems.take()
        cp = sems.copy(src, dst, i, at.partner())
        cp.start()
        return cp, sems.copy(src, arrives, i, at.partner())

    rq, ru = wq.shape[1], wu.shape[1]
    mine = lambda r: pl.ds(pl.multiple_of(c * r, r), r)
    other = lambda r: pl.ds(pl.multiple_of(o * r, r), r)
    pairs = [
        swap(wq.at[o], bq.at[me + (mine(rq), col(bq))], bq.at[me + (other(rq), col(bq))]),
        swap(wu.at[o], bu.at[me + (mine(ru), col(bu))], bu.at[me + (other(ru), col(bu))]),
        swap(vec, vecs.at[me + (c,)], vecs.at[me + (o,)]),
        swap(doc, doc2.at[c], doc2.at[o]),
        swap(tok, tok2.at[c], tok2.at[o]),
        swap(cot, cot2.at[c], cot2.at[o]),
    ]
    locals_ = [
        put(wq.at[c], bq.at[me + (mine(rq), col(bq))]),
        put(wd, bd.at[me + (slice(None), col(bd))]),
        put(wu.at[c], bu.at[me + (mine(ru), col(bu))]),
        put(ww, bw.at[me + (slice(None), col(bw))]),
        put(vec, vecs.at[me + (c,)]),
        put(doc, doc2.at[c]),
        put(tok, tok2.at[c]),
        put(cot, cot2.at[c]),
    ]
    streams = []
    for buf in (bq, bd, bu, bw):
        for (start, size), order in zip(shares(buf.shape[-2]), orders(at.nbits)):
            if size:
                streams.append(gather_stream(at, sems, buf, start, size, order))
    small = []
    done = []
    for b in range(at.nbits):
        i = sems.take()
        m = vecs.at[at.slot(done)]
        t = vecs.at[at.slot(done, flip=b)]
        small.append((sems.copy(m, m, i, at.across(b)), sems.copy(t, t, i, at.across(b))))
        done = done + [b]
    for k in range(4):
        locals_[k].wait()
    pairs[0][1].wait_recv()
    pairs[1][1].wait_recv()
    for s in streams:
        s[0][0]()
    locals_[4].wait()
    pairs[2][1].wait_recv()
    for out, back in small:
        out.start()
        back.wait_recv()
    n = len(streams[0])
    for r in range(n):
        for s in streams:
            s[r][1]()
            if r + 1 < n:
                s[r + 1][0]()
    for k in range(5, 8):
        locals_[k].wait()
    for k in range(3, 6):
        pairs[k][1].wait_recv()
    for out, back in pairs:
        out.wait_send()
    for out, back in small:
        out.wait_send()
    for s in streams:
        for r in s:
            r[2]()

def gather(nf, nz, tok, cot, doc, vec, wq, wd, wu, ww):
    bits = (2,) * ((nf // 2).bit_length() - 1)
    nb = len(bits)
    sd = jax.ShapeDtypeStruct
    outs = [
        sd((2,) + tok.shape, BF16), sd((2,) + cot.shape, BF16), sd((2,) + doc.shape, doc.dtype),
        sd(bits + (2,) + vec.shape, F32),
        sd(bits + (2 * wq.shape[1], nz * wq.shape[2]), BF16),
        sd(bits + (wd.shape[0], nz * wd.shape[1]), BF16),
        sd(bits + (2 * wu.shape[1], nz * wu.shape[2]), BF16),
        sd(bits + (ww.shape[0], nz * ww.shape[1]), BF16),
    ]
    n = 6 + nb + 12 * copies_of(nz, nb)
    return pl.pallas_call(
        partial(gather_kernel, nf, nz), out_shape=outs,
        in_specs=[pl.BlockSpec(memory_space=pl.ANY)] * 8,
        out_specs=[pl.BlockSpec(memory_space=pl.ANY)] * 8,
        scratch_shapes=[pltpu.SemaphoreType.DMA((n,)), pltpu.SemaphoreType.DMA((n,)), pltpu.SemaphoreType.DMA((8,))],
        compiler_params=pltpu.CompilerParams(collective_id=0, has_side_effects=True),
        name="gather",
    )(tok, cot, doc, vec, wq, wd, wu, ww)


CH = 256

def dot(a, b):
    return jnp.dot(a, b, preferred_element_type=F32)

def dot_nt(a, b):
    return lax.dot_general(a, b, (((1,), (1,)), ((), ())), preferred_element_type=F32)

def dot_tn(a, b):
    return lax.dot_general(a, b, (((0,), (0,)), ((), ())), preferred_element_type=F32)

def tile(i, n):
    return pl.ds(pl.multiple_of(i * n, n), n)

def loop(n, body):
    lax.fori_loop(0, n, lambda i, _: (body(i), 0)[1], 0)

def lanes(width):
    return lax.broadcasted_iota(jnp.int32, (1, width), 1)

def normed(x):
    center = x - jnp.mean(x, axis=-1, keepdims=True)
    spread = jnp.mean(center * center, axis=-1, keepdims=True)
    rstd = lax.rsqrt(spread + 1e-05)
    return center * rstd, rstd

def attention_kernel(head, rot, tok, cot, vec, fw, wq, wd, mask, carr, trail, keep, cosp, sina, sinb, mixh, mixl, mixt,
                     mlp_in, o, pg, gq, gd, gf, dy1,
                     attn_in, qf, kf, vv, dd, do, st, cur):
    T = tok.shape[0]
    width = qf.shape[1]
    npair = width // 128
    seq = cosp.shape[0]
    nch = T // CH
    half = rot // 2

    def ln(i):
        r = tile(i, CH)
        n, _ = normed(tok[r, :].astype(F32))
        attn_in[r, :] = (n * vec[0:1, :] + vec[1:2, :]).astype(BF16)
        mlp_in[r, :] = (n * vec[2:3, :] + vec[3:4, :]).astype(BF16)
    loop(nch, ln)

    RT = 512
    def project(i):
        r = tile(i, RT)
        p = tile(lax.rem(i, seq // RT), RT)
        a = attn_in[r, :]
        for part, dst in ((0, qf), (1, kf)):
            x = dot(a, wq[:, part * width:(part + 1) * width])
            for m in range(npair):
                s = slice(m * 128, (m + 1) * 128)
                y = x[:, s]
                y = y * cosp[p, :] + pltpu.roll(y, half, 1) * sina[p, :] + pltpu.roll(y, 128 - half, 1) * sinb[p, :]
                hi = y.astype(BF16)
                lo = (y - hi.astype(F32)).astype(BF16)
                e = dot(hi, mixh[...]) + dot(lo, mixh[...]) + dot(hi, mixl[...])
                dst[r, s] = (fw[:, s] * jnp.exp(e)).astype(BF16)
        vv[r, :] = dot(a, wq[:, 2 * width:3 * width]).astype(BF16)
        do[r, :] = dot_nt(cot[r, :], wd[...]).astype(BF16)
    loop(T // RT, project)

    h0 = (lanes(128) % (2 * head)) < head
    h0w = jnp.concatenate([h0, h0], axis=1)
    rowh = (lax.broadcasted_iota(jnp.int32, (128, 1), 0)) < head
    block = rowh == h0w
    same = (rowh == h0).astype(BF16)
    one = jnp.ones((CH, 128), BF16)
    zero = jnp.zeros((), BF16)

    def scores(q, k, v, m):
        s0 = dot_nt(jnp.where(h0, q, zero), k)
        s1 = dot_nt(jnp.where(h0, zero, q), k)
        return (s0 * m).astype(BF16), (s1 * m).astype(BF16)

    cur[...] = jnp.zeros_like(cur)
    place = lanes(128) % head

    def split(x):
        hi = x.astype(BF16)
        return hi, (x - hi.astype(F32)).astype(BF16)

    def forward(i):
        r = tile(i, CH)
        m = mask[r, :].astype(F32)
        cw = jnp.concatenate([carr[r, :], carr[r, :]], axis=1)
        tr = trail[r, :]
        kp = keep[i]
        kpw = jnp.concatenate([kp, kp], axis=1)
        for j in range(npair):
            s = slice(j * 128, (j + 1) * 128)
            q, k, v = qf[r, s], kf[r, s], vv[r, s]
            va = jnp.concatenate([v, one], axis=1)
            p0, p1 = scores(q, k, v, m)
            state = cur[j]
            hi, lo = split(state)
            st[i, j, 0] = hi
            st[i, j, 1] = lo
            res = dot(p0, jnp.where(h0w, va, zero)) + dot(p1, jnp.where(h0w, zero, va)) + cw * (dot(q, hi) + dot(q, lo))
            rd = 1.0 / res[:, 128:]
            att = res[:, :128] * rd
            o[r, s] = att.astype(BF16)
            dnb = (do[r, s].astype(F32) * rd).astype(BF16)
            do[r, s] = dnb
            hi, lo = split(dnb.astype(F32) * att)
            hi, lo = split(-(dot(hi, same) + dot(lo, same)))
            dd[r, s] = jnp.where(place == 0, hi, jnp.where(place == 1, lo, zero))
            kt = (k.astype(F32) * tr).astype(BF16)
            cur[j] = kpw * state + jnp.where(block, dot_tn(kt, va), 0.0)
    loop(nch, forward)

    cur[...] = jnp.zeros_like(cur)
    gf[...] = jnp.zeros_like(gf)

    def backward(ii):
        i = nch - 1 - ii
        r = tile(i, CH)
        p = tile(lax.rem(i, seq // CH), CH)
        m = mask[r, :].astype(F32)
        cr, tr = carr[r, :], trail[r, :]
        kp = keep[i]
        kpw = jnp.concatenate([kp, kp], axis=1)
        cos, sa, sb = cosp[p, :], sina[p, :], sinb[p, :]

        def unfeature(d, f, s, base):
            de = d * f.astype(F32)
            gf[:, s] += jnp.sum(de.reshape(CH // 8, 8, 128), axis=0)
            g = dot(de.astype(BF16), mixt[...])
            g = g * cos + pltpu.roll(g * sa, 128 - half, 1) + pltpu.roll(g * sb, half, 1)
            pg[r, base + s.start:base + s.stop] = g.astype(BF16)

        for j in range(npair):
            s = slice(j * 128, (j + 1) * 128)
            q, k, v = qf[r, s], kf[r, s], vv[r, s]
            va = jnp.concatenate([v, one], axis=1)
            p0, p1 = scores(q, k, v, m)
            dnb = do[r, s]
            dy = jnp.concatenate([dnb, dd[r, s]], axis=1)
            ds0 = (dot_nt(dy, jnp.where(h0w, va, zero)) * m).astype(BF16)
            ds1 = (dot_nt(dy, jnp.where(h0w, zero, va)) * m).astype(BF16)
            dst = cur[j]
            dhi, dlo = split(dst)
            dq = dot(ds0, jnp.where(h0, k, zero)) + dot(ds1, jnp.where(h0, zero, k)) + cr * (dot_nt(dy, st[i, j, 0]) + dot_nt(dy, st[i, j, 1]))
            dk = dot_tn(ds0, jnp.where(h0, q, zero)) + dot_tn(ds1, jnp.where(h0, zero, q)) + tr * (dot_nt(va, dhi) + dot_nt(va, dlo))
            dv = dot_tn(p0, jnp.where(h0, dnb, zero)) + dot_tn(p1, jnp.where(h0, zero, dnb)) + tr * dot(k, dhi[:, :128])
            qc = (q.astype(F32) * cr).astype(BF16)
            cur[j] = kpw * dst + jnp.where(block, dot_tn(qc, dy), 0.0)
            unfeature(dq, q, s, 0)
            unfeature(dk, k, s, width)
            pg[r, 2 * width + s.start:2 * width + s.stop] = dv.astype(BF16)
    loop(nch, backward)

    D = tok.shape[1]
    gd[...] = dot_tn(o[...], cot[...]).astype(BF16)
    def gqkv(i):
        gq[:, tile(i, width)] = dot_tn(attn_in[...], pg[:, tile(i, width)]).astype(BF16)
    loop(3, gqkv)
    def dattn(i):
        r = tile(i, RT)
        dy1[r, :] = dot_nt(pg[r, :], wq[...]).astype(BF16)
    loop(T // RT, dattn)

def attention(head, rot, tok, cot, vec, fw, wq, wd, mask, carr, trail, keep, cosp, sina, sinb, mixh, mixl, mixt):
    T, D = tok.shape
    W = fw.shape[1]
    sd = jax.ShapeDtypeStruct
    vm = pl.BlockSpec(memory_space=pltpu.VMEM)
    outs = [sd((T, D), BF16), sd((T, W), BF16), sd((T, 3 * W), BF16), sd((D, 3 * W), BF16), sd((W, D), BF16), sd((8, W), F32), sd((T, D), BF16)]
    return pl.pallas_call(
        partial(attention_kernel, head, rot), out_shape=outs, in_specs=[vm] * 16, out_specs=[vm] * 7,
        scratch_shapes=[pltpu.VMEM((T, D), BF16), pltpu.VMEM((T, W), BF16), pltpu.VMEM((T, W), BF16), pltpu.VMEM((T, W), BF16),
                        pltpu.VMEM((T, W), BF16), pltpu.VMEM((T, W), BF16), pltpu.VMEM((T // CH, W // 128, 2, 128, 256), BF16), pltpu.VMEM((W // 128, 128, 256), F32)],
        compiler_params=pltpu.CompilerParams(vmem_limit_bytes=62 << 20), name="attention",
    )(tok, cot, vec, fw, wq, wd, mask, carr, trail, keep, cosp, sina, sinb, mixh, mixl, mixt)

def gelu_pair(x):
    e = jnp.exp(-0.5 * x * x)
    t = 1.0 / (1.0 + (0.3275911 / math.sqrt(2.0)) * jnp.abs(x))
    poly = t * (0.254829592 + t * (-0.284496736 + t * (1.421413741 + t * (-1.453152027 + t * 1.061405429))))
    tail = 0.5 * poly * e
    phi = jnp.where(x >= 0, 1.0 - tail, tail)
    return x * phi, phi + x * e * (1.0 / math.sqrt(2.0 * math.pi))

def mlp_kernel(mlp_in, cot, o, wd, wu, ww, out, gu, gw, dy2, h, pre):
    T, D = mlp_in.shape
    FB = 512
    nb = wu.shape[1] // FB
    RT = 512
    def hidden(i):
        m = lax.div(i, T // RT)
        r = tile(lax.rem(i, T // RT), RT)
        c = tile(m, FB)
        hid = dot(mlp_in[r, :], wu[:, c])
        act, slope = gelu_pair(hid)
        h[r, c] = act.astype(BF16)
        pre[r, c] = (dot_nt(cot[r, :], ww[c, :]) * slope).astype(BF16)
    loop(nb * (T // RT), hidden)
    def grads(m):
        c = tile(m, FB)
        gw[c, :] = dot_tn(h[:, c], cot[...]).astype(BF16)
        gu[:, c] = dot_tn(mlp_in[...], pre[:, c]).astype(BF16)
    loop(nb, grads)
    def last(i):
        r = tile(i, RT)
        out[r, :] = (dot(h[r, :], ww[...]) + dot(o[r, :], wd[...])).astype(BF16)
        dy2[r, :] = dot_nt(pre[r, :], wu[...]).astype(BF16)
    loop(T // RT, last)

def mlp(mlp_in, cot, o, wd, wu, ww):
    T, D = mlp_in.shape
    FH = wu.shape[1]
    sd = jax.ShapeDtypeStruct
    vm = pl.BlockSpec(memory_space=pltpu.VMEM)
    outs = [sd((T, D), BF16), sd((D, FH), BF16), sd((FH, D), BF16), sd((T, D), BF16)]
    return pl.pallas_call(mlp_kernel, out_shape=outs, in_specs=[vm] * 6, out_specs=[vm] * 4,
        scratch_shapes=[pltpu.VMEM((T, FH), BF16), pltpu.VMEM((T, FH), BF16)],
        compiler_params=pltpu.CompilerParams(vmem_limit_bytes=62 << 20), name="mlp")(mlp_in, cot, o, wd, wu, ww)

def tables(seq, rot, head, feats):
    half = rot // 2
    angles = np.arange(seq)[:, None] / 10000.0 ** (np.arange(0, rot, 2) / rot)[None, :]
    cosp, sina, sinb = np.ones((seq, 128)), np.zeros((seq, 128)), np.zeros((seq, 128))
    for base in range(0, 128, head):
        cosp[:, base:base + half] = np.cos(angles)
        cosp[:, base + half:base + rot] = np.cos(angles)
        sina[:, base + half:base + rot] = np.sin(angles)
        sinb[:, base:base + half] = -np.sin(angles)
    k, i = np.arange(head)[:, None], np.arange(head)[None, :]
    cosine = np.where(k == 0, math.sqrt(1.0 / head), math.sqrt(2.0 / head)) * np.cos(math.pi * (i + 0.5) * k / head)
    j = np.arange(feats)[None, :]
    level = (((j * (2 * k + 1) + k) % feats) + 0.5) / feats
    normals = np.vectorize(NormalDist().inv_cdf)(level)
    mixing = cosine.T @ normals / math.sqrt(head)
    mix = np.zeros((128, 128), np.float32)
    for base in range(0, 128, head):
        mix[base:base + head, base:base + feats] = mixing
    return cosp.astype(np.float32), sina.astype(np.float32), sinb.astype(np.float32), mix

def doc_masks(doc, seq):
    n = doc.shape[0]
    d = doc.reshape(n, seq // CH, CH)
    causal = jnp.arange(CH)[:, None] >= jnp.arange(CH)[None, :]
    mask = ((d[:, :, :, None] == d[:, :, None, :]) & causal).astype(BF16).reshape(-1, CH)
    last = d[:, :, -1]
    before = jnp.concatenate([jnp.full((n, 1), -1, doc.dtype), last[:, :-1]], axis=1)
    carr = jnp.broadcast_to((d == before[:, :, None]).astype(F32).reshape(-1, 1), (n * seq, 128))
    trail = jnp.broadcast_to((d == last[:, :, None]).astype(F32).reshape(-1, 1), (n * seq, 128))
    keep = jnp.broadcast_to((last == before).astype(F32).reshape(-1, 1, 1), (n * seq // CH, 1, 128))
    return mask, carr, trail, keep


def all_streams(at, sems, accs, holds):
    streams = []
    it = iter(holds)
    nb = at.nbits
    for acc in accs:
        for (start, size), order in zip(shares(acc.shape[-2]), orders(nb)):
            if size:
                n = len(hold_shapes(at.nz, nb, size, acc.shape[-1], order))
                streams.append(scatter_stream(at, sems, acc, [next(it) for _ in range(n)], start, size, order))
    return streams

def settle_kernel(nf, nz, nh, *refs):
    (gq, gd, gu, gw, gf, fw, part, dy1, dy2, tok, cot, vec,
     oq, od, ou, ow, ovec, output, input_grad) = refs[:19]
    aq, ad, au, aw = refs[19:23]
    holds = refs[23:23 + nh]
    hq, hu, pr, gv, vh, send, recv, local = refs[23 + nh:]
    at = Place(nf, nz)
    sems = Sems(send, recv)
    c, o = at.core, 1 - at.core
    rows, D = tok.shape
    at.greet(far=True)
    swaps = []
    for k, ref in enumerate((part, dy1, dy2)):
        cp = sems.copy(ref.at[o], pr.at[2 * k], sems.take(), at.partner())
        cp.start()
        swaps.append(cp)
    loads = []
    for k, (src, dst) in enumerate(((gq, aq), (gd, ad), (gu, au), (gw, aw), (part.at[c], pr.at[1]), (dy1.at[c], pr.at[3]), (dy2.at[c], pr.at[5]))):
        cp = pltpu.make_async_copy(src, dst, local.at[k])
        cp.start()
        loads.append(cp)
    streams = all_streams(at, sems, (aq, ad, au, aw), holds)
    for cp in loads[:4]:
        cp.wait()
    for s in streams:
        s[0][0]()
    for cp in loads[4:]:
        cp.wait()
    for cp in swaps:
        cp.wait_recv()
    gv[...] = jnp.zeros_like(gv)

    def finish(i):
        r = tile(i, CH)
        x = tok[r, :].astype(F32)
        n, rstd = normed(x)
        get = lambda k: pr[2 * k, r, :].astype(F32) + pr[2 * k + 1, r, :].astype(F32)
        output[r, :] = (x + get(0)).astype(BF16)
        d1, d2 = get(1), get(2)
        fold = lambda y: jnp.sum(y, axis=0, keepdims=True)
        gv[0:1, :] += fold(d1 * n)
        gv[1:2, :] += fold(d1)
        gv[2:3, :] += fold(d2 * n)
        gv[3:4, :] += fold(d2)
        dn = d1 * vec[0:1, :] + d2 * vec[2:3, :]
        dx = rstd * (dn - jnp.mean(dn, axis=-1, keepdims=True) - n * jnp.mean(dn * n, axis=-1, keepdims=True))
        input_grad[r, :] = cot[r, :].astype(F32) + dx
    loop(rows // CH, finish)
    for m in range(gf.shape[1] // 128):
        s = slice(m * 128, (m + 1) * 128)
        gv[4:5, pl.ds(pl.multiple_of((2 * m + c) * 128, 128), 128)] = jnp.sum(gf[:, s], axis=0, keepdims=True) / fw[:, s]

    n = len(streams[0])
    for r in range(n):
        for s in streams:
            s[r][1]()
            if r + 1 < n:
                s[r + 1][0]()
    peers = [at.partner()] + [at.across(b) for b in range(at.nbits)]
    step = 1
    while step < nz:
        peers.append(at.fold(step))
        step *= 2
    small = []
    for k, peer in enumerate(peers):
        cp = sems.copy(gv, vh.at[k], sems.take(), peer)
        cp.start()
        cp.wait()
        gv[...] += vh[k]
    ovec[...] = gv[...]
    me = at.slot(())
    last = []
    for acc, hold, out in ((aq, hq, oq), (au, hu, ou)):
        half = hold.shape[0]
        cols = at.columns(acc, at.z)
        cp = sems.copy(acc.at[me + (tile(o, half), cols)], hold, sems.take(), at.partner())
        cp.start()
        out[c] = acc[me + (tile(c, half), cols)]
        last.append((cp, hold, out))
    od[...] = ad[me + (slice(None), at.columns(ad, at.z))]
    ow[...] = aw[me + (slice(None), at.columns(aw, at.z))]
    for cp, hold, out in last:
        cp.wait_recv()
        out[o] = hold[...]
        cp.wait_send()
    for cp in swaps:
        cp.wait_send()
    for s in streams:
        for r in s:
            r[2]()

def settle(nf, nz, gq, gd, gu, gw, gf, fw, part, dy1, dy2, tok, cot, vec):
    sd = jax.ShapeDtypeStruct
    bits = (2,) * ((nf // 2).bit_length() - 1)
    nb, chips = len(bits), nf // 2
    cut = lambda g: g.reshape(bits + (g.shape[0] // chips, g.shape[1]))
    accs = [cut(g) for g in (gq, gd, gu, gw)]
    rows, D = tok.shape
    two = lambda x: x.reshape(2, rows, D)
    own = lambda a: (a.shape[-2], a.shape[-1] // nz)
    holds = []
    for a in accs:
        for (start, size), order in zip(shares(a.shape[-2]), orders(nb)):
            if size:
                holds += hold_shapes(nz, nb, size, a.shape[-1], order)
    halves = [(own(a)[0] // 2, own(a)[1]) for a in (accs[0], accs[2])]
    nsteps = 1 + nb + max(nz.bit_length() - 1, 0)
    ncopies = 3 + 12 * copies_of(nz, nb) + nsteps + 2
    vm, hb = pl.BlockSpec(memory_space=pltpu.VMEM), pl.BlockSpec(memory_space=pl.ANY)
    outs = [sd((2,) + halves[0], BF16), sd(own(accs[1]), BF16), sd((2,) + halves[1], BF16), sd(own(accs[3]), BF16), sd(vec.shape, F32), sd((rows, D), BF16), sd((rows, D), F32)]
    return pl.pallas_call(
        partial(settle_kernel, nf, nz, len(holds)), out_shape=outs,
        in_specs=[hb] * 4 + [vm] * 2 + [hb] * 3 + [vm] * 3, out_specs=[vm] * 7,
        scratch_shapes=[pltpu.VMEM(a.shape, BF16) for a in accs] + [pltpu.VMEM(h, BF16) for h in holds]
        + [pltpu.VMEM(h, BF16) for h in halves] + [pltpu.VMEM((6, rows, D), BF16), pltpu.VMEM(vec.shape, F32), pltpu.VMEM((nsteps,) + vec.shape, F32)]
        + [pltpu.SemaphoreType.DMA((ncopies,)), pltpu.SemaphoreType.DMA((ncopies,)), pltpu.SemaphoreType.DMA((7,))],
        compiler_params=pltpu.CompilerParams(collective_id=1, has_side_effects=True, vmem_limit_bytes=62 << 20), name="settle",
    )(*accs, gf, fw, two(part), two(dy1), two(dy2), tok, cot, vec)

def body(nf, nz, tokens, doc_starts, w_qkv, w_dense, w_up, w_down, norm1_gain, norm1_bias, norm2_gain, norm2_bias, feature_weight, cotangent):
    rows, D = tokens.shape
    core = lax.rem(lax.axis_index("fsdp"), 2)
    width = D // 2
    unit = w_down.shape[0]
    def turn(w, block):
        r, n = w.shape
        return w.reshape(r, n // (2 * block), 2, block).transpose(2, 0, 1, 3).reshape(2, r, n // 2)

    def unturn(g, block):
        two, r, n = g.shape
        return g.reshape(2, r, n // block, block).transpose(1, 2, 0, 3).reshape(r, 2 * n)

    sub = 128 // (2 * w_dense.shape[0])
    pairs = [(f, f ^ 1) for f in range(nf)]

    def heads_of(w):
        if not sub:
            return w
        w = w.reshape(-1, 2, sub, w_dense.shape[0], D)
        kept = lax.dynamic_index_in_dim(w, core, 1, keepdims=False)
        other = lax.ppermute(lax.dynamic_index_in_dim(w, 1 - core, 1, keepdims=False), "fsdp", pairs)
        both = jnp.where(core == 0, jnp.stack([kept, other], 2), jnp.stack([other, kept], 2))
        return both.reshape(-1, D)

    def shards_of(g):
        if not sub:
            return g
        g = g.reshape(-1, sub, 2, w_dense.shape[0], D)
        kept = lax.dynamic_index_in_dim(g, core, 2, keepdims=False)
        other = lax.ppermute(lax.dynamic_index_in_dim(g, 1 - core, 2, keepdims=False), "fsdp", pairs)
        both = jnp.where(core == 0, jnp.stack([kept, other], 1), jnp.stack([other, kept], 1))
        return both.reshape(-1, D)

    doc = jnp.cumsum(doc_starts.reshape(-1, SEQ_LEN), axis=1).astype(jnp.int32)
    vec = jnp.stack([norm1_gain, norm1_bias, norm2_gain, norm2_bias, feature_weight] + [jnp.zeros_like(norm1_gain)] * 3)
    tok2, cot2, doc2, vecs, bq, bd, bu, bw = gather(
        nf, nz, tokens, cotangent, doc.reshape(8, -1), vec, turn(w_qkv, 128), w_dense, turn(w_up, unit), w_down
    )
    join = lambda b: b.reshape(-1, b.shape[-1])
    dense = heads_of(join(bd))
    vec8 = vecs.reshape(nf, 8, -1).transpose(1, 0, 2).reshape(8, D)
    fw = lax.dynamic_index_in_dim(vec8[4].reshape(D // 256, 2, 128), core, 1, keepdims=False).reshape(1, width)
    masks = doc_masks(doc2.reshape(-1, SEQ_LEN), SEQ_LEN)
    cosp, sina, sinb, mix = tables(SEQ_LEN, ROT, HEAD, FEATS)
    mix = jnp.asarray(mix)
    mixh = mix.astype(BF16)
    mixl = (mix - mixh.astype(F32)).astype(BF16)
    tok_all, cot_all = tok2.reshape(2 * rows, D), cot2.reshape(2 * rows, D)
    mlp_in, mixed, pg, gq, gd, gf, dy1 = attention(
        HEAD, ROT, tok_all, cot_all, vec8, fw, join(bq), dense, *masks, cosp, sina, sinb, mixh, mixl, mixh.T
    )
    part, gu, gw, dy2 = mlp(mlp_in, cot_all, mixed, dense, join(bu), join(bw))
    oq, od, ou, ow, gv, output, input_grad = settle(nf, nz, gq, shards_of(gd), gu, gw, gf, fw, part, dy1, dy2, tokens, cotangent, vec8)
    own = gv.reshape(8, nf, -1)
    own = lax.dynamic_index_in_dim(own, lax.axis_index("fsdp"), 1, keepdims=False)
    return (
        output, input_grad,
        unturn(oq, 128).astype(F32), od.astype(F32), unturn(ou, unit).astype(F32), ow.astype(F32),
        own[0], own[1], own[2], own[3], own[4],
    )


def solution(mesh):
    nf, nz = mesh.shape["fsdp"], mesh.shape["inner"]
    rows, mat, vec = P(("fsdp", "inner"), None), P("fsdp", "inner"), P("fsdp")
    in_specs = (rows, P(("fsdp", "inner"))) + (mat,) * 4 + (vec,) * 5 + (rows,)
    out_specs = (rows, rows) + (mat,) * 4 + (vec,) * 5
    return jax.shard_map(partial(body, nf, nz), mesh=mesh, in_specs=in_specs, out_specs=out_specs, check_vma=False)
```

```python
from functools import partial
import math
from statistics import NormalDist

import jax
import jax.numpy as jnp
import numpy as np
from jax import lax
from jax.experimental import pallas as pl
from jax.experimental.pallas import tpu as pltpu
from jax.sharding import PartitionSpec as P

MESH = pl.DeviceIdType.MESH
BF16 = jnp.bfloat16
F32 = jnp.float32


HEAD = 64
ROT = 16
FEATS = 64
SEQ_LEN = 1024

class Place:
    def __init__(self, nf, nz):
        self.nf, self.nz = nf, nz
        self.nbits = (nf // 2).bit_length() - 1
        self.f = lax.axis_index("fsdp")
        self.z = lax.axis_index("inner")
        self.core = lax.rem(self.f, 2)
        self.bits = [lax.rem(lax.div(self.f, 2 << b), 2) for b in range(self.nbits)]

    def partner(self):
        return (self.f + 1 - 2 * self.core, self.z)

    def across(self, b):
        return (self.f + (1 - 2 * self.bits[b]) * (2 << b), self.z)

    def along(self, step):
        return (self.f, self.z + step)

    def slot(self, done, flip=None):
        index = []
        for b in reversed(range(self.nbits)):
            if b in done:
                index.append(slice(None))
            elif b == flip:
                index.append(1 - self.bits[b])
            else:
                index.append(self.bits[b])
        return tuple(index)

    def columns(self, buf, zsel):
        if zsel is None:
            return slice(None)
        width = buf.shape[-1] // self.nz
        return pl.ds(pl.multiple_of(zsel * width, width), width)

    def greet(self, far=False):
        bar = pltpu.get_barrier_semaphore()
        z, nz = self.z, self.nz
        fixed = [self.partner()] + [self.across(b) for b in range(self.nbits)]
        for peer in fixed:
            pl.semaphore_signal(bar, inc=1, device_id=peer, device_id_type=MESH)

        @pl.when(z > 0)
        def _():
            pl.semaphore_signal(bar, inc=1, device_id=self.along(-1), device_id_type=MESH)

        @pl.when(z < nz - 1)
        def _():
            pl.semaphore_signal(bar, inc=1, device_id=self.along(1), device_id_type=MESH)

        count = len(fixed)
        if far and nz > 2:
            step = 2
            while step < nz:
                pl.semaphore_signal(
                    bar, inc=1, device_id=self.fold(step), device_id_type=MESH
                )
                count += 1
                step *= 2
        inner = (z > 0).astype(jnp.int32) + (z < nz - 1).astype(jnp.int32)
        pl.semaphore_wait(bar, count + inner)

    def fold(self, step):
        bit = lax.rem(lax.div(self.z, step), 2)
        return (self.f, self.z + (1 - 2 * bit) * step)


class Sems:
    def __init__(self, send, recv):
        self.send, self.recv, self.count = send, recv, 0

    def take(self):
        self.count += 1
        return self.count - 1

    def copy(self, src, dst, i, peer):
        return pltpu.make_async_remote_copy(
            src_ref=src,
            dst_ref=dst,
            send_sem=self.send.at[i],
            recv_sem=self.recv.at[i],
            device_id=peer,
            device_id_type=MESH,
        )


def shares(rows):
    units = rows // 16
    last = units // 4
    first = (units - last + 1) // 2
    sizes = [first * 16, (units - last - first) * 16, last * 16]
    starts = [0, sizes[0], sizes[0] + sizes[1]]
    return list(zip(starts, sizes))


def orders(nbits):
    up, down = list(range(nbits)), list(reversed(range(nbits)))
    return [["z"] + up, ["z"] + down, up + ["z"]]


def copies_of(nz, nbits):
    return nbits + 2 * (nz - 1)


def gather_stream(at, sems, buf, start, size, order):
    rows = pl.ds(start, size)
    rounds = []
    done, zdone = (), False

    def along(k, done):
        ids = (sems.take(), sems.take())

        def right(zsel):
            ref = buf.at[at.slot(done) + (rows, at.columns(buf, zsel))]
            return sems.copy(ref, ref, ids[0], at.along(1))

        def left(zsel):
            ref = buf.at[at.slot(done) + (rows, at.columns(buf, zsel))]
            return sems.copy(ref, ref, ids[1], at.along(-1))

        z, nz = at.z, at.nz
        goes_right = (z < nz - 1) & (z - k + 1 >= 0)
        goes_left = (z > 0) & (z + k - 1 <= nz - 1)

        def send():
            pl.when(goes_right)(lambda: right(z - k + 1).start())
            pl.when(goes_left)(lambda: left(z + k - 1).start())

        def arrive():
            pl.when(z - k >= 0)(lambda: right(z - k).wait_recv())
            pl.when(z + k <= nz - 1)(lambda: left(z + k).wait_recv())

        def leave():
            pl.when(goes_right)(lambda: right(z - k + 1).wait_send())
            pl.when(goes_left)(lambda: left(z + k - 1).wait_send())

        return send, arrive, leave

    def across(b, done, zsel):
        i = sems.take()
        mine = buf.at[at.slot(done) + (rows, at.columns(buf, zsel))]
        theirs = buf.at[at.slot(done, flip=b) + (rows, at.columns(buf, zsel))]
        out = sems.copy(mine, mine, i, at.across(b))
        back = sems.copy(theirs, theirs, i, at.across(b))
        return out.start, back.wait_recv, out.wait_send

    piece = size * (buf.shape[-1] // at.nz) * 2
    for dim in order:
        if dim == "z":
            rounds += [along(k, done) + ("z", piece << len(done)) for k in range(1, at.nz)]
            zdone = True
        else:
            nbytes = (piece << len(done)) * (at.nz if zdone else 1)
            rounds.append(across(dim, done, None if zdone else at.z) + (dim, nbytes))
            done = done + (dim,)
    return rounds


def scatter_stream(at, sems, acc, holds, start, size, order):
    rows = pl.ds(start, size)
    rounds = []
    left_bits, zleft = set(range(at.nbits)), True

    def along(k, remaining, hold):
        ids = (sems.take(), sems.take())
        z, nz = at.z, at.nz

        def part(zsel):
            return acc.at[at.slot(remaining) + (rows, at.columns(acc, zsel))]

        def right(zsel):
            return sems.copy(part(zsel), hold.at[2 * k - 2], ids[0], at.along(1))

        def left(zsel):
            return sems.copy(part(zsel), hold.at[2 * k - 1], ids[1], at.along(-1))

        goes_right = z + k <= nz - 1
        goes_left = z - k >= 0

        def send():
            pl.when(goes_right)(lambda: right(z + k).start())
            pl.when(goes_left)(lambda: left(z - k).start())

        def arrive():
            @pl.when((z >= 1) & (z - 1 + k <= nz - 1))
            def _():
                right(z - 1 + k).wait_recv()
                ref = part(z - 1 + k)
                ref[...] += hold[2 * k - 2]

            @pl.when((z <= nz - 2) & (z + 1 - k >= 0))
            def _():
                left(z + 1 - k).wait_recv()
                ref = part(z + 1 - k)
                ref[...] += hold[2 * k - 1]

        def leave():
            pl.when(goes_right)(lambda: right(z + k).wait_send())
            pl.when(goes_left)(lambda: left(z - k).wait_send())

        return send, arrive, leave

    def across(b, remaining, zsel, hold):
        i = sems.take()
        out = sems.copy(
            acc.at[at.slot(remaining, flip=b) + (rows, at.columns(acc, zsel))], hold, i, at.across(b)
        )

        def arrive():
            out.wait_recv()
            ref = acc.at[at.slot(remaining) + (rows, at.columns(acc, zsel))]
            ref[...] += hold[...]

        return out.start, arrive, out.wait_send

    piece = size * (acc.shape[-1] // at.nz) * 2
    holds = iter(holds)
    for dim in reversed(order):
        if dim == "z":
            hold = next(holds)
            rounds += [
                along(k, tuple(left_bits), hold) + ("z", piece << len(left_bits))
                for k in range(at.nz - 1, 0, -1)
            ]
            zleft = False
        else:
            left_bits = left_bits - {dim}
            nbytes = (piece << len(left_bits)) * (at.nz if zleft else 1)
            rounds.append(across(dim, tuple(left_bits), None if zleft else at.z, next(holds)) + (dim, nbytes))
    return rounds


def hold_shapes(nz, nbits, size, width, order):
    shapes, bits, zleft = [], nbits, True
    for dim in reversed(order):
        if dim == "z":
            shapes.append((2 * (nz - 1),) + (2,) * bits + (size, width // nz))
            zleft = False
        else:
            bits -= 1
            shapes.append((2,) * bits + (size, width if zleft else width // nz))
    return shapes


LINK_RATE = 45000.0
HOP = 1.5


class Agenda:
    def __init__(self):
        self.events, self.now, self.free = [], 0.0, {}

    def add(self, streams, ready, rank=0):
        state = [[0, t] for t, _ in ready]
        while True:
            best = None
            for i, rounds in enumerate(streams):
                r, t = state[i]
                if r == len(rounds):
                    continue
                begin = max(t, self.free.get(rounds[r][3], 0.0))
                if best is None or begin < best[0] - 1e-9:
                    best = (begin, i)
            if best is None:
                break
            begin, i = best
            r = state[i][0]
            rounds = streams[i]
            wait = ready[i][1] if r == 0 else rounds[r - 1][1]
            took = rounds[r][4] / LINK_RATE

            def act(wait=wait, send=rounds[r][0]):
                if wait is not None:
                    wait()
                send()

            self.events.append((begin, act))
            self.free[rounds[r][3]] = begin + took
            state[i] = [r + 1, begin + took + HOP]
            if r + 1 == len(rounds):
                self.events.append((begin + took + HOP, rounds[r][1]))
        self.events.sort(key=lambda e: e[0])
        return [t for _, t in state]

    def at(self, time, act):
        self.events.append((time, act))
        self.events.sort(key=lambda e: e[0])

    def until(self, time):
        while self.events and self.events[0][0] <= time:
            self.events.pop(0)[1]()
        self.now = max(self.now, time)

    def loop(self, n, body, took):
        due = [[] for _ in range(n)]
        while self.events and self.events[0][0] < self.now + n * took:
            time, act = self.events.pop(0)
            due[max(0, int((time - self.now) / took))].append(act)
        self.now += n * took

        def step(i, carry):
            for u, acts in enumerate(due):
                if acts:

                    @pl.when(i == u)
                    def _(acts=acts):
                        for act in acts:
                            act()

            body(i)
            return carry

        lax.fori_loop(0, n, step, 0)


CH = 256

def dot(a, b):
    return jnp.dot(a, b, preferred_element_type=F32)

def dot_nt(a, b):
    return lax.dot_general(a, b, (((1,), (1,)), ((), ())), preferred_element_type=F32)

def dot_tn(a, b):
    return lax.dot_general(a, b, (((0,), (0,)), ((), ())), preferred_element_type=F32)

def tile(i, n):
    return pl.ds(pl.multiple_of(i * n, n), n)

def lanes(width):
    return lax.broadcasted_iota(jnp.int32, (1, width), 1)

def normed(x):
    center = x - jnp.mean(x, axis=-1, keepdims=True)
    spread = jnp.mean(center * center, axis=-1, keepdims=True)
    rstd = lax.rsqrt(spread + 1e-05)
    return center * rstd, rstd

def attend_kernel(nf, nz, head, rot, tok, cot, docc1, docr1, vec1, wq1, wd1, wu1, ww1, cosp, sina, sinb, mixh, mixl, mixt,
                  cot2, mlp_in2, bu, bw, gq2, gd2, dy1, dy1in, out1, out1in, vec, fw, gf,
                  tok_v, cot_v, docc, docr, vecs, bq, bd, attn_in, mlp_in, qf, kf, vv, dd, do, o, pg, gq, gd, st, cur,
                  send, recv, local):
    at = Place(nf, nz)
    sems = Sems(send, recv)
    c, p = at.core, 1 - at.core
    S, D = tok.shape
    T = 2 * S
    width = qf.shape[1]
    npair = width // 128
    seq = cosp.shape[0]
    nch = T // CH
    half = rot // 2
    me = at.slot(())
    own_rows, other_rows = tile(c, S), tile(p, S)
    at.greet()

    locals_ = []
    def put(src, dst):
        cp = pltpu.make_async_copy(src, dst, local.at[len(locals_)])
        cp.start()
        locals_.append(cp)
        return cp

    swaps = []
    def swap(src, dst, arrives):
        i = sems.take()
        cp = sems.copy(src, dst, i, at.partner())
        cp.start()
        swaps.append(cp)
        return sems.copy(src, arrives, i, at.partner())

    def piece(buf, w, i):
        r = w.shape[-2]
        return buf.at[me + (tile(i, r), at.columns(buf, at.z))]

    z = lambda b: at.columns(b, at.z)
    in_q = [swap(wq1.at[p], piece(bq, wq1, c), piece(bq, wq1, p)).wait_recv, put(wq1.at[c], piece(bq, wq1, c)).wait]
    in_d = [put(wd1, bd.at[me + (slice(None), z(bd))]).wait]
    in_vec = [swap(vec1, vecs.at[me + (c,)], vecs.at[me + (p,)]).wait_recv, put(vec1, vecs.at[me + (c,)]).wait]
    in_tok = [put(tok, tok_v.at[own_rows]).wait, swap(tok, tok_v.at[own_rows], tok_v.at[other_rows]).wait_recv]
    n1 = docr1.shape[0]
    in_doc = [
        put(docc1, docc.at[own_rows]).wait, swap(docc1, docc.at[own_rows], docc.at[other_rows]).wait_recv,
        put(docr1, docr.at[tile(c, n1)]).wait, swap(docr1, docr.at[tile(c, n1)], docr.at[tile(p, n1)]).wait_recv,
    ]
    in_u = [swap(wu1.at[p], piece(bu, wu1, c), piece(bu, wu1, p)).wait_recv, put(wu1.at[c], piece(bu, wu1, c)).wait]
    in_w = [put(ww1, bw.at[me + (slice(None), z(bw))]).wait]
    in_cot = [put(cot, cot_v.at[own_rows]).wait, swap(cot, cot_v.at[own_rows], cot_v.at[other_rows]).wait_recv]

    def once(waits):
        done = []

        def wait():
            if not done:
                for w in waits:
                    w()
                done.append(1)

        return wait

    agenda = Agenda()
    streams, ready, first = [], [], 0
    for buf, waits, time in ((bq, in_q, 2.0), (bd, in_d, 2.0), (bu, in_u, 12.0), (bw, in_w, 4.0)):
        wait = once(waits)
        for (start, size), order in zip(shares(buf.shape[-2]), orders(at.nbits)):
            if size:
                streams.append(gather_stream(at, sems, buf, start, size, order))
                ready.append((time, wait))
        if buf is bd:
            first = len(streams)
    ends = agenda.add(streams, ready)
    agenda.until(4.0)
    for w in in_vec:
        w()
    done, small = (), []
    for b in range(at.nbits):
        i = sems.take()
        m, t = vecs.at[at.slot(done)], vecs.at[at.slot(done, flip=b)]
        out = sems.copy(m, m, i, at.across(b))
        out.start()
        sems.copy(t, t, i, at.across(b)).wait_recv()
        small.append(out)
        done = done + (b,)
    w = vec1.shape[1]
    for f in range(nf):
        at_f = tuple((f >> (b + 1)) & 1 for b in reversed(range(at.nbits))) + (f & 1,)
        vec[:, f * w:(f + 1) * w] = vecs[at_f]
    for m in range(npair):
        fw[:, m * 128:(m + 1) * 128] = vec[4:5, pl.ds(pl.multiple_of((2 * m + c) * 128, 128), 128)]
    agenda.until(11.0)
    for w in in_tok:
        w()

    def ln(i):
        r = tile(i, CH)
        n, _ = normed(tok_v[r, :].astype(F32))
        attn_in[r, :] = (n * vec[0:1, :] + vec[1:2, :]).astype(BF16)
        mlp_in[r, :] = (n * vec[2:3, :] + vec[3:4, :]).astype(BF16)
    agenda.loop(nch, ln, 0.5)
    keep_mlp = put(mlp_in, mlp_in2)
    for w in in_cot + in_doc:
        w()
    put(cot_v, cot2)
    agenda.until(max(ends[:first]))

    wq = lambda cols=slice(None): bq[(slice(None),) * at.nbits + (slice(None), cols)].reshape(D, -1)
    RT = 512
    def project(i):
        r = tile(i, RT)
        ps = tile(lax.rem(i, seq // RT), RT)
        a = attn_in[r, :]
        for part, dst in ((0, qf), (1, kf)):
            x = dot(a, wq(slice(part * width, (part + 1) * width)))
            for m in range(npair):
                s = slice(m * 128, (m + 1) * 128)
                y = x[:, s]
                y = y * cosp[ps, :] + pltpu.roll(y, half, 1) * sina[ps, :] + pltpu.roll(y, 128 - half, 1) * sinb[ps, :]
                hi = y.astype(BF16)
                lo = (y - hi.astype(F32)).astype(BF16)
                e = dot(hi, mixh[...]) + dot(lo, mixh[...]) + dot(hi, mixl[...])
                dst[r, s] = (fw[:, s] * jnp.exp(e)).astype(BF16)
        vv[r, :] = dot(a, wq(slice(2 * width, 3 * width))).astype(BF16)
        do[r, :] = dot_nt(cot_v[r, :], bd[...].reshape(width, D)).astype(BF16)
    agenda.loop(T // RT, project, 3.9)

    h0 = (lanes(128) % (2 * head)) < head
    h0w = jnp.concatenate([h0, h0], axis=1)
    rowh = lax.broadcasted_iota(jnp.int32, (128, 1), 0) < head
    block = rowh == h0w
    same = (rowh == h0).astype(BF16)
    one = jnp.ones((CH, 128), BF16)
    zero = jnp.zeros((), BF16)
    place = lanes(128) % head
    causal = lax.broadcasted_iota(jnp.int32, (CH, 1), 0) >= lanes(CH)

    def split(x):
        hi = x.astype(BF16)
        return hi, (x - hi.astype(F32)).astype(BF16)

    def masks(i):
        d = docc[tile(i, CH), :]
        inside = jnp.where(causal & (jnp.concatenate([d, d], axis=1) == docr[i]), 1.0, 0.0)
        start = lax.rem(i, seq // CH) == 0
        before = jnp.where(start, -1, docc[pl.ds(jnp.maximum(i * CH - 1, 0), 1), :])
        last = docc[pl.ds(i * CH + CH - 1, 1), :]
        ones = lambda x: jnp.where(x, 1.0, 0.0)
        return inside, ones(d == before), ones(d == last), ones(before == last)

    twice = lambda x: jnp.concatenate([x, x], axis=1)

    def scores(q, k, m):
        s0 = dot_nt(jnp.where(h0, q, zero), k)
        s1 = dot_nt(jnp.where(h0, zero, q), k)
        return (s0 * m).astype(BF16), (s1 * m).astype(BF16)

    cur[...] = jnp.zeros_like(cur)

    def forward(i):
        r = tile(i, CH)
        m, cr, tr, kp = masks(i)
        cw, kpw = twice(cr), twice(kp)
        for j in range(npair):
            s = slice(j * 128, (j + 1) * 128)
            q, k, v = qf[r, s], kf[r, s], vv[r, s]
            va = jnp.concatenate([v, one], axis=1)
            p0, p1 = scores(q, k, m)
            state = cur[j]
            hi, lo = split(state)
            st[i, j, 0] = hi
            st[i, j, 1] = lo
            res = dot(p0, jnp.where(h0w, va, zero)) + dot(p1, jnp.where(h0w, zero, va)) + cw * (dot(q, hi) + dot(q, lo))
            rd = 1.0 / res[:, 128:]
            att = res[:, :128] * rd
            o[r, s] = att.astype(BF16)
            dnb = (do[r, s].astype(F32) * rd).astype(BF16)
            do[r, s] = dnb
            hi, lo = split(dnb.astype(F32) * att)
            hi, lo = split(-(dot(hi, same) + dot(lo, same)))
            dd[r, s] = jnp.where(place == 0, hi, jnp.where(place == 1, lo, zero))
            kt = (k.astype(F32) * tr).astype(BF16)
            cur[j] = kpw * state + jnp.where(block, dot_tn(kt, va), 0.0)
    agenda.loop(nch, forward, 1.95)

    cur[...] = jnp.zeros_like(cur)
    gf[...] = jnp.zeros_like(gf)

    def backward(ii):
        i = nch - 1 - ii
        r = tile(i, CH)
        ps = tile(lax.rem(i, seq // CH), CH)
        m, cr, tr, kp = masks(i)
        kpw = twice(kp)
        cos, sa, sb = cosp[ps, :], sina[ps, :], sinb[ps, :]

        def unfeature(d, f, s, base):
            de = d * f.astype(F32)
            gf[:, s] += jnp.sum(de.reshape(CH // 8, 8, 128), axis=0)
            g = dot(de.astype(BF16), mixt[...])
            g = g * cos + pltpu.roll(g * sa, 128 - half, 1) + pltpu.roll(g * sb, half, 1)
            pg[r, base + s.start:base + s.stop] = g.astype(BF16)

        for j in range(npair):
            s = slice(j * 128, (j + 1) * 128)
            q, k, v = qf[r, s], kf[r, s], vv[r, s]
            va = jnp.concatenate([v, one], axis=1)
            p0, p1 = scores(q, k, m)
            dnb = do[r, s]
            dy = jnp.concatenate([dnb, dd[r, s]], axis=1)
            ds0 = (dot_nt(dy, jnp.where(h0w, va, zero)) * m).astype(BF16)
            ds1 = (dot_nt(dy, jnp.where(h0w, zero, va)) * m).astype(BF16)
            dst = cur[j]
            dhi, dlo = split(dst)
            dq = dot(ds0, jnp.where(h0, k, zero)) + dot(ds1, jnp.where(h0, zero, k)) + cr * (dot_nt(dy, st[i, j, 0]) + dot_nt(dy, st[i, j, 1]))
            dk = dot_tn(ds0, jnp.where(h0, q, zero)) + dot_tn(ds1, jnp.where(h0, zero, q)) + tr * (dot_nt(va, dhi) + dot_nt(va, dlo))
            dv = dot_tn(p0, jnp.where(h0, dnb, zero)) + dot_tn(p1, jnp.where(h0, zero, dnb)) + tr * dot(k, dhi[:, :128])
            qc = (q.astype(F32) * cr).astype(BF16)
            cur[j] = kpw * dst + jnp.where(block, dot_tn(qc, dy), 0.0)
            unfeature(dq, q, s, 0)
            unfeature(dk, k, s, width)
            pg[r, 2 * width + s.start:2 * width + s.stop] = dv.astype(BF16)
    agenda.loop(nch, backward, 3.1)

    keep_mlp.wait()
    turn = lambda i: tile(lax.rem(i + p * (S // RT), T // RT), RT)
    def dattn(i):
        r = turn(i)
        tok_v[r, :] = dot_nt(pg[r, :], wq()).astype(BF16)
        mlp_in[r, :] = dot(o[r, :], bd[...].reshape(width, D)).astype(BF16)
    agenda.loop(S // RT, dattn, 2.5)
    arrivals = [
        swap(tok_v.at[other_rows], dy1in, dy1in).wait_recv,
        swap(mlp_in.at[other_rows], out1in, out1in).wait_recv,
    ]
    agenda.loop(S // RT, lambda i: dattn(i + S // RT), 2.5)
    put(tok_v.at[own_rows], dy1)
    put(mlp_in.at[own_rows], out1)
    gd[...] = dot_tn(o[...], cot_v[...]).astype(BF16)
    put(gd, gd2)
    def gqkv(i):
        gq[:, tile(i, width)] = dot_tn(attn_in[...], pg[:, tile(i, width)]).astype(BF16)
    agenda.loop(3, gqkv, 2.4)
    put(gq, gq2)
    agenda.until(1e9)
    for w in arrivals:
        w()
    for cp in locals_[LOCAL_DONE:]:
        if cp is not keep_mlp:
            cp.wait()
    for cp in swaps + small:
        cp.wait_send()
    for s in streams:
        for r in s:
            r[2]()


LOCAL_DONE = 9


def attend(nf, nz, head, rot, tok, cot, docc, docr, vec, wq, wd, wu, ww, cosp, sina, sinb, mixh, mixl, mixt):
    bits = (2,) * ((nf // 2).bit_length() - 1)
    nb = len(bits)
    S, D = tok.shape
    T, W = 2 * S, D // 2
    sd = jax.ShapeDtypeStruct
    hb, vm = pl.BlockSpec(memory_space=pl.ANY), pl.BlockSpec(memory_space=pltpu.VMEM)
    full_u = bits + (2 * wu.shape[1], nz * wu.shape[2])
    full_w = bits + (ww.shape[0], nz * ww.shape[1])
    full_q = bits + (2 * wq.shape[1], nz * wq.shape[2])
    full_d = bits + (wd.shape[0], nz * wd.shape[1])
    outs = [sd((T, D), BF16), sd((T, D), BF16), sd(full_u, BF16), sd(full_w, BF16), sd((D, 3 * W), BF16), sd((W, D), BF16)]
    outs += [sd((S, D), BF16)] * 4 + [sd((8, D), F32), sd((1, W), F32), sd((8, W), F32)]
    n = 10 + nb + 12 * copies_of(nz, nb)
    v = lambda *shape: pltpu.VMEM(shape, BF16)
    i32 = lambda *shape: pltpu.VMEM(shape, jnp.int32)
    return pl.pallas_call(
        partial(attend_kernel, nf, nz, head, rot), out_shape=outs,
        in_specs=[hb] * 9 + [vm] * 6, out_specs=[hb] * 10 + [vm] * 3,
        scratch_shapes=[
            v(T, D), v(T, D), i32(T, 128), i32(2 * docr.shape[0], 1, CH), pltpu.VMEM(bits + (2,) + vec.shape, F32), v(*full_q), v(*full_d),
            v(T, D), v(T, D), v(T, W), v(T, W), v(T, W), v(T, W), v(T, W), v(T, W), v(T, 3 * W), v(D, 3 * W), v(W, D),
            v(T // CH, W // 128, 2, 128, 256), pltpu.VMEM((W // 128, 128, 256), F32),
            pltpu.SemaphoreType.DMA((n,)), pltpu.SemaphoreType.DMA((n,)), pltpu.SemaphoreType.DMA((16,)),
        ],
        compiler_params=pltpu.CompilerParams(collective_id=0, has_side_effects=True, vmem_limit_bytes=63 << 20), name="attend",
    )(tok, cot, docc, docr, vec, wq, wd, wu, ww, cosp, sina, sinb, mixh, mixl, mixt)

def gelu_pair(x):
    e = jnp.exp(-0.5 * x * x)
    t = 1.0 / (1.0 + (0.3275911 / math.sqrt(2.0)) * jnp.abs(x))
    poly = t * (0.254829592 + t * (-0.284496736 + t * (1.421413741 + t * (-1.453152027 + t * 1.061405429))))
    tail = 0.5 * poly * e
    phi = jnp.where(x >= 0, 1.0 - tail, tail)
    return x * phi, phi + x * e * (1.0 / math.sqrt(2.0 * math.pi))

def tables(seq, rot, head, feats):
    half = rot // 2
    angles = np.arange(seq)[:, None] / 10000.0 ** (np.arange(0, rot, 2) / rot)[None, :]
    cosp, sina, sinb = np.ones((seq, 128)), np.zeros((seq, 128)), np.zeros((seq, 128))
    for base in range(0, 128, head):
        cosp[:, base:base + half] = np.cos(angles)
        cosp[:, base + half:base + rot] = np.cos(angles)
        sina[:, base + half:base + rot] = np.sin(angles)
        sinb[:, base:base + half] = -np.sin(angles)
    k, i = np.arange(head)[:, None], np.arange(head)[None, :]
    cosine = np.where(k == 0, math.sqrt(1.0 / head), math.sqrt(2.0 / head)) * np.cos(math.pi * (i + 0.5) * k / head)
    j = np.arange(feats)[None, :]
    level = (((j * (2 * k + 1) + k) % feats) + 0.5) / feats
    normals = np.vectorize(NormalDist().inv_cdf)(level)
    mixing = cosine.T @ normals / math.sqrt(head)
    mix = np.zeros((128, 128), np.float32)
    for base in range(0, 128, head):
        mix[base:base + head, base:base + feats] = mixing
    return cosp.astype(np.float32), sina.astype(np.float32), sinb.astype(np.float32), mix


def feed_kernel(nf, nz, nh, *refs):
    (mlp_in, cot2, bu, bw, gq, gd, dy1, dy1in, out1, out1in, tok, vec, fw, gf,
     output, input_grad, out2in, dy2in, oq, od, ou, ow, ovec) = refs[:23]
    (mlp_v, cot_v, wu, ww, h, pre, aq, ad, au, aw) = refs[23:33]
    hold_u, hold_w = refs[33:33 + nh[0]], refs[33 + nh[0]:33 + sum(nh)]
    hq, hu, gv, vh, outs, igs, send, recv, local, free_u, free_w = refs[33 + sum(nh):]
    at = Place(nf, nz)
    nb = at.nbits
    sems = Sems(send, recv)
    c, p = at.core, 1 - at.core
    S, D = tok.shape
    T = 2 * S
    FH = h.shape[1]
    RT, FB = 512, 512
    every = (slice(None),) * nb
    at.greet(far=True)
    count = [0]

    def put(src, dst):
        cp = pltpu.make_async_copy(src, dst, local.at[count[0]])
        count[0] += 1
        cp.start()
        return cp

    load_g = [put(gq, aq), put(gd, ad)]
    load_m = [put(mlp_in, mlp_v), put(bu, wu)]
    load_c = [put(cot2, cot_v), put(bw, ww)]

    def streams_of(acc, holds, like):
        streams, it = [], iter(holds)
        for (start, size), (_, room), order in zip(shares(acc.shape[-2]), shares(like.shape[-2]), orders(nb)):
            if room:
                shapes = hold_shapes(nz, nb, size, acc.shape[-1], order)
                mine = [next(it) for _ in shapes]
                if size:
                    cut = [
                        hold.at[(slice(None),) * (len(s) - 2) + (pl.ds(0, s[-2]), pl.ds(0, s[-1]))]
                        for hold, s in zip(mine, shapes)
                    ]
                    streams.append(scatter_stream(at, sems, acc, cut, start, size, order))
        return streams

    def release(free):
        for b in range(nb):
            pl.semaphore_signal(free, inc=1, device_id=at.across(b), device_id_type=MESH)

        @pl.when(at.z > 0)
        def _():
            pl.semaphore_signal(free, inc=1, device_id=at.along(-1), device_id_type=MESH)

        @pl.when(at.z < nz - 1)
        def _():
            pl.semaphore_signal(free, inc=1, device_id=at.along(1), device_id_type=MESH)

    def wait_free(free):
        inner = (at.z > 0).astype(jnp.int32) + (at.z < nz - 1).astype(jnp.int32)
        pl.semaphore_wait(free, nb + inner)

    def once(act):
        done = []

        def run():
            if not done:
                act()
                done.append(1)

        return run

    agenda = Agenda()
    streams = streams_of(aq, hold_u, au)
    n_q = len(streams)
    streams += streams_of(ad, hold_w, aw)
    for cp in load_g:
        cp.wait()
    ends = agenda.add(streams, [(1.0, None)] * len(streams))
    end_q, end_d = max(ends[:n_q]), max(ends[n_q:])
    agenda.at(end_q + 0.1, lambda: release(free_u))
    agenda.at(end_d + 0.1, lambda: release(free_w))
    agenda.until(2.0)
    for cp in load_m + load_c:
        cp.wait()

    top = (FH // FB).bit_length() - 1
    wu2 = wu.reshape(D, FH)
    wu_all = lambda cols=slice(None): wu2[:, cols]
    ww2 = ww.reshape(FH, D)
    ww_all = lambda: ww2[...]

    def ww_rows(m):
        fixed = tuple((m >> b) & 1 for b in reversed(range(top)))
        return ww[fixed + (slice(None),) * (nb - top + 2)].reshape(FB, D)

    for m in range(FH // FB):
        cols = slice(m * FB, (m + 1) * FB)

        def hidden(i):
            r = tile(i, RT)
            act, slope = gelu_pair(dot(mlp_v[r, :], wu_all(cols)))
            h[r, cols] = act.astype(BF16)
            pre[r, cols] = (dot_nt(cot_v[r, :], ww_rows(m)) * slope).astype(BF16)

        agenda.loop(T // RT, hidden, 1.9)

    def gu(m):
        cols = tile(m, FB)
        au[every + (slice(None), cols)] = dot_tn(mlp_v[...], pre[:, cols]).astype(BF16).reshape(au.shape[:-1] + (FB,))

    agenda.loop(FH // FB, gu, 2.5)
    su = streams_of(au, hold_u, au)
    wait_u, wait_w = once(lambda: wait_free(free_u)), once(lambda: wait_free(free_w))
    end_u = max(agenda.add(su, [(max(agenda.now, end_q + 2.0), wait_u)] * len(su)))

    for m in range(FH // FB):
        fixed = tuple((m >> b) & 1 for b in reversed(range(top)))
        cols = slice(m * FB, (m + 1) * FB)

        def gw(i):
            val = dot_tn(h[:, cols], cot_v[...]).astype(BF16)
            aw[fixed + (slice(None),) * (nb - top + 2)] = val.reshape(aw.shape[top:])

        agenda.loop(1, gw, 2.5)
    sw = streams_of(aw, hold_w, aw)
    end_w = max(agenda.add(sw, [(max(agenda.now, end_d + 2.0), wait_w)] * len(sw)))

    def other(i):
        r = tile(i + p * (S // CH), CH)
        cot_v[tile(i, CH), :] = dot(h[r, :], ww_all()).astype(BF16)
        cot_v[tile(i + S // CH, CH), :] = dot_nt(pre[r, :], wu_all()).astype(BF16)

    agenda.loop(S // CH, other, 2.7)
    swaps = []
    for k, dst in enumerate((out2in, dy2in)):
        cp = sems.copy(cot_v.at[pl.ds(k * S, S)], dst, sems.take(), at.partner())
        cp.start()
        swaps.append(cp)

    gv[0] = jnp.zeros((8, D), F32)
    for m in range(gf.shape[1] // 128):
        s = slice(m * 128, (m + 1) * 128)
        gv[0, 4:5, pl.ds(pl.multiple_of((2 * m + c) * 128, 128), 128)] = jnp.sum(gf[:, s], axis=0, keepdims=True) / fw[:, s]
    first = count[0]

    def finish(i):
        r = tile(i, CH)
        mine = tile(i + c * (S // CH), CH)
        sources = (tok.at[r], cot2.at[mine], dy1.at[r], dy1in.at[r], out1.at[r], out1in.at[r], out2in.at[r], dy2in.at[r])
        loads = [
            pltpu.make_async_copy(src, mlp_v.at[pl.ds(k * CH, CH)], local.at[first + k]) for k, src in enumerate(sources)
        ]
        for cp in loads[:6]:
            cp.start()
        outs[...] = dot(h[mine, :], ww_all()).astype(BF16)
        igs[...] = dot_nt(pre[mine, :], wu_all())

        @pl.when(i == 0)
        def _():
            for cp in swaps:
                cp.wait_recv()

        for cp in loads[6:]:
            cp.start()
        for cp in loads:
            cp.wait()

        def rows(t, sums):
            part = tile(t, 32)
            get = lambda k: mlp_v[pl.ds(pl.multiple_of(k * CH + t * 32, 32), 32), :].astype(F32)
            x = get(0)
            n, rstd = normed(x)
            outs[part, :] = (x + (get(4) + get(5)) + (outs[part, :].astype(F32) + get(6))).astype(BF16)
            d1 = get(2) + get(3)
            d2 = igs[part, :] + get(7)
            dn = d1 * vec[0:1, :] + d2 * vec[2:3, :]
            dx = rstd * (dn - jnp.mean(dn, axis=-1, keepdims=True) - n * jnp.mean(dn * n, axis=-1, keepdims=True))
            igs[part, :] = get(1) + dx
            fold = lambda y: jnp.sum(y.reshape(4, 8, D), axis=0)
            return tuple(a + fold(y) for a, y in zip(sums, (d1 * n, d1, d2 * n, d2)))

        sums = lax.fori_loop(0, CH // 32, rows, (jnp.zeros((8, D), F32),) * 4)
        for k, y in enumerate(sums):
            gv[0, k:k + 1, :] += jnp.sum(y, axis=0, keepdims=True)
        stores = [
            pltpu.make_async_copy(outs, output.at[r], local.at[first + 8]),
            pltpu.make_async_copy(igs, input_grad.at[r], local.at[first + 9]),
        ]
        for cp in stores:
            cp.start()
        for cp in stores:
            cp.wait()

    agenda.loop(S // CH, finish, 6.0)

    peers = [at.partner()] + [at.across(b) for b in range(nb)]
    step = 1
    while step < nz:
        peers.append(at.fold(step))
        step *= 2
    rounds = []
    for k, peer in enumerate(peers):
        cp = sems.copy(gv.at[k], vh.at[k], sems.take(), peer)

        def arrive(cp=cp, k=k):
            cp.wait_recv()
            gv[k + 1] = gv[k] + vh[k]

        rounds.append((cp.start, arrive, cp.wait_send, "small", 4.0 * 8 * D))
    agenda.add([rounds], [(agenda.now, None)])
    me = at.slot(())
    sent = []
    for acc, hold, out, end in ((aq, hq, oq, end_q), (au, hu, ou, end_u)):
        half = hold.shape[0]
        cols = at.columns(acc, at.z)
        cp = sems.copy(acc.at[me + (tile(p, half), cols)], hold, sems.take(), at.partner())

        def act(cp=cp, acc=acc, out=out, half=half, cols=cols):
            cp.start()
            out[c] = acc[me + (tile(c, half), cols)]

        def arrive(cp=cp, hold=hold, out=out):
            cp.wait_recv()
            out[p] = hold[...]

        begin = max(end + 0.1, agenda.now)
        agenda.at(begin, act)
        agenda.at(begin + 4.0, arrive)
        sent.append(cp)

    def keep(acc, out):
        out[...] = acc[me + (slice(None), at.columns(acc, at.z))]

    agenda.at(max(end_d + 0.1, agenda.now), lambda: keep(ad, od))
    agenda.at(end_w + 0.1, lambda: keep(aw, ow))
    agenda.until(1e9)
    ovec[...] = gv[len(peers)]
    for cp in swaps + sent:
        cp.wait_send()
    for s in streams + su + sw + [rounds]:
        for r in s:
            r[2]()


def feed(nf, nz, mlp_in, cot2, bu, bw, gq, gd, dy1, dy1in, out1, out1in, tok, vec, fw, gf):
    sd = jax.ShapeDtypeStruct
    bits = (2,) * ((nf // 2).bit_length() - 1)
    nb, chips = len(bits), nf // 2
    cut = lambda g: g.reshape(bits + (g.shape[0] // chips, g.shape[1]))
    aq, ad = cut(gq), cut(gd)
    S, D = tok.shape
    T, FH = 2 * S, bu.shape[-1]
    own = lambda a: (a.shape[-2], a.shape[-1] // nz)

    def holds(a):
        shapes = []
        for (_, size), order in zip(shares(a.shape[-2]), orders(nb)):
            if size:
                shapes += hold_shapes(nz, nb, size, a.shape[-1], order)
        return shapes

    hu, hw = holds(bu), holds(bw)
    halves = [(own(a)[0] // 2, own(a)[1]) for a in (aq, bu)]
    nsteps = 1 + nb + nz.bit_length() - 1
    ncopies = 12 * copies_of(nz, nb) + 2 + nsteps + 2
    vm, hb = pl.BlockSpec(memory_space=pltpu.VMEM), pl.BlockSpec(memory_space=pl.ANY)
    v = lambda shape: pltpu.VMEM(shape, BF16)
    outs = [sd((S, D), BF16), sd((S, D), F32), sd((S, D), BF16), sd((S, D), BF16)]
    outs += [sd((2,) + halves[0], BF16), sd(own(ad), BF16), sd((2,) + halves[1], BF16), sd(own(bw), BF16), sd((8, D), F32)]
    return pl.pallas_call(
        partial(feed_kernel, nf, nz, (len(hu), len(hw))), out_shape=outs,
        in_specs=[hb] * 11 + [vm] * 3, out_specs=[hb] * 4 + [vm] * 5,
        scratch_shapes=[v((T, D)), v((T, D)), v(bu.shape), v(bw.shape), v((T, FH)), v((T, FH)), v(aq.shape), v(ad.shape), v(bu.shape), v(bw.shape)]
        + [v(s) for s in hu + hw] + [v(s) for s in halves]
        + [pltpu.VMEM((nsteps + 1, 8, D), F32), pltpu.VMEM((nsteps, 8, D), F32), v((CH, D)), pltpu.VMEM((CH, D), F32)]
        + [pltpu.SemaphoreType.DMA((ncopies,)), pltpu.SemaphoreType.DMA((ncopies,)), pltpu.SemaphoreType.DMA((16,))]
        + [pltpu.SemaphoreType.REGULAR, pltpu.SemaphoreType.REGULAR],
        compiler_params=pltpu.CompilerParams(collective_id=1, has_side_effects=True, vmem_limit_bytes=63 << 20), name="feed",
    )(mlp_in, cot2, bu, bw, aq, ad, dy1, dy1in, out1, out1in, tok, vec, fw, gf)

def body(nf, nz, tokens, doc_starts, w_qkv, w_dense, w_up, w_down, norm1_gain, norm1_bias, norm2_gain, norm2_bias, feature_weight, cotangent):
    rows, D = tokens.shape
    unit = w_down.shape[0]

    def turn(w, block):
        r, n = w.shape
        return w.reshape(r, n // (2 * block), 2, block).transpose(2, 0, 1, 3).reshape(2, r, n // 2)

    def unturn(g, block):
        _, r, n = g.shape
        return g.reshape(2, r, n // block, block).transpose(1, 2, 0, 3).reshape(r, 2 * n)

    per = 128 // w_dense.shape[0]
    source = [(2 * (k // per) + c) * per + k % per for k in range(nf // 2) for c in range(2)]
    if per > 1:
        w_dense = lax.ppermute(w_dense, "fsdp", [(s, d) for d, s in enumerate(source)])

    doc = jnp.cumsum(doc_starts.reshape(-1, SEQ_LEN), axis=1).astype(jnp.int32).reshape(rows)
    vec = jnp.stack([norm1_gain, norm1_bias, norm2_gain, norm2_bias, feature_weight] + [jnp.zeros_like(norm1_gain)] * 3)
    cosp, sina, sinb, mix = tables(SEQ_LEN, ROT, HEAD, FEATS)
    mix = jnp.asarray(mix)
    mixh = mix.astype(BF16)
    mixl = (mix - mixh.astype(F32)).astype(BF16)
    cot2, mlp_in, bu, bw, gq, gd, dy1, dy1in, out1, out1in, vec8, fw, gf = attend(
        nf, nz, HEAD, ROT, tokens, cotangent, jnp.broadcast_to(doc[:, None], (rows, 128)), doc.reshape(-1, 1, CH), vec,
        turn(w_qkv, 128), w_dense, turn(w_up, unit), w_down, cosp, sina, sinb, mixh, mixl, mixh.T,
    )
    output, input_grad, _, _, oq, od, ou, ow, gv = feed(
        nf, nz, mlp_in, cot2, bu, bw, gq, gd, dy1, dy1in, out1, out1in, tokens, vec8, fw, gf
    )
    if per > 1:
        od = lax.ppermute(od, "fsdp", [(d, s) for d, s in enumerate(source)])
    own = gv.reshape(8, nf, -1)
    own = lax.dynamic_index_in_dim(own, lax.axis_index("fsdp"), 1, keepdims=False)
    return (
        output, input_grad,
        unturn(oq, 128).astype(F32), od.astype(F32), unturn(ou, unit).astype(F32), ow.astype(F32),
        own[0], own[1], own[2], own[3], own[4],
    )


def solution(mesh):
    nf, nz = mesh.shape["fsdp"], mesh.shape["inner"]
    rows, mat, vec = P(("fsdp", "inner"), None), P("fsdp", "inner"), P("fsdp")
    in_specs = (rows, P(("fsdp", "inner"))) + (mat,) * 4 + (vec,) * 5 + (rows,)
    out_specs = (rows, rows) + (mat,) * 4 + (vec,) * 5
    return jax.shard_map(partial(body, nf, nz), mesh=mesh, in_specs=in_specs, out_specs=out_specs, check_vma=False)
```

```python
from functools import partial
import math
from statistics import NormalDist

import jax
import jax.numpy as jnp
import numpy as np
from jax import lax
from jax.experimental import pallas as pl
from jax.experimental.pallas import tpu as pltpu
from jax.sharding import PartitionSpec as P

MESH = pl.DeviceIdType.MESH
BF16 = jnp.bfloat16
F32 = jnp.float32


HEAD = 64
ROT = 16
FEATS = 64
SEQ_LEN = 1024

class Place:
    def __init__(self, nf, nz):
        self.nf, self.nz = nf, nz
        self.nbits = (nf // 2).bit_length() - 1
        self.f = lax.axis_index("fsdp")
        self.z = lax.axis_index("inner")
        self.core = lax.rem(self.f, 2)
        self.bits = [lax.rem(lax.div(self.f, 2 << b), 2) for b in range(self.nbits)]

    def partner(self):
        return (self.f + 1 - 2 * self.core, self.z)

    def across(self, b):
        return (self.f + (1 - 2 * self.bits[b]) * (2 << b), self.z)

    def along(self, step):
        return (self.f, self.z + step)

    def slot(self, done, flip=None):
        index = []
        for b in reversed(range(self.nbits)):
            if b in done:
                index.append(slice(None))
            elif b == flip:
                index.append(1 - self.bits[b])
            else:
                index.append(self.bits[b])
        return tuple(index)

    def columns(self, buf, zsel):
        if zsel is None:
            return slice(None)
        width = buf.shape[-1] // self.nz
        return pl.ds(pl.multiple_of(zsel * width, width), width)

    def greet(self, far=False):
        bar = pltpu.get_barrier_semaphore()
        z, nz = self.z, self.nz
        fixed = [self.partner()] + [self.across(b) for b in range(self.nbits)]
        for peer in fixed:
            pl.semaphore_signal(bar, inc=1, device_id=peer, device_id_type=MESH)

        @pl.when(z > 0)
        def _():
            pl.semaphore_signal(bar, inc=1, device_id=self.along(-1), device_id_type=MESH)

        @pl.when(z < nz - 1)
        def _():
            pl.semaphore_signal(bar, inc=1, device_id=self.along(1), device_id_type=MESH)

        count = len(fixed)
        if far and nz > 2:
            step = 2
            while step < nz:
                pl.semaphore_signal(
                    bar, inc=1, device_id=self.fold(step), device_id_type=MESH
                )
                count += 1
                step *= 2
        inner = (z > 0).astype(jnp.int32) + (z < nz - 1).astype(jnp.int32)
        pl.semaphore_wait(bar, count + inner)

    def fold(self, step):
        bit = lax.rem(lax.div(self.z, step), 2)
        return (self.f, self.z + (1 - 2 * bit) * step)


class Sems:
    def __init__(self, send, recv):
        self.send, self.recv, self.count = send, recv, 0

    def take(self):
        self.count += 1
        return self.count - 1

    def copy(self, src, dst, i, peer):
        return pltpu.make_async_remote_copy(
            src_ref=src,
            dst_ref=dst,
            send_sem=self.send.at[i],
            recv_sem=self.recv.at[i],
            device_id=peer,
            device_id_type=MESH,
        )


def streams_of(rows, nbits):
    up, down = list(range(nbits)), list(reversed(range(nbits)))
    orders = [["z"] + up, ["z"] + down, up + ["z"]]
    parts, units, at = [3, 3, 2], rows // 16, 0
    cuts = []
    for k, order in enumerate(orders):
        end = round(units * sum(parts[:k + 1]) / sum(parts))
        if end > at:
            cuts.append((at * 16, (end - at) * 16, order))
        at = end
    return cuts


def copies_of(nz, nbits):
    return nbits + 2 * (nz - 1)


def gather_stream(at, sems, buf, start, size, order):
    rows = pl.ds(start, size)
    rounds = []
    done, zdone = (), False

    def along(k, done):
        ids = (sems.take(), sems.take())

        def right(zsel):
            ref = buf.at[at.slot(done) + (rows, at.columns(buf, zsel))]
            return sems.copy(ref, ref, ids[0], at.along(1))

        def left(zsel):
            ref = buf.at[at.slot(done) + (rows, at.columns(buf, zsel))]
            return sems.copy(ref, ref, ids[1], at.along(-1))

        z, nz = at.z, at.nz
        goes_right = (z < nz - 1) & (z - k + 1 >= 0)
        goes_left = (z > 0) & (z + k - 1 <= nz - 1)

        def send():
            pl.when(goes_right)(lambda: right(z - k + 1).start())
            pl.when(goes_left)(lambda: left(z + k - 1).start())

        def arrive():
            pl.when(z - k >= 0)(lambda: right(z - k).wait_recv())
            pl.when(z + k <= nz - 1)(lambda: left(z + k).wait_recv())

        def leave():
            pl.when(goes_right)(lambda: right(z - k + 1).wait_send())
            pl.when(goes_left)(lambda: left(z + k - 1).wait_send())

        return send, arrive, leave

    def across(b, done, zsel):
        i = sems.take()
        mine = buf.at[at.slot(done) + (rows, at.columns(buf, zsel))]
        theirs = buf.at[at.slot(done, flip=b) + (rows, at.columns(buf, zsel))]
        out = sems.copy(mine, mine, i, at.across(b))
        back = sems.copy(theirs, theirs, i, at.across(b))
        return out.start, back.wait_recv, out.wait_send

    piece = size * (buf.shape[-1] // at.nz) * 2
    for dim in order:
        if dim == "z":
            rounds += [along(k, done) + ("z", piece << len(done)) for k in range(1, at.nz)]
            zdone = True
        else:
            nbytes = (piece << len(done)) * (at.nz if zdone else 1)
            rounds.append(across(dim, done, None if zdone else at.z) + (dim, nbytes))
            done = done + (dim,)
    return rounds


def scatter_stream(at, sems, acc, holds, start, size, order):
    rows = pl.ds(start, size)
    rounds = []
    left_bits, zleft = set(range(at.nbits)), True

    def along(k, remaining, hold):
        ids = (sems.take(), sems.take())
        z, nz = at.z, at.nz

        def part(zsel):
            return acc.at[at.slot(remaining) + (rows, at.columns(acc, zsel))]

        def right(zsel):
            return sems.copy(part(zsel), hold.at[2 * k - 2], ids[0], at.along(1))

        def left(zsel):
            return sems.copy(part(zsel), hold.at[2 * k - 1], ids[1], at.along(-1))

        goes_right = z + k <= nz - 1
        goes_left = z - k >= 0

        def send():
            pl.when(goes_right)(lambda: right(z + k).start())
            pl.when(goes_left)(lambda: left(z - k).start())

        def arrive():
            @pl.when((z >= 1) & (z - 1 + k <= nz - 1))
            def _():
                right(z - 1 + k).wait_recv()
                ref = part(z - 1 + k)
                ref[...] += hold[2 * k - 2]

            @pl.when((z <= nz - 2) & (z + 1 - k >= 0))
            def _():
                left(z + 1 - k).wait_recv()
                ref = part(z + 1 - k)
                ref[...] += hold[2 * k - 1]

        def leave():
            pl.when(goes_right)(lambda: right(z + k).wait_send())
            pl.when(goes_left)(lambda: left(z - k).wait_send())

        return send, arrive, leave

    def across(b, remaining, zsel, hold):
        i = sems.take()
        out = sems.copy(
            acc.at[at.slot(remaining, flip=b) + (rows, at.columns(acc, zsel))], hold, i, at.across(b)
        )

        def arrive():
            out.wait_recv()
            ref = acc.at[at.slot(remaining) + (rows, at.columns(acc, zsel))]
            ref[...] += hold[...]

        return out.start, arrive, out.wait_send

    piece = size * (acc.shape[-1] // at.nz) * 2
    holds = iter(holds)
    for dim in reversed(order):
        if dim == "z":
            hold = next(holds)
            rounds += [
                along(k, tuple(left_bits), hold) + ("z", piece << len(left_bits))
                for k in range(at.nz - 1, 0, -1)
            ]
            zleft = False
        else:
            left_bits = left_bits - {dim}
            nbytes = (piece << len(left_bits)) * (at.nz if zleft else 1)
            rounds.append(across(dim, tuple(left_bits), None if zleft else at.z, next(holds)) + (dim, nbytes))
    return rounds


def hold_shapes(nz, nbits, size, width, order):
    shapes, bits, zleft = [], nbits, True
    for dim in reversed(order):
        if dim == "z":
            shapes.append((2 * (nz - 1),) + (2,) * bits + (size, width // nz))
            zleft = False
        else:
            bits -= 1
            shapes.append((2,) * bits + (size, width if zleft else width // nz))
    return shapes


LINK_RATE = 45000.0
HOP = 1.5


class Agenda:
    def __init__(self):
        self.events, self.now, self.free = [], 0.0, {}

    def add(self, streams, ready, rank=None):
        rank = rank or [0] * len(streams)
        took = [[rounds[r][4] / LINK_RATE for r in range(len(rounds))] for rounds in streams]
        left = [[sum(t[r:]) + HOP * (len(t) - r) for r in range(len(t) + 1)] for t in took]
        state = [[0, t] for t, _ in ready]
        while True:
            best = None
            for i, rounds in enumerate(streams):
                r, t = state[i]
                if r < len(rounds):
                    begin = max(t, self.free.get(rounds[r][3], 0.0))
                    key = (begin, rank[i], -left[i][r], i)
                    best = key if best is None or key < best else best
            if best is None:
                break
            begin, i = best[0], best[3]
            r = state[i][0]
            rounds = streams[i]
            wait = ready[i][1] if r == 0 else rounds[r - 1][1]

            def act(wait=wait, send=rounds[r][0]):
                if wait is not None:
                    wait()
                send()

            self.events.append((begin, act))
            self.free[rounds[r][3]] = begin + took[i][r]
            state[i] = [r + 1, begin + took[i][r] + HOP]
            if r + 1 == len(rounds):
                self.events.append((state[i][1], rounds[r][1]))
        self.events.sort(key=lambda e: e[0])
        return [t for _, t in state]

    def at(self, time, act):
        self.events.append((time, act))
        self.events.sort(key=lambda e: e[0])

    def until(self, time):
        while self.events and self.events[0][0] <= time:
            self.events.pop(0)[1]()
        self.now = max(self.now, time)

    def loop(self, n, body, took):
        due = [[] for _ in range(n)]
        while self.events and self.events[0][0] < self.now + n * took:
            time, act = self.events.pop(0)
            due[max(0, int((time - self.now) / took))].append(act)
        self.now += n * took

        def step(i, carry):
            for u, acts in enumerate(due):
                if acts:

                    @pl.when(i == u)
                    def _(acts=acts):
                        for act in acts:
                            act()

            body(i)
            return carry

        lax.fori_loop(0, n, step, 0)


def once(acts):
    done = []

    def run():
        if not done:
            for act in acts:
                act()
            done.append(1)

    return run


class Copies:
    def __init__(self, at, sems, local):
        self.at, self.sems, self.local, self.count, self.sent = at, sems, local, 0, []

    def put(self, src, dst):
        cp = pltpu.make_async_copy(src, dst, self.local.at[self.count])
        self.count += 1
        cp.start()
        return cp

    def swap(self, src, dst, arrives):
        i = self.sems.take()
        cp = self.sems.copy(src, dst, i, self.at.partner())
        cp.start()
        self.sent.append(cp)
        return self.sems.copy(src, arrives, i, self.at.partner()).wait_recv

    def leave(self):
        for cp in self.sent:
            cp.wait_send()


CH = 256

def dot(a, b):
    return jnp.dot(a, b, preferred_element_type=F32)

def dot_nt(a, b):
    return lax.dot_general(a, b, (((1,), (1,)), ((), ())), preferred_element_type=F32)

def dot_tn(a, b):
    return lax.dot_general(a, b, (((0,), (0,)), ((), ())), preferred_element_type=F32)

def tile(i, n):
    return pl.ds(pl.multiple_of(i * n, n), n)

def lanes(width):
    return lax.broadcasted_iota(jnp.int32, (1, width), 1)

def normed(x):
    center = x - jnp.mean(x, axis=-1, keepdims=True)
    spread = jnp.mean(center * center, axis=-1, keepdims=True)
    rstd = lax.rsqrt(spread + 1e-05)
    return center * rstd, rstd

def gelu_pair(x):
    e = jnp.exp2((-0.5 * math.log2(math.e)) * (x * x))
    d = 1.0 + (0.3275911 / math.sqrt(2.0)) * jnp.abs(x)
    t = 1.0 / d
    poly = t * (0.127414796 + t * (-0.142248368 + t * (0.7107068705 + t * (-0.7265760135 + t * 0.5307027145))))
    tail = poly * e
    phi = jnp.where(x >= 0, 1.0 - tail, tail)
    return x * phi, phi + x * e * (1.0 / math.sqrt(2.0 * math.pi))


def tables(seq, rot, head, feats):
    half = rot // 2
    angles = np.arange(seq)[:, None] / 10000.0 ** (np.arange(0, rot, 2) / rot)[None, :]
    cosp, sina, sinb = np.ones((seq, 128)), np.zeros((seq, 128)), np.zeros((seq, 128))
    for base in range(0, 128, head):
        cosp[:, base:base + half] = np.cos(angles)
        cosp[:, base + half:base + rot] = np.cos(angles)
        sina[:, base + half:base + rot] = np.sin(angles)
        sinb[:, base:base + half] = -np.sin(angles)
    k, i = np.arange(head)[:, None], np.arange(head)[None, :]
    cosine = np.where(k == 0, math.sqrt(1.0 / head), math.sqrt(2.0 / head)) * np.cos(math.pi * (i + 0.5) * k / head)
    j = np.arange(feats)[None, :]
    level = (((j * (2 * k + 1) + k) % feats) + 0.5) / feats
    normals = np.vectorize(NormalDist().inv_cdf)(level)
    mixing = cosine.T @ normals / math.sqrt(head)
    mix = np.zeros((128, 128), np.float32)
    for base in range(0, 128, head):
        mix[base:base + head, base:base + feats] = mixing
    return cosp.astype(np.float32), sina.astype(np.float32), sinb.astype(np.float32), mix


def feed_kernel(nf, nz, tok, cot, vec1, wq1, wd1, wu1, ww1,
                attn_in, cot2, bq, bd, gu2, gw2, out2, out2in, dy2, dy2in, vec, fw,
                tok_v, mlp_v, cot_v, wu, ww, h, pre, gu, gw, vecs, send, recv, local):
    at = Place(nf, nz)
    nb = at.nbits
    sems = Sems(send, recv)
    copies = Copies(at, sems, local)
    put, swap = copies.put, copies.swap
    c, p = at.core, 1 - at.core
    S, D = tok.shape
    T = 2 * S
    FH = h.shape[1]
    RT, FB = 512, 512
    every = (slice(None),) * nb
    me = at.slot(())
    own_rows, other_rows = tile(c, S), tile(p, S)
    at.greet()

    def piece(buf, w, i):
        r = w.shape[-2]
        return buf.at[me + (tile(i, r), at.columns(buf, at.z))]

    z = lambda b: at.columns(b, at.z)
    in_u = [swap(wu1.at[p], piece(wu, wu1, c), piece(wu, wu1, p)), put(wu1.at[c], piece(wu, wu1, c)).wait]
    in_vec = [swap(vec1, vecs.at[me + (c,)], vecs.at[me + (p,)]), put(vec1, vecs.at[me + (c,)]).wait]
    in_tok = [put(tok, tok_v.at[own_rows]).wait, swap(tok, tok_v.at[own_rows], tok_v.at[other_rows])]
    in_w = [put(ww1, ww.at[me + (slice(None), z(ww))]).wait]
    in_q = [swap(wq1.at[p], piece(bq, wq1, c), piece(bq, wq1, p)), put(wq1.at[c], piece(bq, wq1, c)).wait]
    in_d = [put(wd1, bd.at[me + (slice(None), z(bd))]).wait]
    in_cot = [put(cot, cot_v.at[own_rows]).wait, swap(cot, cot_v.at[own_rows], cot_v.at[other_rows])]

    agenda = Agenda()
    streams, ready, rank, ends = [], [], [], []
    for buf, waits, time, r in ((wu, in_u, 2.0, 0), (ww, in_w, 2.0, 1), (bq, in_q, 12.0, 2), (bd, in_d, 4.0, 2)):
        wait = once(waits)
        for start, size, order in streams_of(buf.shape[-2], nb):
            streams.append(gather_stream(at, sems, buf, start, size, order))
            ready.append((time, wait))
            rank.append(r)
    ends = agenda.add(streams, ready, rank)
    end_u, end_w = (max(e for e, r in zip(ends, rank) if r == k) for k in (0, 1))
    agenda.until(4.0)
    for w in in_vec:
        w()
    done, small = (), []
    for b in range(nb):
        i = sems.take()
        m, t = vecs.at[at.slot(done)], vecs.at[at.slot(done, flip=b)]
        out = sems.copy(m, m, i, at.across(b))
        out.start()
        sems.copy(t, t, i, at.across(b)).wait_recv()
        small.append(out)
        done = done + (b,)
    w = vec1.shape[1]
    for f in range(nf):
        at_f = tuple((f >> (b + 1)) & 1 for b in reversed(range(nb))) + (f & 1,)
        vec[:, f * w:(f + 1) * w] = vecs[at_f]
    for m in range(fw.shape[1] // 128):
        fw[:, m * 128:(m + 1) * 128] = vec[4:5, pl.ds(pl.multiple_of((2 * m + c) * 128, 128), 128)]
    agenda.until(11.0)
    for w in in_tok:
        w()

    def ln(i):
        r = tile(i, CH)
        n, _ = normed(tok_v[r, :].astype(F32))
        tok_v[r, :] = (n * vec[0:1, :] + vec[1:2, :]).astype(BF16)
        mlp_v[r, :] = (n * vec[2:3, :] + vec[3:4, :]).astype(BF16)

    agenda.loop(T // CH, ln, 0.5)
    stores = [put(tok_v, attn_in)]
    agenda.until(end_u)

    top = (FH // FB).bit_length() - 1
    bits_of = lambda m: tuple((m >> b) & 1 for b in reversed(range(top))) + (slice(None),) * (nb - top)
    wu2, ww2 = wu.reshape(D, FH), ww.reshape(FH, D)

    for m in range(FH // FB):
        cols = slice(m * FB, (m + 1) * FB)

        def hidden(i, cols=cols):
            r = tile(i, RT)
            act, slope = gelu_pair(dot(mlp_v[r, :], wu2[:, cols]))
            h[r, cols] = act.astype(BF16)
            pre[r, cols] = slope.astype(BF16)

        agenda.loop(T // RT, hidden, 1.1)
    for w in in_cot:
        w()
    keep_cot = put(cot_v, cot2)
    gu_flat, gw_flat = gu.reshape(D, FH), gw.reshape(FH, D)

    def grad_down(m):
        gw_flat[tile(m, FB), :] = dot_tn(h[:, tile(m, FB)], cot_v[...]).astype(BF16)

    agenda.loop(FH // FB, grad_down, 2.4)
    stores.append(put(gw, gw2))
    agenda.until(end_w)

    for m in range(FH // FB):
        cols = slice(m * FB, (m + 1) * FB)

        def slopes(i, cols=cols, m=m):
            r = tile(i, RT)
            dh = dot_nt(cot_v[r, :], ww2[cols, :])
            pre[r, cols] = (dh * pre[r, cols].astype(F32)).astype(BF16)

        agenda.loop(T // RT, slopes, 0.75)


    def grad_up(m):
        gu_flat[:, tile(m, FB)] = dot_tn(mlp_v[...], pre[:, tile(m, FB)]).astype(BF16)

    agenda.loop(FH // FB, grad_up, 2.5)
    stores.append(put(gu, gu2))

    keep_cot.wait()

    def back(i, rows, into):
        r = tile(i + rows * (S // RT), RT)
        into[tile(i, RT), :] = dot(h[r, :], ww2[...]).astype(BF16)
        into[tile(i + S // RT, RT), :] = dot_nt(pre[r, :], wu2[...]).astype(BF16)

    agenda.loop(S // RT, lambda i: back(i, p, cot_v), 5.0)
    arrive = [
        swap(cot_v.at[pl.ds(0, S)], out2in, out2in),
        swap(cot_v.at[pl.ds(S, S)], dy2in, dy2in),
    ]
    agenda.loop(S // RT, lambda i: back(i, c, mlp_v), 5.0)
    stores += [put(mlp_v.at[pl.ds(0, S)], out2), put(mlp_v.at[pl.ds(S, S)], dy2)]
    agenda.until(1e9)
    for w in arrive:
        w()
    for cp in stores:
        cp.wait()
    copies.leave()
    for cp in small:
        cp.wait_send()
    for s in streams:
        for r in s:
            r[2]()


def feed(nf, nz, tok, cot, vec, wq, wd, wu, ww):
    bits = (2,) * ((nf // 2).bit_length() - 1)
    nb = len(bits)
    S, D = tok.shape
    T, W = 2 * S, D // 2
    sd = jax.ShapeDtypeStruct
    hb, vm = pl.BlockSpec(memory_space=pl.ANY), pl.BlockSpec(memory_space=pltpu.VMEM)
    full_u = bits + (2 * wu.shape[1], nz * wu.shape[2])
    full_w = bits + (ww.shape[0], nz * ww.shape[1])
    full_q = bits + (2 * wq.shape[1], nz * wq.shape[2])
    full_d = bits + (wd.shape[0], nz * wd.shape[1])
    FH = full_u[-1]
    outs = [sd((T, D), BF16), sd((T, D), BF16), sd(full_q, BF16), sd(full_d, BF16), sd(full_u, BF16), sd(full_w, BF16)]
    outs += [sd((S, D), BF16)] * 4 + [sd((8, D), F32), sd((1, W), F32)]
    n = 7 + nb + 12 * copies_of(nz, nb)
    v = lambda *shape: pltpu.VMEM(shape, BF16)
    return pl.pallas_call(
        partial(feed_kernel, nf, nz), out_shape=outs,
        in_specs=[hb] * 7, out_specs=[hb] * 10 + [vm] * 2,
        scratch_shapes=[
            v(T, D), v(T, D), v(T, D), v(*full_u), v(*full_w), v(T, FH), v(T, FH), v(*full_u), v(*full_w),
            pltpu.VMEM(bits + (2,) + vec.shape, F32),
            pltpu.SemaphoreType.DMA((n,)), pltpu.SemaphoreType.DMA((n,)), pltpu.SemaphoreType.DMA((16,)),
        ],
        compiler_params=pltpu.CompilerParams(collective_id=0, has_side_effects=True, vmem_limit_bytes=63 << 20),
        name="feed",
    )(tok, cot, vec, wq, wd, wu, ww)


def attend_kernel(nf, nz, head, rot, nh, *refs):
    (attn_in, cot2, bq2, bd2, gu, gw, out2, out2in, dy2, dy2in, tok, docc1, docr1,
     vec, fw, cosp, sina, sinb, mixh, mixl, mixt,
     output, input_grad, oq, od, ou, ow, ovec) = refs[:28]
    (attn_v, cot_v, bq, bd, qkv, dd, do, o, st, cur, docc, docr, aq, ad, au, aw) = refs[28:44]
    hold_u, hold_w, hold_d = refs[44:44 + nh[0]], refs[44 + nh[0]:44 + nh[0] + nh[1]], refs[44 + nh[0] + nh[1]:44 + sum(nh)]
    hq, hu, gv, vh, gf, outs, igs, send, recv, local, free_u, free_d = refs[44 + sum(nh):]
    at = Place(nf, nz)
    nb = at.nbits
    sems = Sems(send, recv)
    copies = Copies(at, sems, local)
    put, swap = copies.put, copies.swap
    c, p = at.core, 1 - at.core
    S, D = tok.shape
    T = 2 * S
    width = D // 2
    npair = width // 128
    seq = cosp.shape[0]
    nch = T // CH
    half = rot // 2
    RT, FT = 512, outs.shape[1]
    every = (slice(None),) * nb
    own_rows, other_rows = tile(c, S), tile(p, S)
    at.greet(far=True)

    in_g = [put(gu, au), put(gw, aw)]
    in_p = [put(attn_in, attn_v), put(bq2, bq), put(cot2, cot_v), put(bd2, bd)]
    n1 = docr1.shape[0]
    in_doc = [
        put(docc1, docc.at[own_rows]).wait, swap(docc1, docc.at[own_rows], docc.at[other_rows]),
        put(docr1, docr.at[tile(c, n1)]).wait, swap(docr1, docr.at[tile(c, n1)], docr.at[tile(p, n1)]),
    ]

    def scatters(acc, holds, like=None):
        streams, it = [], iter(holds)
        for start, size, order in streams_of(acc.shape[-2], nb):
            shapes = hold_shapes(nz, nb, size, acc.shape[-1], order)
            mine = [next(it) for _ in shapes]
            if like is not None:
                mine = [hold.at[(slice(None),) * (len(s) - 1) + (pl.ds(0, s[-1]),)] for hold, s in zip(mine, shapes)]
            streams.append(scatter_stream(at, sems, acc, mine, start, size, order))
        return streams

    def release(free):
        for b in range(nb):
            pl.semaphore_signal(free, inc=1, device_id=at.across(b), device_id_type=MESH)

        @pl.when(at.z > 0)
        def _():
            pl.semaphore_signal(free, inc=1, device_id=at.along(-1), device_id_type=MESH)

        @pl.when(at.z < nz - 1)
        def _():
            pl.semaphore_signal(free, inc=1, device_id=at.along(1), device_id_type=MESH)

    def wait_free(free):
        inner = (at.z > 0).astype(jnp.int32) + (at.z < nz - 1).astype(jnp.int32)
        pl.semaphore_wait(free, nb + inner)

    agenda = Agenda()
    su, sw = scatters(au, hold_u), scatters(aw, hold_w)
    for cp in in_g:
        cp.wait()
    ends = agenda.add(su + sw, [(1.0, None)] * (len(su) + len(sw)))
    end_u, end_w = max(ends[:len(su)]), max(ends[len(su):])
    agenda.at(end_u + 0.1, lambda: release(free_u))
    agenda.until(2.0)
    for cp in in_p:
        cp.wait()

    wq = bq.reshape(D, 3 * width)
    wd = bd.reshape(width, D)

    def project(i):
        r = tile(i, RT)
        ps = tile(lax.rem(i, seq // RT), RT)
        a = attn_v[r, :]
        for part in range(2):
            x = dot(a, wq[:, part * width:(part + 1) * width])
            for m in range(npair):
                s = slice(m * 128, (m + 1) * 128)
                y = x[:, s]
                y = y * cosp[ps, :] + pltpu.roll(y, half, 1) * sina[ps, :] + pltpu.roll(y, 128 - half, 1) * sinb[ps, :]
                hi = y.astype(BF16)
                lo = (y - hi.astype(F32)).astype(BF16)
                e = dot(hi, mixh[...]) + dot(lo, mixh[...]) + dot(hi, mixl[...])
                qkv[r, part * width + s.start:part * width + s.stop] = (fw[:, s] * jnp.exp(e)).astype(BF16)
        qkv[r, 2 * width:] = dot(a, wq[:, 2 * width:]).astype(BF16)
        do[r, :] = dot_nt(cot_v[r, :], wd[...]).astype(BF16)

    agenda.loop(T // RT, project, 3.9)
    for w in in_doc:
        w()

    h0 = (lanes(128) % (2 * head)) < head
    h0w = jnp.concatenate([h0, h0], axis=1)
    rowh = lax.broadcasted_iota(jnp.int32, (128, 1), 0) < head
    block = rowh == h0w
    same = (rowh == h0).astype(BF16)
    one = jnp.ones((CH, 128), BF16)
    zero = jnp.zeros((), BF16)
    place = lanes(128) % head
    causal = lax.broadcasted_iota(jnp.int32, (CH, 1), 0) >= lanes(CH)

    def split(x):
        hi = x.astype(BF16)
        return hi, (x - hi.astype(F32)).astype(BF16)

    def masks(i):
        d = docc[tile(i, CH), :]
        inside = jnp.where(causal & (jnp.concatenate([d, d], axis=1) == docr[i]), 1.0, 0.0)
        start = lax.rem(i, seq // CH) == 0
        before = jnp.where(start, -1, docc[pl.ds(jnp.maximum(i * CH - 1, 0), 1), :])
        last = docc[pl.ds(i * CH + CH - 1, 1), :]
        ones = lambda x: jnp.where(x, 1.0, 0.0)
        return inside, ones(d == before), ones(d == last), ones(before == last)

    twice = lambda x: jnp.concatenate([x, x], axis=1)

    def scores(q, k, m):
        s0 = dot_nt(jnp.where(h0, q, zero), k)
        s1 = dot_nt(jnp.where(h0, zero, q), k)
        return (s0 * m).astype(BF16), (s1 * m).astype(BF16)

    cur[...] = jnp.zeros_like(cur)

    def forward(i):
        r = tile(i, CH)
        m, cr, tr, kp = masks(i)
        cw, kpw = twice(cr), twice(kp)
        for j in range(npair):
            s = slice(j * 128, (j + 1) * 128)
            q, k, v = (qkv[r, x * width + s.start:x * width + s.stop] for x in range(3))
            va = jnp.concatenate([v, one], axis=1)
            p0, p1 = scores(q, k, m)
            state = cur[j]
            hi, lo = split(state)
            st[i, j, 0] = hi
            st[i, j, 1] = lo
            res = dot(p0, jnp.where(h0w, va, zero)) + dot(p1, jnp.where(h0w, zero, va)) + cw * (dot(q, hi) + dot(q, lo))
            rd = 1.0 / res[:, 128:]
            att = res[:, :128] * rd
            o[r, s] = att.astype(BF16)
            dnb = (do[r, s].astype(F32) * rd).astype(BF16)
            do[r, s] = dnb
            hi, lo = split(dnb.astype(F32) * att)
            hi, lo = split(-(dot(hi, same) + dot(lo, same)))
            dd[r, s] = jnp.where(place == 0, hi, jnp.where(place == 1, lo, zero))
            kt = (k.astype(F32) * tr).astype(BF16)
            cur[j] = kpw * state + jnp.where(block, dot_tn(kt, va), 0.0)
    agenda.loop(nch, forward, 1.95)

    def grad_dense(i):
        ad[...] = dot_tn(o[...], cot_v[...]).astype(BF16).reshape(ad.shape)

    agenda.loop(1, grad_dense, 3.0)
    sdn = scatters(ad, hold_d)
    end_d = max(agenda.add(sdn, [(agenda.now, None)] * len(sdn)))

    cur[...] = jnp.zeros_like(cur)
    gf[...] = jnp.zeros_like(gf)

    def backward(ii):
        i = nch - 1 - ii
        r = tile(i, CH)
        ps = tile(lax.rem(i, seq // CH), CH)
        m, cr, tr, kp = masks(i)
        kpw = twice(kp)
        cos, sa, sb = cosp[ps, :], sina[ps, :], sinb[ps, :]

        def unfeature(d, f, s, base):
            de = d * f.astype(F32)
            gf[:, s] += jnp.sum(de.reshape(CH // 8, 8, 128), axis=0)
            g = dot(de.astype(BF16), mixt[...])
            g = g * cos + pltpu.roll(g * sa, 128 - half, 1) + pltpu.roll(g * sb, half, 1)
            qkv[r, base + s.start:base + s.stop] = g.astype(BF16)

        for j in range(npair):
            s = slice(j * 128, (j + 1) * 128)
            q, k, v = (qkv[r, x * width + s.start:x * width + s.stop] for x in range(3))
            va = jnp.concatenate([v, one], axis=1)
            p0, p1 = scores(q, k, m)
            dnb = do[r, s]
            dy = jnp.concatenate([dnb, dd[r, s]], axis=1)
            ds0 = (dot_nt(dy, jnp.where(h0w, va, zero)) * m).astype(BF16)
            ds1 = (dot_nt(dy, jnp.where(h0w, zero, va)) * m).astype(BF16)
            dst = cur[j]
            dhi, dlo = split(dst)
            dq = dot(ds0, jnp.where(h0, k, zero)) + dot(ds1, jnp.where(h0, zero, k)) + cr * (dot_nt(dy, st[i, j, 0]) + dot_nt(dy, st[i, j, 1]))
            dk = dot_tn(ds0, jnp.where(h0, q, zero)) + dot_tn(ds1, jnp.where(h0, zero, q)) + tr * (dot_nt(va, dhi) + dot_nt(va, dlo))
            dv = dot_tn(p0, jnp.where(h0, dnb, zero)) + dot_tn(p1, jnp.where(h0, zero, dnb)) + tr * dot(k, dhi[:, :128])
            qc = (q.astype(F32) * cr).astype(BF16)
            cur[j] = kpw * dst + jnp.where(block, dot_tn(qc, dy), 0.0)
            unfeature(dq, q, s, 0)
            unfeature(dk, k, s, width)
            qkv[r, 2 * width + s.start:2 * width + s.stop] = dv.astype(BF16)
    agenda.loop(nch, backward, 3.15)


    pl.semaphore_signal(free_d, inc=1, device_id=at.partner(), device_id_type=MESH)
    st_flat = st.reshape(st.shape[0] * st.shape[1] * 2 * 128, 256)

    def cut(ref, width, at_row=0):
        return [ref.at[pl.ds(at_row + k * S, S)] for k in range(D // width)]

    def fetch(src, parts):
        w = D // len(parts)
        return [put(src.at[:, pl.ds(k * w, w)], part) for k, part in enumerate(parts)]

    fetched = fetch(out2in, cut(st_flat, 256)) + fetch(dy2, cut(st_flat, 256, 4 * S))
    fetched.append(put(dy2in, cot_v.at[other_rows]))

    def grad_qkv(i):
        val = dot_tn(attn_v[...], qkv[:, tile(i, width)]).astype(BF16)
        aq[every + (slice(None), tile(i, width))] = val.reshape(aq.shape[:-1] + (width,))

    agenda.loop(3, grad_qkv, 2.4)
    sq = scatters(aq, hold_u, au)
    wait_u = once([lambda: wait_free(free_u)])
    end_q = max(agenda.add(sq, [(max(agenda.now, end_u + 2.0), wait_u)] * len(sq)))

    def back_qkv(i, rows):
        r = tile(i + rows * (S // RT), RT)
        attn_v[r, :] = dot_nt(qkv[r, :], wq[...]).astype(BF16)

    def back_dense(i, rows):
        r = tile(i + rows * (S // RT), RT)
        qkv[r, :D] = dot(o[r, :], wd[...]).astype(BF16)

    def send_back(src, dst):
        return [
            swap(src.at[other_rows, pl.ds(k * width, width)], part, part) for k, part in enumerate(cut(dst, width))
        ]

    agenda.loop(S // RT, lambda i: back_qkv(i, p), 1.9)
    pl.semaphore_wait(free_d, 1)
    arrive = send_back(attn_v, do)
    agenda.loop(S // RT, lambda i: back_dense(i, p), 0.7)
    arrive += send_back(qkv, dd)
    agenda.loop(S // RT, lambda i: back_qkv(i, c), 1.9)
    fetched.append(put(out2, wq.at[pl.ds(0, S), pl.ds(0, D)]))
    agenda.loop(S // RT, lambda i: back_dense(i, c), 0.7)
    fetched += fetch(tok, cut(o, width))
    agenda.until(agenda.now)

    gv[0] = jnp.zeros((8, D), F32)
    for m in range(npair):
        s = slice(m * 128, (m + 1) * 128)
        gv[0, 4:5, pl.ds(pl.multiple_of((2 * m + c) * 128, 128), 128)] = jnp.sum(gf[:, s], axis=0, keepdims=True) / fw[:, s]
    for cp in fetched:
        cp.wait()
    for w in arrive:
        w()
    first = copies.count

    def stores(i):
        k, r = lax.rem(i, 2), tile(i, FT)
        return [
            pltpu.make_async_copy(outs.at[k], output.at[r], local.at[first + 2 * k]),
            pltpu.make_async_copy(igs.at[k], input_grad.at[r], local.at[first + 2 * k + 1]),
        ]

    def finish(i):
        k = lax.rem(i, 2)

        @pl.when(i >= 2)
        def _():
            for cp in stores(i - 2):
                cp.wait()

        def rows(t, sums):
            part = tile(t, 32)
            at_row = i * FT + t * 32
            own = pl.ds(pl.multiple_of(at_row + c * S, 32), 32)

            def joined(ref, n, base=0):
                return jnp.concatenate(
                    [ref[pl.ds(pl.multiple_of(at_row + base + q * S, 32), 32), :] for q in range(n)], axis=1
                ).astype(F32)

            here = pl.ds(pl.multiple_of(at_row, 32), 32)
            x = joined(o, D // width)
            n, rstd = normed(x)
            out1 = qkv[own, :D].astype(F32) + joined(dd, D // width)
            outs[k, part, :] = (x + out1 + (wq[here, :D].astype(F32) + joined(st_flat, D // 256))).astype(BF16)
            d1 = attn_v[own, :].astype(F32) + joined(do, D // width)
            d2 = joined(st_flat, D // 256, 4 * S) + cot_v[pl.ds(pl.multiple_of(at_row + p * S, 32), 32), :].astype(F32)
            dn = d1 * vec[0:1, :] + d2 * vec[2:3, :]
            dx = rstd * (dn - jnp.mean(dn, axis=-1, keepdims=True) - n * jnp.mean(dn * n, axis=-1, keepdims=True))
            igs[k, part, :] = cot_v[own, :].astype(F32) + dx
            fold = lambda y: jnp.sum(y.reshape(4, 8, D), axis=0)
            return tuple(a + fold(y) for a, y in zip(sums, (d1 * n, d1, d2 * n, d2)))

        sums = lax.fori_loop(0, FT // 32, rows, (jnp.zeros((8, D), F32),) * 4)
        for q, y in enumerate(sums):
            gv[0, q:q + 1, :] += jnp.sum(y, axis=0, keepdims=True)
        for cp in stores(i):
            cp.start()

    agenda.loop(S // FT, finish, 1.5)
    for i in range(S // FT - 2, S // FT):
        for cp in stores(i):
            cp.wait()

    peers = [at.partner()] + [at.across(b) for b in range(nb)]
    step = 1
    while step < nz:
        peers.append(at.fold(step))
        step *= 2
    rounds = []
    for k, peer in enumerate(peers):
        cp = sems.copy(gv.at[k], vh.at[k], sems.take(), peer)

        def arrive(cp=cp, k=k):
            cp.wait_recv()
            gv[k + 1] = gv[k] + vh[k]

        rounds.append((cp.start, arrive, cp.wait_send, "small", 4.0 * 8 * D))
    agenda.add([rounds], [(agenda.now, None)])
    me = at.slot(())
    sent = []
    for acc, hold, out, end in ((aq, hq, oq, end_q), (au, hu, ou, end_u)):
        half = hold.shape[0]
        cols = at.columns(acc, at.z)
        cp = sems.copy(acc.at[me + (tile(p, half), cols)], hold, sems.take(), at.partner())

        def act(cp=cp, acc=acc, out=out, half=half, cols=cols):
            cp.start()
            out[c] = acc[me + (tile(c, half), cols)]

        def arrive(cp=cp, hold=hold, out=out):
            cp.wait_recv()
            out[p] = hold[...]

        begin = max(end + 0.1, agenda.now)
        agenda.at(begin, act)
        agenda.at(begin + 4.0, arrive)
        sent.append(cp)

    def keep(acc, out):
        out[...] = acc[me + (slice(None), at.columns(acc, at.z))]

    agenda.at(max(end_d + 0.1, agenda.now), lambda: keep(ad, od))
    agenda.at(end_w + 0.1, lambda: keep(aw, ow))
    agenda.until(1e9)
    ovec[...] = gv[len(peers)]
    copies.leave()
    for cp in sent:
        cp.wait_send()
    for s in su + sw + sdn + sq + [rounds]:
        for r in s:
            r[2]()


def attend(nf, nz, head, rot, attn_in, cot2, bq, bd, gu, gw, out2, out2in, dy2, dy2in, tok, docc, docr, vec, fw, *tabs):
    sd = jax.ShapeDtypeStruct
    nb = (nf // 2).bit_length() - 1
    S, D = tok.shape
    T, W = 2 * S, D // 2
    own = lambda a: (a.shape[-2], a.shape[-1] // nz)

    def holds(a):
        shapes = []
        for _, size, order in streams_of(a.shape[-2], nb):
            shapes += hold_shapes(nz, nb, size, a.shape[-1], order)
        return shapes

    room = [holds(a) for a in (gu, gw, bd)]
    halves = [(own(a)[0] // 2, own(a)[1]) for a in (bq, gu)]
    nsteps = 1 + nb + nz.bit_length() - 1
    ncopies = 12 * copies_of(nz, nb) + 6 + nsteps + 2
    vm, hb = pl.BlockSpec(memory_space=pltpu.VMEM), pl.BlockSpec(memory_space=pl.ANY)
    v = lambda *shape: pltpu.VMEM(shape, BF16)
    f = lambda *shape: pltpu.VMEM(shape, F32)
    i32 = lambda *shape: pltpu.VMEM(shape, jnp.int32)
    outs = [sd((S, D), BF16), sd((S, D), F32)]
    outs += [sd((2,) + halves[0], BF16), sd(own(bd), BF16), sd((2,) + halves[1], BF16), sd(own(gw), BF16), sd((8, D), F32)]
    return pl.pallas_call(
        partial(attend_kernel, nf, nz, head, rot, tuple(len(r) for r in room)), out_shape=outs,
        in_specs=[hb] * 13 + [vm] * 8, out_specs=[hb] * 2 + [vm] * 5,
        scratch_shapes=[
            v(T, D), v(T, D), v(*bq.shape), v(*bd.shape), v(T, 3 * W), v(T, W), v(T, W), v(T, W),
            v(T // CH, W // 128, 2, 128, 256), f(W // 128, 128, 256), i32(T, 128), i32(2 * docr.shape[0], 1, CH),
            v(*bq.shape), v(*bd.shape), v(*gu.shape), v(*gw.shape),
        ]
        + [v(*s) for r in room for s in r] + [v(*s) for s in halves]
        + [f(nsteps + 1, 8, D), f(nsteps, 8, D), f(8, W), v(2, 128, D), f(2, 128, D)]
        + [pltpu.SemaphoreType.DMA((ncopies,)), pltpu.SemaphoreType.DMA((ncopies,)), pltpu.SemaphoreType.DMA((28,))]
        + [pltpu.SemaphoreType.REGULAR] * 2,
        compiler_params=pltpu.CompilerParams(collective_id=1, has_side_effects=True, vmem_limit_bytes=63 << 20),
        name="attend",
    )(attn_in, cot2, bq, bd, gu, gw, out2, out2in, dy2, dy2in, tok, docc, docr, vec, fw, *tabs)


def body(nf, nz, tokens, doc_starts, w_qkv, w_dense, w_up, w_down, norm1_gain, norm1_bias, norm2_gain, norm2_bias, feature_weight, cotangent):
    rows, D = tokens.shape
    unit = w_down.shape[0]

    def turn(w, block):
        r, n = w.shape
        return w.reshape(r, n // (2 * block), 2, block).transpose(2, 0, 1, 3).reshape(2, r, n // 2)

    def unturn(g, block):
        _, r, n = g.shape
        return g.reshape(2, r, n // block, block).transpose(1, 2, 0, 3).reshape(r, 2 * n)

    per = 128 // w_dense.shape[0]
    source = [(2 * (k // per) + c) * per + k % per for k in range(nf // 2) for c in range(2)]
    if per > 1:
        w_dense = lax.ppermute(w_dense, "fsdp", [(s, d) for d, s in enumerate(source)])

    doc = jnp.cumsum(doc_starts.reshape(-1, SEQ_LEN), axis=1).astype(jnp.int32).reshape(rows)
    vec = jnp.stack([norm1_gain, norm1_bias, norm2_gain, norm2_bias, feature_weight] + [jnp.zeros_like(norm1_gain)] * 3)
    cosp, sina, sinb, mix = tables(SEQ_LEN, ROT, HEAD, FEATS)
    mix = jnp.asarray(mix)
    mixh = mix.astype(BF16)
    mixl = (mix - mixh.astype(F32)).astype(BF16)
    attn_in, cot2, bq, bd, gu, gw, out2, out2in, dy2, dy2in, vec8, fw = feed(
        nf, nz, tokens, cotangent, vec, turn(w_qkv, 128), w_dense, turn(w_up, unit), w_down
    )
    output, input_grad, oq, od, ou, ow, gv = attend(
        nf, nz, HEAD, ROT, attn_in, cot2, bq, bd, gu, gw, out2, out2in, dy2, dy2in, tokens,
        jnp.broadcast_to(doc[:, None], (rows, 128)), doc.reshape(-1, 1, CH), vec8, fw, cosp, sina, sinb, mixh, mixl, mixh.T,
    )
    if per > 1:
        od = lax.ppermute(od, "fsdp", [(d, s) for d, s in enumerate(source)])
    own = gv.reshape(8, nf, -1)
    own = lax.dynamic_index_in_dim(own, lax.axis_index("fsdp"), 1, keepdims=False)
    return (
        output, input_grad,
        unturn(oq, 128).astype(F32), od.astype(F32), unturn(ou, unit).astype(F32), ow.astype(F32),
        own[0], own[1], own[2], own[3], own[4],
    )


def solution(mesh):
    nf, nz = mesh.shape["fsdp"], mesh.shape["inner"]
    rows, mat, vec = P(("fsdp", "inner"), None), P("fsdp", "inner"), P("fsdp")
    in_specs = (rows, P(("fsdp", "inner"))) + (mat,) * 4 + (vec,) * 5 + (rows,)
    out_specs = (rows, rows) + (mat,) * 4 + (vec,) * 5
    return jax.shard_map(partial(body, nf, nz), mesh=mesh, in_specs=in_specs, out_specs=out_specs, check_vma=False)
```

```python
from functools import partial
import math
from statistics import NormalDist

import jax
import jax.numpy as jnp
import numpy as np
from jax import lax
from jax.experimental import pallas as pl
from jax.experimental.pallas import tpu as pltpu
from jax.sharding import PartitionSpec as P

MESH = pl.DeviceIdType.MESH
BF16 = jnp.bfloat16
F32 = jnp.float32


HEAD = 64
ROT = 16
FEATS = 64
SEQ_LEN = 1024

class Place:
    def __init__(self, nf, nz):
        self.nf, self.nz = nf, nz
        self.nbits = (nf // 2).bit_length() - 1
        self.f = lax.axis_index("fsdp")
        self.z = lax.axis_index("inner")
        self.core = lax.rem(self.f, 2)
        self.bits = [lax.rem(lax.div(self.f, 2 << b), 2) for b in range(self.nbits)]

    def partner(self):
        return (self.f + 1 - 2 * self.core, self.z)

    def across(self, b):
        return (self.f + (1 - 2 * self.bits[b]) * (2 << b), self.z)

    def along(self, step):
        return (self.f, self.z + step)

    def slot(self, done, flip=None):
        index = []
        for b in reversed(range(self.nbits)):
            if b in done:
                index.append(slice(None))
            elif b == flip:
                index.append(1 - self.bits[b])
            else:
                index.append(self.bits[b])
        return tuple(index)

    def columns(self, buf, zsel):
        if zsel is None:
            return slice(None)
        width = buf.shape[-1] // self.nz
        return pl.ds(pl.multiple_of(zsel * width, width), width)

    def greet(self, far=False):
        bar = pltpu.get_barrier_semaphore()
        z, nz = self.z, self.nz
        fixed = [self.partner()] + [self.across(b) for b in range(self.nbits)]
        for peer in fixed:
            pl.semaphore_signal(bar, inc=1, device_id=peer, device_id_type=MESH)

        @pl.when(z > 0)
        def _():
            pl.semaphore_signal(bar, inc=1, device_id=self.along(-1), device_id_type=MESH)

        @pl.when(z < nz - 1)
        def _():
            pl.semaphore_signal(bar, inc=1, device_id=self.along(1), device_id_type=MESH)

        count = len(fixed)
        if far and nz > 2:
            step = 2
            while step < nz:
                pl.semaphore_signal(
                    bar, inc=1, device_id=self.fold(step), device_id_type=MESH
                )
                count += 1
                step *= 2
        inner = (z > 0).astype(jnp.int32) + (z < nz - 1).astype(jnp.int32)
        pl.semaphore_wait(bar, count + inner)

    def fold(self, step):
        bit = lax.rem(lax.div(self.z, step), 2)
        return (self.f, self.z + (1 - 2 * bit) * step)


class Sems:
    def __init__(self, send, recv):
        self.send, self.recv, self.count = send, recv, 0

    def take(self):
        self.count += 1
        return self.count - 1

    def copy(self, src, dst, i, peer):
        return pltpu.make_async_remote_copy(
            src_ref=src,
            dst_ref=dst,
            send_sem=self.send.at[i],
            recv_sem=self.recv.at[i],
            device_id=peer,
            device_id_type=MESH,
        )


def streams_of(rows, nbits, cuts=1):
    up, down = list(range(nbits)), list(reversed(range(nbits)))
    parts = [(3, ["z"] + up), (3, ["z"] + down)] * cuts + [(2, up + ["z"]), (2, down + ["z"])][:cuts]
    whole, units, at, streams = sum(n for n, _ in parts), rows // 16, 0, []
    for k, (_, order) in enumerate(parts):
        end = round(units * sum(n for n, _ in parts[:k + 1]) / whole)
        if end > at:
            streams.append((at * 16, (end - at) * 16, order))
        at = end
    return streams


def copies_of(nz, nbits):
    return nbits + 2 * (nz - 1)


def gather_stream(at, sems, buf, start, size, order):
    rows = pl.ds(start, size)
    rounds = []
    done, zdone = (), False

    def along(k, done):
        ids = (sems.take(), sems.take())

        def right(zsel):
            ref = buf.at[at.slot(done) + (rows, at.columns(buf, zsel))]
            return sems.copy(ref, ref, ids[0], at.along(1))

        def left(zsel):
            ref = buf.at[at.slot(done) + (rows, at.columns(buf, zsel))]
            return sems.copy(ref, ref, ids[1], at.along(-1))

        z, nz = at.z, at.nz
        goes_right = (z < nz - 1) & (z - k + 1 >= 0)
        goes_left = (z > 0) & (z + k - 1 <= nz - 1)

        def send():
            pl.when(goes_right)(lambda: right(z - k + 1).start())
            pl.when(goes_left)(lambda: left(z + k - 1).start())

        def arrive():
            pl.when(z - k >= 0)(lambda: right(z - k).wait_recv())
            pl.when(z + k <= nz - 1)(lambda: left(z + k).wait_recv())

        def leave():
            pl.when(goes_right)(lambda: right(z - k + 1).wait_send())
            pl.when(goes_left)(lambda: left(z + k - 1).wait_send())

        return send, arrive, leave

    def across(b, done, zsel):
        i = sems.take()
        mine = buf.at[at.slot(done) + (rows, at.columns(buf, zsel))]
        theirs = buf.at[at.slot(done, flip=b) + (rows, at.columns(buf, zsel))]
        out = sems.copy(mine, mine, i, at.across(b))
        back = sems.copy(theirs, theirs, i, at.across(b))
        return out.start, back.wait_recv, out.wait_send

    piece = size * (buf.shape[-1] // at.nz) * 2
    for dim in order:
        if dim == "z":
            rounds += [along(k, done) + ("z", piece << len(done)) for k in range(1, at.nz)]
            zdone = True
        else:
            nbytes = (piece << len(done)) * (at.nz if zdone else 1)
            rounds.append(across(dim, done, None if zdone else at.z) + (dim, nbytes))
            done = done + (dim,)
    return rounds


def scatter_stream(at, sems, acc, holds, start, size, order):
    rows = pl.ds(start, size)
    rounds = []
    left_bits, zleft = set(range(at.nbits)), True

    def along(k, remaining, hold):
        ids = (sems.take(), sems.take())
        z, nz = at.z, at.nz

        def part(zsel):
            return acc.at[at.slot(remaining) + (rows, at.columns(acc, zsel))]

        def right(zsel):
            return sems.copy(part(zsel), hold.at[2 * k - 2], ids[0], at.along(1))

        def left(zsel):
            return sems.copy(part(zsel), hold.at[2 * k - 1], ids[1], at.along(-1))

        goes_right = z + k <= nz - 1
        goes_left = z - k >= 0

        def send():
            pl.when(goes_right)(lambda: right(z + k).start())
            pl.when(goes_left)(lambda: left(z - k).start())

        def arrive():
            @pl.when((z >= 1) & (z - 1 + k <= nz - 1))
            def _():
                right(z - 1 + k).wait_recv()
                ref = part(z - 1 + k)
                ref[...] += hold[2 * k - 2]

            @pl.when((z <= nz - 2) & (z + 1 - k >= 0))
            def _():
                left(z + 1 - k).wait_recv()
                ref = part(z + 1 - k)
                ref[...] += hold[2 * k - 1]

        def leave():
            pl.when(goes_right)(lambda: right(z + k).wait_send())
            pl.when(goes_left)(lambda: left(z - k).wait_send())

        return send, arrive, leave

    def across(b, remaining, zsel, hold):
        i = sems.take()
        out = sems.copy(
            acc.at[at.slot(remaining, flip=b) + (rows, at.columns(acc, zsel))], hold, i, at.across(b)
        )

        def arrive():
            out.wait_recv()
            ref = acc.at[at.slot(remaining) + (rows, at.columns(acc, zsel))]
            ref[...] += hold[...]

        return out.start, arrive, out.wait_send

    piece = size * (acc.shape[-1] // at.nz) * 2
    holds = iter(holds)
    for dim in reversed(order):
        if dim == "z":
            hold = next(holds)
            rounds += [
                along(k, tuple(left_bits), hold) + ("z", piece << len(left_bits))
                for k in range(at.nz - 1, 0, -1)
            ]
            zleft = False
        else:
            left_bits = left_bits - {dim}
            nbytes = (piece << len(left_bits)) * (at.nz if zleft else 1)
            rounds.append(across(dim, tuple(left_bits), None if zleft else at.z, next(holds)) + (dim, nbytes))
    return rounds


def hold_shapes(nz, nbits, size, width, order):
    shapes, bits, zleft = [], nbits, True
    for dim in reversed(order):
        if dim == "z":
            shapes.append((2 * (nz - 1),) + (2,) * bits + (size, width // nz))
            zleft = False
        else:
            bits -= 1
            shapes.append((2,) * bits + (size, width if zleft else width // nz))
    return shapes


LINK_RATE = 48000.0


class Agenda:
    def __init__(self, hop):
        self.hop, self.events, self.now, self.free = hop, [], 0.0, {}

    def add(self, streams, ready, rank=None):
        rank = rank or [0] * len(streams)
        took = [[rounds[r][4] / LINK_RATE for r in range(len(rounds))] for rounds in streams]
        left = [[sum(t[r:]) + self.hop * (len(t) - r) for r in range(len(t) + 1)] for t in took]
        state = [[0, t] for t, _ in ready]
        while True:
            best = None
            for i, rounds in enumerate(streams):
                r, t = state[i]
                if r < len(rounds):
                    begin = max(t, self.free.get(rounds[r][3], 0.0))
                    key = (begin, rank[i], -left[i][r], i)
                    best = key if best is None or key < best else best
            if best is None:
                break
            begin, i = best[0], best[3]
            r = state[i][0]
            rounds = streams[i]
            wait = ready[i][1] if r == 0 else rounds[r - 1][1]

            def act(wait=wait, send=rounds[r][0]):
                if wait is not None:
                    wait()
                send()

            self.events.append((begin, act))
            self.free[rounds[r][3]] = begin + took[i][r]
            state[i] = [r + 1, begin + took[i][r] + self.hop]
            if r + 1 == len(rounds):
                self.events.append((state[i][1], rounds[r][1]))
        self.events.sort(key=lambda e: e[0])
        return [t for _, t in state]

    def at(self, time, act):
        self.events.append((time, act))
        self.events.sort(key=lambda e: e[0])

    def until(self, time):
        while self.events and self.events[0][0] <= time:
            self.events.pop(0)[1]()
        self.now = max(self.now, time)

    def loop(self, n, body, took):
        due = [[] for _ in range(n)]
        while self.events:
            step = max(0, math.ceil((self.events[0][0] - self.now) / took - 0.5))
            if step >= n:
                break
            due[step].append(self.events.pop(0)[1])
        self.now += n * took

        def step(i, carry):
            for u, acts in enumerate(due):
                if acts:

                    @pl.when(i == u)
                    def _(acts=acts):
                        for act in acts:
                            act()

            body(i)
            return carry

        lax.fori_loop(0, n, step, 0)


def once(acts):
    done = []

    def run():
        if not done:
            for act in acts:
                act()
            done.append(1)

    return run


class Copies:
    def __init__(self, at, sems, local):
        self.at, self.sems, self.local, self.count, self.sent = at, sems, local, 0, []

    def put(self, src, dst):
        cp = pltpu.make_async_copy(src, dst, self.local.at[self.count])
        self.count += 1
        cp.start()
        return cp

    def swap(self, src, dst, arrives):
        i = self.sems.take()
        cp = self.sems.copy(src, dst, i, self.at.partner())
        cp.start()
        self.sent.append(cp)
        return self.sems.copy(src, arrives, i, self.at.partner()).wait_recv

    def leave(self):
        for cp in self.sent:
            cp.wait_send()


CH = 256

def dot(a, b):
    return jnp.dot(a, b, preferred_element_type=F32)

def dot_nt(a, b):
    return lax.dot_general(a, b, (((1,), (1,)), ((), ())), preferred_element_type=F32)

def dot_tn(a, b):
    return lax.dot_general(a, b, (((0,), (0,)), ((), ())), preferred_element_type=F32)

def tile(i, n):
    return pl.ds(pl.multiple_of(i * n, n), n)

def lanes(width):
    return lax.broadcasted_iota(jnp.int32, (1, width), 1)

def normed(x):
    center = x - jnp.mean(x, axis=-1, keepdims=True)
    spread = jnp.mean(center * center, axis=-1, keepdims=True)
    rstd = lax.rsqrt(spread + 1e-05)
    return center * rstd, rstd

def gelu_pair(x):
    e = jnp.exp2((-0.5 * math.log2(math.e)) * (x * x))
    d = 1.0 + (0.3275911 / math.sqrt(2.0)) * jnp.abs(x)
    t = 1.0 / d
    poly = t * (0.127414796 + t * (-0.142248368 + t * (0.7107068705 + t * (-0.7265760135 + t * 0.5307027145))))
    tail = poly * e
    phi = jnp.where(x >= 0, 1.0 - tail, tail)
    return x * phi, phi + x * e * (1.0 / math.sqrt(2.0 * math.pi))


def tables(seq, rot, head, feats):
    half = rot // 2
    angles = np.arange(seq)[:, None] / 10000.0 ** (np.arange(0, rot, 2) / rot)[None, :]
    cosp, sina, sinb = np.ones((seq, 128)), np.zeros((seq, 128)), np.zeros((seq, 128))
    for base in range(0, 128, head):
        cosp[:, base:base + half] = np.cos(angles)
        cosp[:, base + half:base + rot] = np.cos(angles)
        sina[:, base + half:base + rot] = np.sin(angles)
        sinb[:, base:base + half] = -np.sin(angles)
    k, i = np.arange(head)[:, None], np.arange(head)[None, :]
    cosine = np.where(k == 0, math.sqrt(1.0 / head), math.sqrt(2.0 / head)) * np.cos(math.pi * (i + 0.5) * k / head)
    j = np.arange(feats)[None, :]
    level = (((j * (2 * k + 1) + k) % feats) + 0.5) / feats
    normals = np.vectorize(NormalDist().inv_cdf)(level)
    mixing = cosine.T @ normals / math.sqrt(head)
    mix = np.zeros((128, 128), np.float32)
    for base in range(0, 128, head):
        mix[base:base + head, base:base + feats] = mixing
    return cosp.astype(np.float32), sina.astype(np.float32), sinb.astype(np.float32), mix


def feed_kernel(nf, nz, unit, tok, cot, vec1, wq1, wd1, wu1, ww1,
                attn_in, cot2, bq, bd, gu2, gw2, out2, out2in, dy2, dy2in, vec, fw,
                tok_v, mlp_v, cot_v, wu, ww, h, pre, gu, gw, vecs, send, recv, local):
    at = Place(nf, nz)
    nb = at.nbits
    sems = Sems(send, recv)
    copies = Copies(at, sems, local)
    put, swap = copies.put, copies.swap
    c, p = at.core, 1 - at.core
    S, D = tok.shape
    T = 2 * S
    FH = h.shape[1]
    RT, FB = 512, 512
    every = (slice(None),) * nb
    me = at.slot(())
    own_rows, other_rows = tile(c, S), tile(p, S)
    at.greet()

    def halves(w, buf, block):
        r, n = w.shape
        here, there = [], []
        for t in range(n // (2 * block)):
            def part(core, t=t):
                return w.at[:, pl.ds(pl.multiple_of((2 * t + core) * block, block), block)]

            def place(core, t=t):
                cols = pl.ds(pl.multiple_of(at.z * (n // 2) + t * block, 128), block)
                return buf.at[me + (tile(core, r), cols)]

            there.append(swap(part(p), place(c), place(p)))
            here.append(put(part(c), place(c)).wait)
        return there + here

    z = lambda b: at.columns(b, at.z)
    in_u = halves(wu1, wu, unit)
    in_vec = [swap(vec1, vecs.at[me + (c,)], vecs.at[me + (p,)]), put(vec1, vecs.at[me + (c,)]).wait]
    in_tok = [put(tok, tok_v.at[own_rows]).wait, swap(tok, tok_v.at[own_rows], tok_v.at[other_rows])]
    in_w = [put(ww1, ww.at[me + (slice(None), z(ww))]).wait]
    in_q = halves(wq1, bq, 128)
    in_d = [put(wd1, bd.at[me + (slice(None), z(bd))]).wait]
    in_cot = [put(cot, cot_v.at[own_rows]).wait, swap(cot, cot_v.at[own_rows], cot_v.at[other_rows])]

    agenda = Agenda(4.5)
    streams, ready, rank, ends = [], [], [], []
    for buf, waits, time, r, cuts in (
        (wu, in_u, 2.0, 0, 2), (ww, in_w, 2.0, 1, 1), (bq, in_q, 12.0, 2, 1), (bd, in_d, 4.0, 2, 1)
    ):
        wait = once(waits)
        for start, size, order in streams_of(buf.shape[-2], nb, cuts):
            streams.append(gather_stream(at, sems, buf, start, size, order))
            ready.append((time, wait))
            rank.append(r)
    ends = agenda.add(streams, ready, rank)
    end_u, end_w = (max(e for e, r in zip(ends, rank) if r == k) for k in (0, 1))
    agenda.until(4.0)
    for w in in_vec:
        w()
    done, small = (), []
    for b in range(nb):
        i = sems.take()
        m, t = vecs.at[at.slot(done)], vecs.at[at.slot(done, flip=b)]
        out = sems.copy(m, m, i, at.across(b))
        out.start()
        sems.copy(t, t, i, at.across(b)).wait_recv()
        small.append(out)
        done = done + (b,)
    w = vec1.shape[1]
    for f in range(nf):
        at_f = tuple((f >> (b + 1)) & 1 for b in reversed(range(nb))) + (f & 1,)
        vec[:, f * w:(f + 1) * w] = vecs[at_f]
    for m in range(fw.shape[1] // 128):
        fw[:, m * 128:(m + 1) * 128] = vec[4:5, pl.ds(pl.multiple_of((2 * m + c) * 128, 128), 128)]
    agenda.until(11.0)
    for w in in_tok:
        w()

    def ln(i):
        r = tile(i, CH)
        n, _ = normed(tok_v[r, :].astype(F32))
        tok_v[r, :] = (n * vec[0:1, :] + vec[1:2, :]).astype(BF16)
        mlp_v[r, :] = (n * vec[2:3, :] + vec[3:4, :]).astype(BF16)

    agenda.loop(T // CH, ln, 0.5)
    stores = [put(tok_v, attn_in)]
    agenda.until(end_u)

    top = (FH // FB).bit_length() - 1
    bits_of = lambda m: tuple((m >> b) & 1 for b in reversed(range(top))) + (slice(None),) * (nb - top)
    wu2, ww2 = wu.reshape(D, FH), ww.reshape(FH, D)

    for m in range(FH // FB):
        cols = slice(m * FB, (m + 1) * FB)

        def hidden(i, cols=cols):
            r = tile(i, RT)
            act, slope = gelu_pair(dot(mlp_v[r, :], wu2[:, cols]))
            h[r, cols] = act.astype(BF16)
            pre[r, cols] = slope.astype(BF16)

        agenda.loop(T // RT, hidden, 1.1)
    for w in in_cot:
        w()
    keep_cot = put(cot_v, cot2)
    gu_flat, gw_flat = gu.reshape(D, FH), gw.reshape(FH, D)

    def grad_down(m):
        gw_flat[tile(m, FB), :] = dot_tn(h[:, tile(m, FB)], cot_v[...]).astype(BF16)

    agenda.loop(FH // FB, grad_down, 2.4)
    stores.append(put(gw, gw2))
    agenda.until(end_w)

    for m in range(FH // FB):
        cols = slice(m * FB, (m + 1) * FB)

        def slopes(i, cols=cols, m=m):
            r = tile(i, RT)
            dh = dot_nt(cot_v[r, :], ww2[cols, :])
            pre[r, cols] = (dh * pre[r, cols].astype(F32)).astype(BF16)

        agenda.loop(T // RT, slopes, 0.75)


    def grad_up(m):
        gu_flat[:, tile(m, FB)] = dot_tn(mlp_v[...], pre[:, tile(m, FB)]).astype(BF16)

    agenda.loop(FH // FB, grad_up, 2.5)
    stores.append(put(gu, gu2))

    keep_cot.wait()

    def back(i, rows, into):
        r = tile(i + rows * (S // RT), RT)
        into[tile(i, RT), :] = dot(h[r, :], ww2[...]).astype(BF16)
        into[tile(i + S // RT, RT), :] = dot_nt(pre[r, :], wu2[...]).astype(BF16)

    agenda.loop(S // RT, lambda i: back(i, p, cot_v), 5.0)
    arrive = [
        swap(cot_v.at[pl.ds(0, S)], out2in, out2in),
        swap(cot_v.at[pl.ds(S, S)], dy2in, dy2in),
    ]
    agenda.loop(S // RT, lambda i: back(i, c, mlp_v), 5.0)
    stores += [put(mlp_v.at[pl.ds(0, S)], out2), put(mlp_v.at[pl.ds(S, S)], dy2)]
    agenda.until(1e9)
    for w in arrive:
        w()
    for cp in stores:
        cp.wait()
    copies.leave()
    for cp in small:
        cp.wait_send()
    for s in streams:
        for r in s:
            r[2]()


def feed(nf, nz, unit, tok, cot, vec, wq, wd, wu, ww):
    bits = (2,) * ((nf // 2).bit_length() - 1)
    nb = len(bits)
    S, D = tok.shape
    T, W = 2 * S, D // 2
    sd = jax.ShapeDtypeStruct
    hb, vm = pl.BlockSpec(memory_space=pl.ANY), pl.BlockSpec(memory_space=pltpu.VMEM)
    full_u = bits + (2 * wu.shape[0], nz * wu.shape[1] // 2)
    full_w = bits + (ww.shape[0], nz * ww.shape[1])
    full_q = bits + (2 * wq.shape[0], nz * wq.shape[1] // 2)
    full_d = bits + (wd.shape[0], nz * wd.shape[1])
    FH = full_u[-1]
    outs = [sd((T, D), BF16), sd((T, D), BF16), sd(full_q, BF16), sd(full_d, BF16), sd(full_u, BF16), sd(full_w, BF16)]
    outs += [sd((S, D), BF16)] * 4 + [sd((8, D), F32), sd((1, W), F32)]
    n = 6 + nb + wu.shape[1] // (2 * unit) + wq.shape[1] // 256 + 15 * copies_of(nz, nb)
    v = lambda *shape: pltpu.VMEM(shape, BF16)
    return pl.pallas_call(
        partial(feed_kernel, nf, nz, unit), out_shape=outs,
        in_specs=[hb] * 7, out_specs=[hb] * 10 + [vm] * 2,
        scratch_shapes=[
            v(T, D), v(T, D), v(T, D), v(*full_u), v(*full_w), v(T, FH), v(T, FH), v(*full_u), v(*full_w),
            pltpu.VMEM(bits + (2,) + vec.shape, F32),
            pltpu.SemaphoreType.DMA((n,)), pltpu.SemaphoreType.DMA((n,)), pltpu.SemaphoreType.DMA((24,)),
        ],
        compiler_params=pltpu.CompilerParams(collective_id=0, has_side_effects=True, vmem_limit_bytes=63 << 20),
        name="feed",
    )(tok, cot, vec, wq, wd, wu, ww)


def attend_kernel(nf, nz, head, rot, nh, *refs):
    (attn_in, cot2, bq2, bd2, gu, gw, out2, out2in, dy2, dy2in, tok, docc1, docr1,
     vec, fw, cosp, sina, sinb, mixh, mixl, mixt,
     output, input_grad, oq, od, ou, ow, ovec) = refs[:28]
    (attn_v, cot_v, bq, bd, qkv, dd, do, o, st, cur, docc, docr, aq, ad, au, aw) = refs[28:44]
    hold_u, hold_w, hold_d = refs[44:44 + nh[0]], refs[44 + nh[0]:44 + nh[0] + nh[1]], refs[44 + nh[0] + nh[1]:44 + sum(nh)]
    hq, hu, gv, vh, gf, outs, igs, send, recv, local, free_u, free_d = refs[44 + sum(nh):]
    at = Place(nf, nz)
    nb = at.nbits
    sems = Sems(send, recv)
    copies = Copies(at, sems, local)
    put, swap = copies.put, copies.swap
    c, p = at.core, 1 - at.core
    S, D = tok.shape
    T = 2 * S
    width = D // 2
    npair = width // 128
    seq = cosp.shape[0]
    nch = T // CH
    half = rot // 2
    RT, FT = 512, outs.shape[1]
    every = (slice(None),) * nb
    own_rows, other_rows = tile(c, S), tile(p, S)
    at.greet(far=True)

    in_u = once([put(gu, au).wait])
    in_p = [put(attn_in, attn_v), put(bq2, bq)]
    in_w = once([put(gw, aw).wait])
    in_do = [put(cot2, cot_v), put(bd2, bd)]
    n1 = docr1.shape[0]
    in_doc = [
        put(docc1, docc.at[own_rows]).wait, swap(docc1, docc.at[own_rows], docc.at[other_rows]),
        put(docr1, docr.at[tile(c, n1)]).wait, swap(docr1, docr.at[tile(c, n1)], docr.at[tile(p, n1)]),
    ]

    def scatters(acc, holds, like=None):
        streams, it = [], iter(holds)
        for start, size, order in streams_of(acc.shape[-2], nb):
            shapes = hold_shapes(nz, nb, size, acc.shape[-1], order)
            mine = [next(it) for _ in shapes]
            if like is not None:
                mine = [hold.at[(slice(None),) * (len(s) - 1) + (pl.ds(0, s[-1]),)] for hold, s in zip(mine, shapes)]
            streams.append(scatter_stream(at, sems, acc, mine, start, size, order))
        return streams

    def release(free):
        for b in range(nb):
            pl.semaphore_signal(free, inc=1, device_id=at.across(b), device_id_type=MESH)

        @pl.when(at.z > 0)
        def _():
            pl.semaphore_signal(free, inc=1, device_id=at.along(-1), device_id_type=MESH)

        @pl.when(at.z < nz - 1)
        def _():
            pl.semaphore_signal(free, inc=1, device_id=at.along(1), device_id_type=MESH)

    def wait_free(free):
        inner = (at.z > 0).astype(jnp.int32) + (at.z < nz - 1).astype(jnp.int32)
        pl.semaphore_wait(free, nb + inner)

    agenda = Agenda(3.0)
    su, sw = scatters(au, hold_u), scatters(aw, hold_w)
    ends = agenda.add(su + sw, [(1.0, in_u)] * len(su) + [(1.5, in_w)] * len(sw), [0] * len(su) + [1] * len(sw))
    end_u, end_w = max(ends[:len(su)]), max(ends[len(su):])
    agenda.at(end_u + 0.1, lambda: release(free_u))
    for cp in in_p:
        cp.wait()

    wq = bq.reshape(D, 3 * width)
    wd = bd.reshape(width, D)

    def project(i):
        r = tile(i, RT)
        ps = tile(lax.rem(i, seq // RT), RT)
        a = attn_v[r, :]
        for part in range(2):
            x = dot(a, wq[:, part * width:(part + 1) * width])
            for m in range(npair):
                s = slice(m * 128, (m + 1) * 128)
                y = x[:, s]
                y = y * cosp[ps, :] + pltpu.roll(y, half, 1) * sina[ps, :] + pltpu.roll(y, 128 - half, 1) * sinb[ps, :]
                hi = y.astype(BF16)
                lo = (y - hi.astype(F32)).astype(BF16)
                e = dot(hi, mixh[...]) + dot(lo, mixh[...]) + dot(hi, mixl[...])
                qkv[r, part * width + s.start:part * width + s.stop] = (fw[:, s] * jnp.exp(e)).astype(BF16)
        qkv[r, 2 * width:] = dot(a, wq[:, 2 * width:]).astype(BF16)

    agenda.until(1.0)
    agenda.loop(T // RT, project, 3.2)
    for cp in in_do:
        cp.wait()

    def mixed_grad(i):
        r = tile(i, RT)
        do[r, :] = dot_nt(cot_v[r, :], wd[...]).astype(BF16)

    agenda.loop(T // RT, mixed_grad, 0.7)
    for w in in_doc:
        w()

    h0 = (lanes(128) % (2 * head)) < head
    h0w = jnp.concatenate([h0, h0], axis=1)
    rowh = lax.broadcasted_iota(jnp.int32, (128, 1), 0) < head
    block = rowh == h0w
    same = (rowh == h0).astype(BF16)
    one = jnp.ones((CH, 128), BF16)
    zero = jnp.zeros((), BF16)
    place = lanes(128) % head
    causal = lax.broadcasted_iota(jnp.int32, (CH, 1), 0) >= lanes(CH)

    def split(x):
        hi = x.astype(BF16)
        return hi, (x - hi.astype(F32)).astype(BF16)

    def masks(i):
        d = docc[tile(i, CH), :]
        inside = jnp.where(causal & (jnp.concatenate([d, d], axis=1) == docr[i]), 1.0, 0.0)
        start = lax.rem(i, seq // CH) == 0
        before = jnp.where(start, -1, docc[pl.ds(jnp.maximum(i * CH - 1, 0), 1), :])
        last = docc[pl.ds(i * CH + CH - 1, 1), :]
        ones = lambda x: jnp.where(x, 1.0, 0.0)
        return inside, ones(d == before), ones(d == last), ones(before == last)

    twice = lambda x: jnp.concatenate([x, x], axis=1)

    def scores(q, k, m):
        s0 = dot_nt(jnp.where(h0, q, zero), k)
        s1 = dot_nt(jnp.where(h0, zero, q), k)
        return (s0 * m).astype(BF16), (s1 * m).astype(BF16)

    cur[...] = jnp.zeros_like(cur)

    def forward(i):
        r = tile(i, CH)
        m, cr, tr, kp = masks(i)
        cw, kpw = twice(cr), twice(kp)
        for j in range(npair):
            s = slice(j * 128, (j + 1) * 128)
            q, k, v = (qkv[r, x * width + s.start:x * width + s.stop] for x in range(3))
            va = jnp.concatenate([v, one], axis=1)
            p0, p1 = scores(q, k, m)
            state = cur[j]
            hi, lo = split(state)
            st[i, j, 0] = hi
            st[i, j, 1] = lo
            res = dot(p0, jnp.where(h0w, va, zero)) + dot(p1, jnp.where(h0w, zero, va)) + cw * (dot(q, hi) + dot(q, lo))
            rd = 1.0 / res[:, 128:]
            att = res[:, :128] * rd
            o[r, s] = att.astype(BF16)
            dnb = (do[r, s].astype(F32) * rd).astype(BF16)
            do[r, s] = dnb
            hi, lo = split(dnb.astype(F32) * att)
            hi, lo = split(-(dot(hi, same) + dot(lo, same)))
            dd[r, s] = jnp.where(place == 0, hi, jnp.where(place == 1, lo, zero))
            kt = (k.astype(F32) * tr).astype(BF16)
            cur[j] = kpw * state + jnp.where(block, dot_tn(kt, va), 0.0)
    agenda.loop(nch, forward, 1.95)

    def grad_dense(i):
        ad[...] = dot_tn(o[...], cot_v[...]).astype(BF16).reshape(ad.shape)

    agenda.loop(1, grad_dense, 3.0)

    cur[...] = jnp.zeros_like(cur)
    gf[...] = jnp.zeros_like(gf)

    def backward(ii):
        i = nch - 1 - ii
        r = tile(i, CH)
        ps = tile(lax.rem(i, seq // CH), CH)
        m, cr, tr, kp = masks(i)
        kpw = twice(kp)
        cos, sa, sb = cosp[ps, :], sina[ps, :], sinb[ps, :]

        def unfeature(d, f, s, base):
            de = d * f.astype(F32)
            gf[:, s] += jnp.sum(de.reshape(CH // 8, 8, 128), axis=0)
            g = dot(de.astype(BF16), mixt[...])
            g = g * cos + pltpu.roll(g * sa, 128 - half, 1) + pltpu.roll(g * sb, half, 1)
            qkv[r, base + s.start:base + s.stop] = g.astype(BF16)

        for j in range(npair):
            s = slice(j * 128, (j + 1) * 128)
            q, k, v = (qkv[r, x * width + s.start:x * width + s.stop] for x in range(3))
            va = jnp.concatenate([v, one], axis=1)
            p0, p1 = scores(q, k, m)
            dnb = do[r, s]
            dy = jnp.concatenate([dnb, dd[r, s]], axis=1)
            ds0 = (dot_nt(dy, jnp.where(h0w, va, zero)) * m).astype(BF16)
            ds1 = (dot_nt(dy, jnp.where(h0w, zero, va)) * m).astype(BF16)
            dst = cur[j]
            dhi, dlo = split(dst)
            dq = dot(ds0, jnp.where(h0, k, zero)) + dot(ds1, jnp.where(h0, zero, k)) + cr * (dot_nt(dy, st[i, j, 0]) + dot_nt(dy, st[i, j, 1]))
            dk = dot_tn(ds0, jnp.where(h0, q, zero)) + dot_tn(ds1, jnp.where(h0, zero, q)) + tr * (dot_nt(va, dhi) + dot_nt(va, dlo))
            dv = dot_tn(p0, jnp.where(h0, dnb, zero)) + dot_tn(p1, jnp.where(h0, zero, dnb)) + tr * dot(k, dhi[:, :128])
            qc = (q.astype(F32) * cr).astype(BF16)
            cur[j] = kpw * dst + jnp.where(block, dot_tn(qc, dy), 0.0)
            unfeature(dq, q, s, 0)
            unfeature(dk, k, s, width)
            qkv[r, 2 * width + s.start:2 * width + s.stop] = dv.astype(BF16)
    agenda.loop(nch, backward, 3.15)


    pl.semaphore_signal(free_d, inc=1, device_id=at.partner(), device_id_type=MESH)
    st_flat = st.reshape(st.shape[0] * st.shape[1] * 2 * 128, 256)

    def cut(ref, width, at_row=0):
        return [ref.at[pl.ds(at_row + k * S, S)] for k in range(D // width)]

    def fetch(src, parts):
        w = D // len(parts)
        return [put(src.at[:, pl.ds(k * w, w)], part) for k, part in enumerate(parts)]

    fetched = fetch(out2in, cut(st_flat, 256)) + fetch(dy2, cut(st_flat, 256, 4 * S))
    fetched.append(put(dy2in, cot_v.at[other_rows]))

    def grad_qkv(i):
        val = dot_tn(attn_v[...], qkv[:, tile(i, width)]).astype(BF16)
        aq[every + (slice(None), tile(i, width))] = val.reshape(aq.shape[:-1] + (width,))

    agenda.loop(3, grad_qkv, 2.4)
    sq, sdn = scatters(aq, hold_u, au), scatters(ad, hold_d)
    wait_u = once([lambda: wait_free(free_u)])
    ready = [(max(agenda.now, end_u + 2.0), wait_u)] * len(sq) + [(agenda.now, None)] * len(sdn)
    ends = agenda.add(sq + sdn, ready, [0] * len(sq) + [1] * len(sdn))
    end_q, end_d = max(ends[:len(sq)]), max(ends[len(sq):])

    def back_qkv(i, rows):
        r = tile(i + rows * (S // RT), RT)
        attn_v[r, :] = dot_nt(qkv[r, :], wq[...]).astype(BF16)

    def back_dense(i, rows):
        r = tile(i + rows * (S // RT), RT)
        qkv[r, :D] = dot(o[r, :], wd[...]).astype(BF16)

    def send_back(src, dst):
        return [
            swap(src.at[other_rows, pl.ds(k * width, width)], part, part) for k, part in enumerate(cut(dst, width))
        ]

    agenda.loop(S // RT, lambda i: back_qkv(i, p), 1.9)
    pl.semaphore_wait(free_d, 1)
    arrive = send_back(attn_v, do)
    agenda.loop(S // RT, lambda i: back_dense(i, p), 0.7)
    arrive += send_back(qkv, dd)
    agenda.loop(S // RT, lambda i: back_qkv(i, c), 1.9)
    fetched.append(put(out2, wq.at[pl.ds(0, S), pl.ds(0, D)]))
    agenda.loop(S // RT, lambda i: back_dense(i, c), 0.7)
    fetched += fetch(tok, cut(o, width))
    agenda.until(agenda.now)

    gv[0] = jnp.zeros((8, D), F32)
    for m in range(npair):
        s = slice(m * 128, (m + 1) * 128)
        gv[0, 4:5, pl.ds(pl.multiple_of((2 * m + c) * 128, 128), 128)] = jnp.sum(gf[:, s], axis=0, keepdims=True) / fw[:, s]
    for cp in fetched:
        cp.wait()
    for w in arrive:
        w()
    first = copies.count

    def stores(i):
        k, r = lax.rem(i, 2), tile(i, FT)
        return [
            pltpu.make_async_copy(outs.at[k], output.at[r], local.at[first + 2 * k]),
            pltpu.make_async_copy(igs.at[k], input_grad.at[r], local.at[first + 2 * k + 1]),
        ]

    def finish(i):
        k = lax.rem(i, 2)

        @pl.when(i >= 2)
        def _():
            for cp in stores(i - 2):
                cp.wait()

        def rows(t, sums):
            part = tile(t, 32)
            at_row = i * FT + t * 32
            own = pl.ds(pl.multiple_of(at_row + c * S, 32), 32)

            def joined(ref, n, base=0):
                return jnp.concatenate(
                    [ref[pl.ds(pl.multiple_of(at_row + base + q * S, 32), 32), :] for q in range(n)], axis=1
                ).astype(F32)

            here = pl.ds(pl.multiple_of(at_row, 32), 32)
            x = joined(o, D // width)
            n, rstd = normed(x)
            out1 = qkv[own, :D].astype(F32) + joined(dd, D // width)
            outs[k, part, :] = (x + out1 + (wq[here, :D].astype(F32) + joined(st_flat, D // 256))).astype(BF16)
            d1 = attn_v[own, :].astype(F32) + joined(do, D // width)
            d2 = joined(st_flat, D // 256, 4 * S) + cot_v[pl.ds(pl.multiple_of(at_row + p * S, 32), 32), :].astype(F32)
            dn = d1 * vec[0:1, :] + d2 * vec[2:3, :]
            dx = rstd * (dn - jnp.mean(dn, axis=-1, keepdims=True) - n * jnp.mean(dn * n, axis=-1, keepdims=True))
            igs[k, part, :] = cot_v[own, :].astype(F32) + dx
            fold = lambda y: jnp.sum(y.reshape(4, 8, D), axis=0)
            return tuple(a + fold(y) for a, y in zip(sums, (d1 * n, d1, d2 * n, d2)))

        sums = lax.fori_loop(0, FT // 32, rows, (jnp.zeros((8, D), F32),) * 4)
        for q, y in enumerate(sums):
            gv[0, q:q + 1, :] += jnp.sum(y, axis=0, keepdims=True)
        for cp in stores(i):
            cp.start()

    agenda.loop(S // FT, finish, 1.5)
    for i in range(S // FT - 2, S // FT):
        for cp in stores(i):
            cp.wait()

    peers = [at.partner()] + [at.across(b) for b in range(nb)]
    step = 1
    while step < nz:
        peers.append(at.fold(step))
        step *= 2
    rounds = []
    for k, peer in enumerate(peers):
        cp = sems.copy(gv.at[k], vh.at[k], sems.take(), peer)

        def arrive(cp=cp, k=k):
            cp.wait_recv()
            gv[k + 1] = gv[k] + vh[k]

        rounds.append((cp.start, arrive, cp.wait_send, "small", 4.0 * 8 * D))
    agenda.add([rounds], [(agenda.now, None)])
    me = at.slot(())
    sent = []
    for acc, hold, out, end in ((aq, hq, oq, end_q), (au, hu, ou, end_u)):
        half = hold.shape[0]
        cols = at.columns(acc, at.z)
        cp = sems.copy(acc.at[me + (tile(p, half), cols)], hold, sems.take(), at.partner())

        def act(cp=cp, acc=acc, out=out, half=half, cols=cols):
            cp.start()
            out[c] = acc[me + (tile(c, half), cols)]

        def arrive(cp=cp, hold=hold, out=out):
            cp.wait_recv()
            out[p] = hold[...]

        begin = max(end + 0.1, agenda.now)
        agenda.at(begin, act)
        agenda.at(begin + 4.0, arrive)
        sent.append(cp)

    def keep(acc, out):
        out[...] = acc[me + (slice(None), at.columns(acc, at.z))]

    agenda.at(max(end_d + 0.1, agenda.now), lambda: keep(ad, od))
    agenda.at(end_w + 0.1, lambda: keep(aw, ow))
    agenda.until(1e9)
    ovec[...] = gv[len(peers)]
    copies.leave()
    for cp in sent:
        cp.wait_send()
    for s in su + sw + sdn + sq + [rounds]:
        for r in s:
            r[2]()


def attend(nf, nz, head, rot, attn_in, cot2, bq, bd, gu, gw, out2, out2in, dy2, dy2in, tok, docc, docr, vec, fw, *tabs):
    sd = jax.ShapeDtypeStruct
    nb = (nf // 2).bit_length() - 1
    S, D = tok.shape
    T, W = 2 * S, D // 2
    own = lambda a: (a.shape[-2], a.shape[-1] // nz)

    def holds(a):
        shapes = []
        for _, size, order in streams_of(a.shape[-2], nb):
            shapes += hold_shapes(nz, nb, size, a.shape[-1], order)
        return shapes

    room = [holds(gu), holds(gw), holds(bd)]
    halves = [(own(a)[0] // 2, own(a)[1]) for a in (bq, gu)]
    nsteps = 1 + nb + nz.bit_length() - 1
    ncopies = 12 * copies_of(nz, nb) + 6 + nsteps + 2
    vm, hb = pl.BlockSpec(memory_space=pltpu.VMEM), pl.BlockSpec(memory_space=pl.ANY)
    v = lambda *shape: pltpu.VMEM(shape, BF16)
    f = lambda *shape: pltpu.VMEM(shape, F32)
    i32 = lambda *shape: pltpu.VMEM(shape, jnp.int32)
    outs = [sd((S, D), BF16), sd((S, D), F32)]
    outs += [sd((2,) + halves[0], BF16), sd(own(bd), BF16), sd((2,) + halves[1], BF16), sd(own(gw), BF16), sd((8, D), F32)]
    return pl.pallas_call(
        partial(attend_kernel, nf, nz, head, rot, tuple(len(r) for r in room)), out_shape=outs,
        in_specs=[hb] * 13 + [vm] * 8, out_specs=[hb] * 2 + [vm] * 5,
        scratch_shapes=[
            v(T, D), v(T, D), v(*bq.shape), v(*bd.shape), v(T, 3 * W), v(T, W), v(T, W), v(T, W),
            v(T // CH, W // 128, 2, 128, 256), f(W // 128, 128, 256), i32(T, 128), i32(2 * docr.shape[0], 1, CH),
            v(*bq.shape), v(*bd.shape), v(*gu.shape), v(*gw.shape),
        ]
        + [v(*s) for r in room for s in r] + [v(*s) for s in halves]
        + [f(nsteps + 1, 8, D), f(nsteps, 8, D), f(8, W), v(2, 128, D), f(2, 128, D)]
        + [pltpu.SemaphoreType.DMA((ncopies,)), pltpu.SemaphoreType.DMA((ncopies,)), pltpu.SemaphoreType.DMA((28,))]
        + [pltpu.SemaphoreType.REGULAR] * 2,
        compiler_params=pltpu.CompilerParams(collective_id=1, has_side_effects=True, vmem_limit_bytes=63 << 20),
        name="attend",
    )(attn_in, cot2, bq, bd, gu, gw, out2, out2in, dy2, dy2in, tok, docc, docr, vec, fw, *tabs)


def body(nf, nz, tokens, doc_starts, w_qkv, w_dense, w_up, w_down, norm1_gain, norm1_bias, norm2_gain, norm2_bias, feature_weight, cotangent):
    rows, D = tokens.shape
    unit = w_down.shape[0]

    block = unit
    if unit % 128:
        block = w_up.shape[1] // 2
        w_up = w_up.reshape(-1, block // unit, 2, unit).swapaxes(1, 2).reshape(w_up.shape)

    def unturn(g, block):
        _, r, n = g.shape
        return g.reshape(2, r, n // block, block).transpose(1, 2, 0, 3).reshape(r, 2 * n)

    per = 128 // w_dense.shape[0]
    source = [(2 * (k // per) + c) * per + k % per for k in range(nf // 2) for c in range(2)]
    if per > 1:
        w_dense = lax.ppermute(w_dense, "fsdp", [(s, d) for d, s in enumerate(source)])

    doc = jnp.cumsum(doc_starts.reshape(-1, SEQ_LEN), axis=1).astype(jnp.int32).reshape(rows)
    vec = jnp.stack([norm1_gain, norm1_bias, norm2_gain, norm2_bias, feature_weight] + [jnp.zeros_like(norm1_gain)] * 3)
    cosp, sina, sinb, mix = tables(SEQ_LEN, ROT, HEAD, FEATS)
    mix = jnp.asarray(mix)
    mixh = mix.astype(BF16)
    mixl = (mix - mixh.astype(F32)).astype(BF16)
    attn_in, cot2, bq, bd, gu, gw, out2, out2in, dy2, dy2in, vec8, fw = feed(
        nf, nz, block, tokens, cotangent, vec, w_qkv, w_dense, w_up, w_down
    )
    output, input_grad, oq, od, ou, ow, gv = attend(
        nf, nz, HEAD, ROT, attn_in, cot2, bq, bd, gu, gw, out2, out2in, dy2, dy2in, tokens,
        jnp.broadcast_to(doc[:, None], (rows, 128)), doc.reshape(-1, 1, CH), vec8, fw, cosp, sina, sinb, mixh, mixl, mixh.T,
    )
    if per > 1:
        od = lax.ppermute(od, "fsdp", [(d, s) for d, s in enumerate(source)])
    own = gv.reshape(8, nf, -1)
    own = lax.dynamic_index_in_dim(own, lax.axis_index("fsdp"), 1, keepdims=False)
    return (
        output, input_grad,
        unturn(oq, 128).astype(F32), od.astype(F32), unturn(ou, unit).astype(F32), ow.astype(F32),
        own[0], own[1], own[2], own[3], own[4],
    )


def solution(mesh):
    nf, nz = mesh.shape["fsdp"], mesh.shape["inner"]
    rows, mat, vec = P(("fsdp", "inner"), None), P("fsdp", "inner"), P("fsdp")
    in_specs = (rows, P(("fsdp", "inner"))) + (mat,) * 4 + (vec,) * 5 + (rows,)
    out_specs = (rows, rows) + (mat,) * 4 + (vec,) * 5
    return jax.shard_map(partial(body, nf, nz), mesh=mesh, in_specs=in_specs, out_specs=out_specs, check_vma=False)
```

```python
from functools import partial
import math
from statistics import NormalDist

import jax
import jax.numpy as jnp
import numpy as np
from jax import lax
from jax.experimental import pallas as pl
from jax.experimental.pallas import tpu as pltpu
from jax.sharding import PartitionSpec as P

MESH = pl.DeviceIdType.MESH
BF16 = jnp.bfloat16
F32 = jnp.float32


HEAD = 64
ROT = 16
FEATS = 64
SEQ_LEN = 1024

class Place:
    def __init__(self, nf, nz):
        self.nf, self.nz = nf, nz
        self.nbits = (nf // 2).bit_length() - 1
        self.f = lax.axis_index("fsdp")
        self.z = lax.axis_index("inner")
        self.core = lax.rem(self.f, 2)
        self.bits = [lax.rem(lax.div(self.f, 2 << b), 2) for b in range(self.nbits)]

    def partner(self):
        return (self.f + 1 - 2 * self.core, self.z)

    def across(self, b):
        return (self.f + (1 - 2 * self.bits[b]) * (2 << b), self.z)

    def along(self, step):
        return (self.f, self.z + step)

    def slot(self, done, flip=None):
        index = []
        for b in reversed(range(self.nbits)):
            if b in done:
                index.append(slice(None))
            elif b == flip:
                index.append(1 - self.bits[b])
            else:
                index.append(self.bits[b])
        return tuple(index)

    def columns(self, buf, zsel):
        if zsel is None:
            return slice(None)
        width = buf.shape[-1] // self.nz
        return pl.ds(pl.multiple_of(zsel * width, width), width)

    def greet(self, far=False):
        bar = pltpu.get_barrier_semaphore()
        z, nz = self.z, self.nz
        fixed = [self.partner()] + [self.across(b) for b in range(self.nbits)]
        for peer in fixed:
            pl.semaphore_signal(bar, inc=1, device_id=peer, device_id_type=MESH)

        @pl.when(z > 0)
        def _():
            pl.semaphore_signal(bar, inc=1, device_id=self.along(-1), device_id_type=MESH)

        @pl.when(z < nz - 1)
        def _():
            pl.semaphore_signal(bar, inc=1, device_id=self.along(1), device_id_type=MESH)

        count = len(fixed)
        if far and nz > 2:
            step = 2
            while step < nz:
                pl.semaphore_signal(
                    bar, inc=1, device_id=self.fold(step), device_id_type=MESH
                )
                count += 1
                step *= 2
        inner = (z > 0).astype(jnp.int32) + (z < nz - 1).astype(jnp.int32)
        pl.semaphore_wait(bar, count + inner)

    def fold(self, step):
        bit = lax.rem(lax.div(self.z, step), 2)
        return (self.f, self.z + (1 - 2 * bit) * step)


class Sems:
    def __init__(self, send, recv):
        self.send, self.recv, self.count = send, recv, 0

    def take(self):
        self.count += 1
        return self.count - 1

    def copy(self, src, dst, i, peer):
        return pltpu.make_async_remote_copy(
            src_ref=src,
            dst_ref=dst,
            send_sem=self.send.at[i],
            recv_sem=self.recv.at[i],
            device_id=peer,
            device_id_type=MESH,
        )


def streams_of(rows, nbits, cuts=1):
    up, down = list(range(nbits)), list(reversed(range(nbits)))
    parts = [(3, ["z"] + up), (3, ["z"] + down)] * cuts + [(2, up + ["z"]), (2, down + ["z"])][:cuts]
    whole, units, at, streams = sum(n for n, _ in parts), rows // 16, 0, []
    for k, (_, order) in enumerate(parts):
        end = round(units * sum(n for n, _ in parts[:k + 1]) / whole)
        if end > at:
            streams.append((at * 16, (end - at) * 16, order))
        at = end
    return streams


def copies_of(nz, nbits):
    return nbits + 2 * (nz - 1)


def gather_stream(at, sems, buf, start, size, order):
    rows = pl.ds(start, size)
    rounds = []
    done, zdone = (), False

    def along(k, done):
        ids = (sems.take(), sems.take())

        def right(zsel):
            ref = buf.at[at.slot(done) + (rows, at.columns(buf, zsel))]
            return sems.copy(ref, ref, ids[0], at.along(1))

        def left(zsel):
            ref = buf.at[at.slot(done) + (rows, at.columns(buf, zsel))]
            return sems.copy(ref, ref, ids[1], at.along(-1))

        z, nz = at.z, at.nz
        goes_right = (z < nz - 1) & (z - k + 1 >= 0)
        goes_left = (z > 0) & (z + k - 1 <= nz - 1)

        def send():
            pl.when(goes_right)(lambda: right(z - k + 1).start())
            pl.when(goes_left)(lambda: left(z + k - 1).start())

        def arrive():
            pl.when(z - k >= 0)(lambda: right(z - k).wait_recv())
            pl.when(z + k <= nz - 1)(lambda: left(z + k).wait_recv())

        def leave():
            pl.when(goes_right)(lambda: right(z - k + 1).wait_send())
            pl.when(goes_left)(lambda: left(z + k - 1).wait_send())

        return send, arrive, leave

    def across(b, done, zsel):
        i = sems.take()
        mine = buf.at[at.slot(done) + (rows, at.columns(buf, zsel))]
        theirs = buf.at[at.slot(done, flip=b) + (rows, at.columns(buf, zsel))]
        out = sems.copy(mine, mine, i, at.across(b))
        back = sems.copy(theirs, theirs, i, at.across(b))
        return out.start, back.wait_recv, out.wait_send

    piece = size * (buf.shape[-1] // at.nz) * 2
    for dim in order:
        if dim == "z":
            rounds += [along(k, done) + ("z", piece << len(done)) for k in range(1, at.nz)]
            zdone = True
        else:
            nbytes = (piece << len(done)) * (at.nz if zdone else 1)
            rounds.append(across(dim, done, None if zdone else at.z) + (dim, nbytes))
            done = done + (dim,)
    return rounds


def scatter_stream(at, sems, acc, holds, start, size, order):
    rows = pl.ds(start, size)
    rounds = []
    left_bits, zleft = set(range(at.nbits)), True

    def along(k, remaining, hold):
        ids = (sems.take(), sems.take())
        z, nz = at.z, at.nz

        def part(zsel):
            return acc.at[at.slot(remaining) + (rows, at.columns(acc, zsel))]

        def right(zsel):
            return sems.copy(part(zsel), hold.at[2 * k - 2], ids[0], at.along(1))

        def left(zsel):
            return sems.copy(part(zsel), hold.at[2 * k - 1], ids[1], at.along(-1))

        goes_right = z + k <= nz - 1
        goes_left = z - k >= 0

        def send():
            pl.when(goes_right)(lambda: right(z + k).start())
            pl.when(goes_left)(lambda: left(z - k).start())

        def arrive():
            @pl.when((z >= 1) & (z - 1 + k <= nz - 1))
            def _():
                right(z - 1 + k).wait_recv()
                ref = part(z - 1 + k)
                ref[...] += hold[2 * k - 2]

            @pl.when((z <= nz - 2) & (z + 1 - k >= 0))
            def _():
                left(z + 1 - k).wait_recv()
                ref = part(z + 1 - k)
                ref[...] += hold[2 * k - 1]

        def leave():
            pl.when(goes_right)(lambda: right(z + k).wait_send())
            pl.when(goes_left)(lambda: left(z - k).wait_send())

        return send, arrive, leave

    def across(b, remaining, zsel, hold):
        i = sems.take()
        out = sems.copy(
            acc.at[at.slot(remaining, flip=b) + (rows, at.columns(acc, zsel))], hold, i, at.across(b)
        )

        def arrive():
            out.wait_recv()
            ref = acc.at[at.slot(remaining) + (rows, at.columns(acc, zsel))]
            ref[...] += hold[...]

        return out.start, arrive, out.wait_send

    piece = size * (acc.shape[-1] // at.nz) * 2
    holds = iter(holds)
    for dim in reversed(order):
        if dim == "z":
            hold = next(holds)
            rounds += [
                along(k, tuple(left_bits), hold) + ("z", piece << len(left_bits))
                for k in range(at.nz - 1, 0, -1)
            ]
            zleft = False
        else:
            left_bits = left_bits - {dim}
            nbytes = (piece << len(left_bits)) * (at.nz if zleft else 1)
            rounds.append(across(dim, tuple(left_bits), None if zleft else at.z, next(holds)) + (dim, nbytes))
    return rounds


def hold_shapes(nz, nbits, size, width, order):
    shapes, bits, zleft = [], nbits, True
    for dim in reversed(order):
        if dim == "z":
            shapes.append((2 * (nz - 1),) + (2,) * bits + (size, width // nz))
            zleft = False
        else:
            bits -= 1
            shapes.append((2,) * bits + (size, width if zleft else width // nz))
    return shapes


LINK_RATE = 48000.0


class Agenda:
    def __init__(self, hop):
        self.hop, self.events, self.now, self.free = hop, [], 0.0, {}

    def add(self, streams, ready, rank=None):
        rank = rank or [0] * len(streams)
        took = [[rounds[r][4] / LINK_RATE for r in range(len(rounds))] for rounds in streams]
        left = [[sum(t[r:]) + self.hop * (len(t) - r) for r in range(len(t) + 1)] for t in took]
        state = [[0, t] for t, _ in ready]
        while True:
            best = None
            for i, rounds in enumerate(streams):
                r, t = state[i]
                if r < len(rounds):
                    begin = max(t, self.free.get(rounds[r][3], 0.0))
                    key = (begin, rank[i], -left[i][r], i)
                    best = key if best is None or key < best else best
            if best is None:
                break
            begin, i = best[0], best[3]
            r = state[i][0]
            rounds = streams[i]
            wait = ready[i][1] if r == 0 else rounds[r - 1][1]

            def act(wait=wait, send=rounds[r][0]):
                if wait is not None:
                    wait()
                send()

            self.events.append((begin, act))
            self.free[rounds[r][3]] = begin + took[i][r]
            state[i] = [r + 1, begin + took[i][r] + self.hop]
            if r + 1 == len(rounds):
                self.events.append((state[i][1], rounds[r][1]))
        self.events.sort(key=lambda e: e[0])
        return [t for _, t in state]

    def at(self, time, act):
        self.events.append((time, act))
        self.events.sort(key=lambda e: e[0])

    def until(self, time):
        while self.events and self.events[0][0] <= time:
            self.events.pop(0)[1]()
        self.now = max(self.now, time)

    def loop(self, n, body, took):
        due = [[] for _ in range(n)]
        while self.events:
            step = max(0, math.ceil((self.events[0][0] - self.now) / took - 0.5))
            if step >= n:
                break
            due[step].append(self.events.pop(0)[1])
        self.now += n * took

        def step(i, carry):
            for u, acts in enumerate(due):
                if acts:

                    @pl.when(i == u)
                    def _(acts=acts):
                        for act in acts:
                            act()

            body(i)
            return carry

        lax.fori_loop(0, n, step, 0)


def once(acts):
    done = []

    def run():
        if not done:
            for act in acts:
                act()
            done.append(1)

    return run


class Copies:
    def __init__(self, at, sems, local):
        self.at, self.sems, self.local, self.count, self.sent = at, sems, local, 0, []

    def put(self, src, dst):
        cp = pltpu.make_async_copy(src, dst, self.local.at[self.count])
        self.count += 1
        cp.start()
        return cp

    def swap(self, src, dst, arrives):
        i = self.sems.take()
        cp = self.sems.copy(src, dst, i, self.at.partner())
        cp.start()
        self.sent.append(cp)
        return self.sems.copy(src, arrives, i, self.at.partner()).wait_recv

    def leave(self):
        for cp in self.sent:
            cp.wait_send()


CH = 256

def dot(a, b):
    return jnp.dot(a, b, preferred_element_type=F32)

def dot_nt(a, b):
    return lax.dot_general(a, b, (((1,), (1,)), ((), ())), preferred_element_type=F32)

def dot_tn(a, b):
    return lax.dot_general(a, b, (((0,), (0,)), ((), ())), preferred_element_type=F32)

def tile(i, n):
    return pl.ds(pl.multiple_of(i * n, n), n)

def lanes(width):
    return lax.broadcasted_iota(jnp.int32, (1, width), 1)

def normed(x):
    center = x - jnp.mean(x, axis=-1, keepdims=True)
    spread = jnp.mean(center * center, axis=-1, keepdims=True)
    rstd = lax.rsqrt(spread + 1e-05)
    return center * rstd, rstd

def gelu_pair(x):
    e = jnp.exp2((-0.5 * math.log2(math.e)) * (x * x))
    d = 1.0 + (0.3275911 / math.sqrt(2.0)) * jnp.abs(x)
    t = 1.0 / d
    poly = t * (0.127414796 + t * (-0.142248368 + t * (0.7107068705 + t * (-0.7265760135 + t * 0.5307027145))))
    tail = poly * e
    phi = jnp.where(x >= 0, 1.0 - tail, tail)
    return x * phi, phi + x * e * (1.0 / math.sqrt(2.0 * math.pi))


def tables(seq, rot, head, feats):
    half = rot // 2
    angles = np.arange(seq)[:, None] / 10000.0 ** (np.arange(0, rot, 2) / rot)[None, :]
    cosp, sina, sinb = np.ones((seq, 128)), np.zeros((seq, 128)), np.zeros((seq, 128))
    for base in range(0, 128, head):
        cosp[:, base:base + half] = np.cos(angles)
        cosp[:, base + half:base + rot] = np.cos(angles)
        sina[:, base + half:base + rot] = np.sin(angles)
        sinb[:, base:base + half] = -np.sin(angles)
    k, i = np.arange(head)[:, None], np.arange(head)[None, :]
    cosine = np.where(k == 0, math.sqrt(1.0 / head), math.sqrt(2.0 / head)) * np.cos(math.pi * (i + 0.5) * k / head)
    j = np.arange(feats)[None, :]
    level = (((j * (2 * k + 1) + k) % feats) + 0.5) / feats
    normals = np.vectorize(NormalDist().inv_cdf)(level)
    mixing = cosine.T @ normals / math.sqrt(head)
    mix = np.zeros((128, 128), np.float32)
    for base in range(0, 128, head):
        mix[base:base + head, base:base + feats] = mixing
    return cosp.astype(np.float32), sina.astype(np.float32), sinb.astype(np.float32), mix


def feed_kernel(nf, nz, unit, tok, cot, vec1, wq1, wd1, wu1, ww1,
                attn_in, cot2, bq, bd, gu2, gw2, out2, out2in, dy2, dy2in, vec, fw,
                tok_v, mlp_v, cot_v, wu, ww, h, pre, gu, gw, vecs, send, recv, local):
    at = Place(nf, nz)
    nb = at.nbits
    sems = Sems(send, recv)
    copies = Copies(at, sems, local)
    put, swap = copies.put, copies.swap
    c, p = at.core, 1 - at.core
    S, D = tok.shape
    T = 2 * S
    FH = h.shape[1]
    RT, FB = 512, 512
    every = (slice(None),) * nb
    me = at.slot(())
    own_rows, other_rows = tile(c, S), tile(p, S)
    at.greet()

    def halves(w, buf, block):
        r, n = w.shape
        here, there = [], []
        for t in range(n // (2 * block)):
            def part(core, t=t):
                return w.at[:, pl.ds(pl.multiple_of((2 * t + core) * block, block), block)]

            def place(core, t=t):
                cols = pl.ds(pl.multiple_of(at.z * (n // 2) + t * block, 128), block)
                return buf.at[me + (tile(core, r), cols)]

            there.append(swap(part(p), place(c), place(p)))
            here.append(put(part(c), place(c)).wait)
        return there + here

    z = lambda b: at.columns(b, at.z)
    in_u = halves(wu1, wu, unit)
    in_vec = [swap(vec1, vecs.at[me + (c,)], vecs.at[me + (p,)]), put(vec1, vecs.at[me + (c,)]).wait]
    in_tok = [put(tok, tok_v.at[own_rows]).wait, swap(tok, tok_v.at[own_rows], tok_v.at[other_rows])]
    in_w = [put(ww1, ww.at[me + (slice(None), z(ww))]).wait]
    in_q = halves(wq1, bq, 128)
    in_d = [put(wd1, bd.at[me + (slice(None), z(bd))]).wait]
    in_cot = [put(cot, cot_v.at[own_rows]).wait, swap(cot, cot_v.at[own_rows], cot_v.at[other_rows])]

    agenda = Agenda(4.5)
    streams, ready, rank, ends = [], [], [], []
    for buf, waits, time, r, cuts in (
        (wu, in_u, 2.0, 0, 2), (ww, in_w, 2.0, 1, 1), (bq, in_q, 12.0, 2, 1), (bd, in_d, 4.0, 2, 1)
    ):
        wait = once(waits)
        for start, size, order in streams_of(buf.shape[-2], nb, cuts):
            streams.append(gather_stream(at, sems, buf, start, size, order))
            ready.append((time, wait))
            rank.append(r)
    ends = agenda.add(streams, ready, rank)
    end_u, end_w = (max(e for e, r in zip(ends, rank) if r == k) for k in (0, 1))
    agenda.until(4.0)
    for w in in_vec:
        w()
    done, small = (), []
    for b in range(nb):
        i = sems.take()
        m, t = vecs.at[at.slot(done)], vecs.at[at.slot(done, flip=b)]
        out = sems.copy(m, m, i, at.across(b))
        out.start()
        sems.copy(t, t, i, at.across(b)).wait_recv()
        small.append(out)
        done = done + (b,)
    w = vec1.shape[1]
    for f in range(nf):
        at_f = tuple((f >> (b + 1)) & 1 for b in reversed(range(nb))) + (f & 1,)
        vec[:, f * w:(f + 1) * w] = vecs[at_f]
    for m in range(fw.shape[1] // 128):
        fw[:, m * 128:(m + 1) * 128] = vec[4:5, pl.ds(pl.multiple_of((2 * m + c) * 128, 128), 128)]
    agenda.until(11.0)
    for w in in_tok:
        w()

    def ln(i):
        r = tile(i, CH)
        n, _ = normed(tok_v[r, :].astype(F32))
        tok_v[r, :] = (n * vec[0:1, :] + vec[1:2, :]).astype(BF16)
        mlp_v[r, :] = (n * vec[2:3, :] + vec[3:4, :]).astype(BF16)

    agenda.loop(T // CH, ln, 0.5)
    stores = [put(tok_v, attn_in)]
    agenda.until(end_u)

    top = (FH // FB).bit_length() - 1
    bits_of = lambda m: tuple((m >> b) & 1 for b in reversed(range(top))) + (slice(None),) * (nb - top)
    wu2, ww2 = wu.reshape(D, FH), ww.reshape(FH, D)

    for m in range(FH // FB):
        cols = slice(m * FB, (m + 1) * FB)

        def hidden(i, cols=cols):
            r = tile(i, RT)
            act, slope = gelu_pair(dot(mlp_v[r, :], wu2[:, cols]))
            h[r, cols] = act.astype(BF16)
            pre[r, cols] = slope.astype(BF16)

        agenda.loop(T // RT, hidden, 1.1)
    for w in in_cot:
        w()
    keep_cot = put(cot_v, cot2)
    gu_flat, gw_flat = gu.reshape(D, FH), gw.reshape(FH, D)

    def grad_down(m):
        gw_flat[tile(m, FB), :] = dot_tn(h[:, tile(m, FB)], cot_v[...]).astype(BF16)

    agenda.loop(FH // FB, grad_down, 2.4)
    stores.append(put(gw, gw2))
    agenda.until(end_w)

    for m in range(FH // FB):
        cols = slice(m * FB, (m + 1) * FB)

        def slopes(i, cols=cols, m=m):
            r = tile(i, RT)
            dh = dot_nt(cot_v[r, :], ww2[cols, :])
            pre[r, cols] = (dh * pre[r, cols].astype(F32)).astype(BF16)

        agenda.loop(T // RT, slopes, 0.75)


    def grad_up(m):
        gu_flat[:, tile(m, FB)] = dot_tn(mlp_v[...], pre[:, tile(m, FB)]).astype(BF16)

    agenda.loop(FH // FB, grad_up, 2.5)
    stores.append(put(gu, gu2))

    keep_cot.wait()

    def back(i, rows, into):
        r = tile(i + rows * (S // RT), RT)
        into[tile(i, RT), :] = dot(h[r, :], ww2[...]).astype(BF16)
        into[tile(i + S // RT, RT), :] = dot_nt(pre[r, :], wu2[...]).astype(BF16)

    agenda.loop(S // RT, lambda i: back(i, p, cot_v), 5.0)
    arrive = [
        swap(cot_v.at[pl.ds(0, S)], out2in, out2in),
        swap(cot_v.at[pl.ds(S, S)], dy2in, dy2in),
    ]
    agenda.loop(S // RT, lambda i: back(i, c, mlp_v), 5.0)
    stores += [put(mlp_v.at[pl.ds(0, S)], out2), put(mlp_v.at[pl.ds(S, S)], dy2)]
    agenda.until(1e9)
    for w in arrive:
        w()
    for cp in stores:
        cp.wait()
    copies.leave()
    for cp in small:
        cp.wait_send()
    for s in streams:
        for r in s:
            r[2]()


def feed(nf, nz, unit, tok, cot, vec, wq, wd, wu, ww):
    bits = (2,) * ((nf // 2).bit_length() - 1)
    nb = len(bits)
    S, D = tok.shape
    T, W = 2 * S, D // 2
    sd = jax.ShapeDtypeStruct
    hb, vm = pl.BlockSpec(memory_space=pl.ANY), pl.BlockSpec(memory_space=pltpu.VMEM)
    full_u = bits + (2 * wu.shape[0], nz * wu.shape[1] // 2)
    full_w = bits + (ww.shape[0], nz * ww.shape[1])
    full_q = bits + (2 * wq.shape[0], nz * wq.shape[1] // 2)
    full_d = bits + (wd.shape[0], nz * wd.shape[1])
    FH = full_u[-1]
    outs = [sd((T, D), BF16), sd((T, D), BF16), sd(full_q, BF16), sd(full_d, BF16), sd(full_u, BF16), sd(full_w, BF16)]
    outs += [sd((S, D), BF16)] * 4 + [sd((8, D), F32), sd((1, W), F32)]
    n = 6 + nb + wu.shape[1] // (2 * unit) + wq.shape[1] // 256 + 15 * copies_of(nz, nb)
    v = lambda *shape: pltpu.VMEM(shape, BF16)
    return pl.pallas_call(
        partial(feed_kernel, nf, nz, unit), out_shape=outs,
        in_specs=[hb] * 7, out_specs=[hb] * 10 + [vm] * 2,
        scratch_shapes=[
            v(T, D), v(T, D), v(T, D), v(*full_u), v(*full_w), v(T, FH), v(T, FH), v(*full_u), v(*full_w),
            pltpu.VMEM(bits + (2,) + vec.shape, F32),
            pltpu.SemaphoreType.DMA((n,)), pltpu.SemaphoreType.DMA((n,)), pltpu.SemaphoreType.DMA((24,)),
        ],
        compiler_params=pltpu.CompilerParams(collective_id=0, has_side_effects=True, vmem_limit_bytes=63 << 20),
        name="feed",
    )(tok, cot, vec, wq, wd, wu, ww)


def attend_kernel(nf, nz, head, rot, nh, *refs):
    (attn_in, cot2, bq2, bd2, gu, gw, out2, out2in, dy2, dy2in, tok, docc1, docr1,
     vec, fw, cosp, sina, sinb, mix, mixt,
     output, input_grad, oq, od, ou, ow, ovec) = refs[:27]
    (attn_v, cot_v, bq, bd, qkv, dd, do, o, st, cur, docc, docr, aq, ad, au, aw) = refs[27:43]
    hold_u, hold_w, hold_d = refs[43:43 + nh[0]], refs[43 + nh[0]:43 + nh[0] + nh[1]], refs[43 + nh[0] + nh[1]:43 + sum(nh)]
    hq, hu, gv, vh, gf, outs, igs, send, recv, local, free_u, free_d = refs[43 + sum(nh):]
    at = Place(nf, nz)
    nb = at.nbits
    sems = Sems(send, recv)
    copies = Copies(at, sems, local)
    put, swap = copies.put, copies.swap
    c, p = at.core, 1 - at.core
    S, D = tok.shape
    T = 2 * S
    width = D // 2
    npair = width // 128
    seq = cosp.shape[0]
    nch = T // CH
    half = rot // 2
    RT, FT = 512, outs.shape[1]
    every = (slice(None),) * nb
    own_rows, other_rows = tile(c, S), tile(p, S)
    at.greet(far=True)

    in_u = once([put(gu, au).wait])
    in_p = [put(attn_in, attn_v), put(bq2, bq)]
    in_w = once([put(gw, aw).wait])
    in_do = [put(cot2, cot_v), put(bd2, bd)]
    n1 = docr1.shape[0]
    in_doc = [
        put(docc1, docc.at[own_rows]).wait, swap(docc1, docc.at[own_rows], docc.at[other_rows]),
        put(docr1, docr.at[tile(c, n1)]).wait, swap(docr1, docr.at[tile(c, n1)], docr.at[tile(p, n1)]),
    ]

    def scatters(acc, holds, like=None):
        streams, it = [], iter(holds)
        for start, size, order in streams_of(acc.shape[-2], nb):
            shapes = hold_shapes(nz, nb, size, acc.shape[-1], order)
            mine = [next(it) for _ in shapes]
            if like is not None:
                mine = [hold.at[(slice(None),) * (len(s) - 1) + (pl.ds(0, s[-1]),)] for hold, s in zip(mine, shapes)]
            streams.append(scatter_stream(at, sems, acc, mine, start, size, order))
        return streams

    def release(free):
        for b in range(nb):
            pl.semaphore_signal(free, inc=1, device_id=at.across(b), device_id_type=MESH)

        @pl.when(at.z > 0)
        def _():
            pl.semaphore_signal(free, inc=1, device_id=at.along(-1), device_id_type=MESH)

        @pl.when(at.z < nz - 1)
        def _():
            pl.semaphore_signal(free, inc=1, device_id=at.along(1), device_id_type=MESH)

    def wait_free(free):
        inner = (at.z > 0).astype(jnp.int32) + (at.z < nz - 1).astype(jnp.int32)
        pl.semaphore_wait(free, nb + inner)

    agenda = Agenda(3.0)
    su, sw = scatters(au, hold_u), scatters(aw, hold_w)
    ends = agenda.add(su + sw, [(1.0, in_u)] * len(su) + [(1.5, in_w)] * len(sw), [0] * len(su) + [1] * len(sw))
    end_u, end_w = max(ends[:len(su)]), max(ends[len(su):])
    agenda.at(end_u + 0.1, lambda: release(free_u))
    for cp in in_p:
        cp.wait()

    wq = bq.reshape(D, 3 * width)
    wd = bd.reshape(width, D)

    def project(i):
        r = tile(i, RT)
        ps = tile(lax.rem(i, seq // RT), RT)
        a = attn_v[r, :]
        for part in range(2):
            x = dot(a, wq[:, part * width:(part + 1) * width])
            for m in range(npair):
                s = slice(m * 128, (m + 1) * 128)
                y = x[:, s]
                y = y * cosp[ps, :] + pltpu.roll(y, half, 1) * sina[ps, :] + pltpu.roll(y, 128 - half, 1) * sinb[ps, :]
                hi = y.astype(BF16)
                lo = (y - hi.astype(F32)).astype(BF16)
                e = dot(jnp.concatenate([hi, lo, hi], axis=1), mix[...])
                qkv[r, part * width + s.start:part * width + s.stop] = (fw[:, s] * jnp.exp(e)).astype(BF16)
        qkv[r, 2 * width:] = dot(a, wq[:, 2 * width:]).astype(BF16)

    agenda.until(1.0)
    agenda.loop(T // RT, project, 3.2)
    for cp in in_do:
        cp.wait()

    def mixed_grad(i):
        r = tile(i, RT)
        do[r, :] = dot_nt(cot_v[r, :], wd[...]).astype(BF16)

    agenda.loop(T // RT, mixed_grad, 0.7)
    for w in in_doc:
        w()

    h0 = (lanes(128) % (2 * head)) < head
    h0w = jnp.concatenate([h0, h0], axis=1)
    rowh = lax.broadcasted_iota(jnp.int32, (128, 1), 0) < head
    block = rowh == h0w
    same = (rowh == h0).astype(BF16)
    one = jnp.ones((CH, 128), BF16)
    zero = jnp.zeros((), BF16)
    place = lanes(128) % head
    causal = lax.broadcasted_iota(jnp.int32, (CH, 1), 0) >= lanes(CH)

    def split(x):
        hi = x.astype(BF16)
        return hi, (x - hi.astype(F32)).astype(BF16)

    def masks(i):
        d = docc[tile(i, CH), :]
        inside = jnp.where(causal & (jnp.concatenate([d, d], axis=1) == docr[i]), 1.0, 0.0)
        start = lax.rem(i, seq // CH) == 0
        before = jnp.where(start, -1, docc[pl.ds(jnp.maximum(i * CH - 1, 0), 1), :])
        last = docc[pl.ds(i * CH + CH - 1, 1), :]
        ones = lambda x: jnp.where(x, 1.0, 0.0)
        return inside, ones(d == before), ones(d == last), ones(before == last)

    twice = lambda x: jnp.concatenate([x, x], axis=1)
    beside = lambda a, b: jnp.concatenate([a, b], axis=1)
    above = lambda a, b: jnp.concatenate([a, b], axis=0)
    same2 = above(same, same)

    def scores(q, k, m):
        s0 = dot_nt(jnp.where(h0, q, zero), k)
        s1 = dot_nt(jnp.where(h0, zero, q), k)
        return (s0 * m).astype(BF16), (s1 * m).astype(BF16)

    cur[...] = jnp.zeros_like(cur)

    def forward(i):
        r = tile(i, CH)
        m, cr, tr, kp = masks(i)
        cw, kpw = twice(cr), twice(kp)
        for j in range(npair):
            s = slice(j * 128, (j + 1) * 128)
            q, k, v = (qkv[r, x * width + s.start:x * width + s.stop] for x in range(3))
            va = jnp.concatenate([v, one], axis=1)
            p0, p1 = scores(q, k, m)
            state = cur[j]
            hi, lo = split(state)
            st[i, j, 0] = hi
            st[i, j, 1] = lo
            res = dot(beside(p0, p1), above(jnp.where(h0w, va, zero), jnp.where(h0w, zero, va))) + cw * dot(twice(q), above(hi, lo))
            rd = 1.0 / res[:, 128:]
            att = res[:, :128] * rd
            o[r, s] = att.astype(BF16)
            dnb = (do[r, s].astype(F32) * rd).astype(BF16)
            do[r, s] = dnb
            hi, lo = split(dnb.astype(F32) * att)
            hi, lo = split(-dot(beside(hi, lo), same2))
            dd[r, s] = jnp.where(place == 0, hi, jnp.where(place == 1, lo, zero))
            kt = (k.astype(F32) * tr).astype(BF16)
            cur[j] = kpw * state + jnp.where(block, dot_tn(kt, va), 0.0)
    agenda.loop(nch, forward, 1.95)

    def grad_dense(i):
        ad[...] = dot_tn(o[...], cot_v[...]).astype(BF16).reshape(ad.shape)

    agenda.loop(1, grad_dense, 3.0)

    cur[...] = jnp.zeros_like(cur)
    gf[...] = jnp.zeros_like(gf)

    def backward(ii):
        i = nch - 1 - ii
        r = tile(i, CH)
        ps = tile(lax.rem(i, seq // CH), CH)
        m, cr, tr, kp = masks(i)
        kpw = twice(kp)
        cos, sa, sb = cosp[ps, :], sina[ps, :], sinb[ps, :]

        def unfeature(d, f, s, base):
            de = d * f.astype(F32)
            gf[:, s] += jnp.sum(de.reshape(CH // 8, 8, 128), axis=0)
            g = dot(de.astype(BF16), mixt[...])
            g = g * cos + pltpu.roll(g * sa, 128 - half, 1) + pltpu.roll(g * sb, half, 1)
            qkv[r, base + s.start:base + s.stop] = g.astype(BF16)

        for j in range(npair):
            s = slice(j * 128, (j + 1) * 128)
            q, k, v = (qkv[r, x * width + s.start:x * width + s.stop] for x in range(3))
            va = jnp.concatenate([v, one], axis=1)
            p0, p1 = scores(q, k, m)
            dnb = do[r, s]
            dy = jnp.concatenate([dnb, dd[r, s]], axis=1)
            ds0 = (dot_nt(dy, jnp.where(h0w, va, zero)) * m).astype(BF16)
            ds1 = (dot_nt(dy, jnp.where(h0w, zero, va)) * m).astype(BF16)
            dst = cur[j]
            dhi, dlo = split(dst)
            dq = dot(beside(ds0, ds1), above(jnp.where(h0, k, zero), jnp.where(h0, zero, k))) + cr * dot_nt(
                twice(dy), beside(st[i, j, 0], st[i, j, 1])
            )
            dk = dot_tn(above(ds0, ds1), above(jnp.where(h0, q, zero), jnp.where(h0, zero, q))) + tr * dot_nt(twice(va), beside(dhi, dlo))
            dv = dot_tn(above(p0, p1), above(jnp.where(h0, dnb, zero), jnp.where(h0, zero, dnb))) + tr * dot(k, dhi[:, :128])
            qc = (q.astype(F32) * cr).astype(BF16)
            cur[j] = kpw * dst + jnp.where(block, dot_tn(qc, dy), 0.0)
            unfeature(dq, q, s, 0)
            unfeature(dk, k, s, width)
            qkv[r, 2 * width + s.start:2 * width + s.stop] = dv.astype(BF16)
    agenda.loop(nch, backward, 3.15)


    pl.semaphore_signal(free_d, inc=1, device_id=at.partner(), device_id_type=MESH)
    st_flat = st.reshape(st.shape[0] * st.shape[1] * 2 * 128, 256)

    def cut(ref, width, at_row=0):
        return [ref.at[pl.ds(at_row + k * S, S)] for k in range(D // width)]

    def fetch(src, parts):
        w = D // len(parts)
        return [put(src.at[:, pl.ds(k * w, w)], part) for k, part in enumerate(parts)]

    fetched = fetch(out2in, cut(st_flat, 256)) + fetch(dy2, cut(st_flat, 256, 4 * S))
    fetched.append(put(dy2in, cot_v.at[other_rows]))

    def grad_qkv(i):
        val = dot_tn(attn_v[...], qkv[:, tile(i, width)]).astype(BF16)
        aq[every + (slice(None), tile(i, width))] = val.reshape(aq.shape[:-1] + (width,))

    agenda.loop(3, grad_qkv, 2.4)
    sq, sdn = scatters(aq, hold_u, au), scatters(ad, hold_d)
    wait_u = once([lambda: wait_free(free_u)])
    ready = [(max(agenda.now, end_u + 2.0), wait_u)] * len(sq) + [(agenda.now, None)] * len(sdn)
    ends = agenda.add(sq + sdn, ready, [0] * len(sq) + [1] * len(sdn))
    end_q, end_d = max(ends[:len(sq)]), max(ends[len(sq):])

    def back_qkv(i, rows):
        r = tile(i + rows * (S // RT), RT)
        attn_v[r, :] = dot_nt(qkv[r, :], wq[...]).astype(BF16)

    def back_dense(i, rows):
        r = tile(i + rows * (S // RT), RT)
        qkv[r, :D] = dot(o[r, :], wd[...]).astype(BF16)

    def send_back(src, dst):
        return [
            swap(src.at[other_rows, pl.ds(k * width, width)], part, part) for k, part in enumerate(cut(dst, width))
        ]

    agenda.loop(S // RT, lambda i: back_qkv(i, p), 1.9)
    pl.semaphore_wait(free_d, 1)
    arrive = send_back(attn_v, do)
    agenda.loop(S // RT, lambda i: back_dense(i, p), 0.7)
    arrive += send_back(qkv, dd)
    agenda.loop(S // RT, lambda i: back_qkv(i, c), 1.9)
    fetched.append(put(out2, wq.at[pl.ds(0, S), pl.ds(0, D)]))
    agenda.loop(S // RT, lambda i: back_dense(i, c), 0.7)
    fetched += fetch(tok, cut(o, width))
    agenda.until(agenda.now)

    gv[0] = jnp.zeros((8, D), F32)
    for m in range(npair):
        s = slice(m * 128, (m + 1) * 128)
        gv[0, 4:5, pl.ds(pl.multiple_of((2 * m + c) * 128, 128), 128)] = jnp.sum(gf[:, s], axis=0, keepdims=True) / fw[:, s]
    for cp in fetched:
        cp.wait()
    for w in arrive:
        w()
    first = copies.count

    def stores(i):
        k, r = lax.rem(i, 2), tile(i, FT)
        return [
            pltpu.make_async_copy(outs.at[k], output.at[r], local.at[first + 2 * k]),
            pltpu.make_async_copy(igs.at[k], input_grad.at[r], local.at[first + 2 * k + 1]),
        ]

    def finish(i):
        k = lax.rem(i, 2)

        @pl.when(i >= 2)
        def _():
            for cp in stores(i - 2):
                cp.wait()

        def rows(t, sums):
            part = tile(t, 32)
            at_row = i * FT + t * 32
            own = pl.ds(pl.multiple_of(at_row + c * S, 32), 32)

            def joined(ref, n, base=0):
                return jnp.concatenate(
                    [ref[pl.ds(pl.multiple_of(at_row + base + q * S, 32), 32), :] for q in range(n)], axis=1
                ).astype(F32)

            here = pl.ds(pl.multiple_of(at_row, 32), 32)
            x = joined(o, D // width)
            n, rstd = normed(x)
            out1 = qkv[own, :D].astype(F32) + joined(dd, D // width)
            outs[k, part, :] = (x + out1 + (wq[here, :D].astype(F32) + joined(st_flat, D // 256))).astype(BF16)
            d1 = attn_v[own, :].astype(F32) + joined(do, D // width)
            d2 = joined(st_flat, D // 256, 4 * S) + cot_v[pl.ds(pl.multiple_of(at_row + p * S, 32), 32), :].astype(F32)
            dn = d1 * vec[0:1, :] + d2 * vec[2:3, :]
            dx = rstd * (dn - jnp.mean(dn, axis=-1, keepdims=True) - n * jnp.mean(dn * n, axis=-1, keepdims=True))
            igs[k, part, :] = cot_v[own, :].astype(F32) + dx
            fold = lambda y: jnp.sum(y.reshape(4, 8, D), axis=0)
            return tuple(a + fold(y) for a, y in zip(sums, (d1 * n, d1, d2 * n, d2)))

        sums = lax.fori_loop(0, FT // 32, rows, (jnp.zeros((8, D), F32),) * 4)
        for q, y in enumerate(sums):
            gv[0, q:q + 1, :] += jnp.sum(y, axis=0, keepdims=True)
        for cp in stores(i):
            cp.start()

    agenda.loop(S // FT, finish, 1.5)
    for i in range(S // FT - 2, S // FT):
        for cp in stores(i):
            cp.wait()

    peers = [at.partner()] + [at.across(b) for b in range(nb)]
    step = 1
    while step < nz:
        peers.append(at.fold(step))
        step *= 2
    rounds = []
    for k, peer in enumerate(peers):
        cp = sems.copy(gv.at[k], vh.at[k], sems.take(), peer)

        def arrive(cp=cp, k=k):
            cp.wait_recv()
            gv[k + 1] = gv[k] + vh[k]

        rounds.append((cp.start, arrive, cp.wait_send, "small", 4.0 * 8 * D))
    agenda.add([rounds], [(agenda.now, None)])
    me = at.slot(())
    sent = []
    for acc, hold, out, end in ((aq, hq, oq, end_q), (au, hu, ou, end_u)):
        half = hold.shape[0]
        cols = at.columns(acc, at.z)
        cp = sems.copy(acc.at[me + (tile(p, half), cols)], hold, sems.take(), at.partner())

        def act(cp=cp, acc=acc, out=out, half=half, cols=cols):
            cp.start()
            out[c] = acc[me + (tile(c, half), cols)]

        def arrive(cp=cp, hold=hold, out=out):
            cp.wait_recv()
            out[p] = hold[...]

        begin = max(end + 0.1, agenda.now)
        agenda.at(begin, act)
        agenda.at(begin + 4.0, arrive)
        sent.append(cp)

    def keep(acc, out):
        out[...] = acc[me + (slice(None), at.columns(acc, at.z))]

    agenda.at(max(end_d + 0.1, agenda.now), lambda: keep(ad, od))
    agenda.at(end_w + 0.1, lambda: keep(aw, ow))
    agenda.until(1e9)
    ovec[...] = gv[len(peers)]
    copies.leave()
    for cp in sent:
        cp.wait_send()
    for s in su + sw + sdn + sq + [rounds]:
        for r in s:
            r[2]()


def attend(nf, nz, head, rot, attn_in, cot2, bq, bd, gu, gw, out2, out2in, dy2, dy2in, tok, docc, docr, vec, fw, *tabs):
    sd = jax.ShapeDtypeStruct
    nb = (nf // 2).bit_length() - 1
    S, D = tok.shape
    T, W = 2 * S, D // 2
    own = lambda a: (a.shape[-2], a.shape[-1] // nz)

    def holds(a):
        shapes = []
        for _, size, order in streams_of(a.shape[-2], nb):
            shapes += hold_shapes(nz, nb, size, a.shape[-1], order)
        return shapes

    room = [holds(gu), holds(gw), holds(bd)]
    halves = [(own(a)[0] // 2, own(a)[1]) for a in (bq, gu)]
    nsteps = 1 + nb + nz.bit_length() - 1
    ncopies = 12 * copies_of(nz, nb) + 6 + nsteps + 2
    vm, hb = pl.BlockSpec(memory_space=pltpu.VMEM), pl.BlockSpec(memory_space=pl.ANY)
    v = lambda *shape: pltpu.VMEM(shape, BF16)
    f = lambda *shape: pltpu.VMEM(shape, F32)
    i32 = lambda *shape: pltpu.VMEM(shape, jnp.int32)
    outs = [sd((S, D), BF16), sd((S, D), F32)]
    outs += [sd((2,) + halves[0], BF16), sd(own(bd), BF16), sd((2,) + halves[1], BF16), sd(own(gw), BF16), sd((8, D), F32)]
    return pl.pallas_call(
        partial(attend_kernel, nf, nz, head, rot, tuple(len(r) for r in room)), out_shape=outs,
        in_specs=[hb] * 13 + [vm] * 7, out_specs=[hb] * 2 + [vm] * 5,
        scratch_shapes=[
            v(T, D), v(T, D), v(*bq.shape), v(*bd.shape), v(T, 3 * W), v(T, W), v(T, W), v(T, W),
            v(T // CH, W // 128, 2, 128, 256), f(W // 128, 128, 256), i32(T, 128), i32(2 * docr.shape[0], 1, CH),
            v(*bq.shape), v(*bd.shape), v(*gu.shape), v(*gw.shape),
        ]
        + [v(*s) for r in room for s in r] + [v(*s) for s in halves]
        + [f(nsteps + 1, 8, D), f(nsteps, 8, D), f(8, W), v(2, 128, D), f(2, 128, D)]
        + [pltpu.SemaphoreType.DMA((ncopies,)), pltpu.SemaphoreType.DMA((ncopies,)), pltpu.SemaphoreType.DMA((28,))]
        + [pltpu.SemaphoreType.REGULAR] * 2,
        compiler_params=pltpu.CompilerParams(collective_id=1, has_side_effects=True, vmem_limit_bytes=63 << 20),
        name="attend",
    )(attn_in, cot2, bq, bd, gu, gw, out2, out2in, dy2, dy2in, tok, docc, docr, vec, fw, *tabs)


def body(nf, nz, tokens, doc_starts, w_qkv, w_dense, w_up, w_down, norm1_gain, norm1_bias, norm2_gain, norm2_bias, feature_weight, cotangent):
    rows, D = tokens.shape
    unit = w_down.shape[0]

    block = unit
    if unit % 128:
        block = w_up.shape[1] // 2
        w_up = w_up.reshape(-1, block // unit, 2, unit).swapaxes(1, 2).reshape(w_up.shape)

    def unturn(g, block):
        _, r, n = g.shape
        return g.reshape(2, r, n // block, block).transpose(1, 2, 0, 3).reshape(r, 2 * n)

    per = 128 // w_dense.shape[0]
    source = [(2 * (k // per) + c) * per + k % per for k in range(nf // 2) for c in range(2)]
    if per > 1:
        w_dense = lax.ppermute(w_dense, "fsdp", [(s, d) for d, s in enumerate(source)])

    doc = jnp.cumsum(doc_starts.reshape(-1, SEQ_LEN), axis=1).astype(jnp.int32).reshape(rows)
    vec = jnp.stack([norm1_gain, norm1_bias, norm2_gain, norm2_bias, feature_weight] + [jnp.zeros_like(norm1_gain)] * 3)
    cosp, sina, sinb, mix = tables(SEQ_LEN, ROT, HEAD, FEATS)
    mix = jnp.asarray(mix)
    mixh = mix.astype(BF16)
    mixl = (mix - mixh.astype(F32)).astype(BF16)
    attn_in, cot2, bq, bd, gu, gw, out2, out2in, dy2, dy2in, vec8, fw = feed(
        nf, nz, block, tokens, cotangent, vec, w_qkv, w_dense, w_up, w_down
    )
    output, input_grad, oq, od, ou, ow, gv = attend(
        nf, nz, HEAD, ROT, attn_in, cot2, bq, bd, gu, gw, out2, out2in, dy2, dy2in, tokens,
        jnp.broadcast_to(doc[:, None], (rows, 128)), doc.reshape(-1, 1, CH), vec8, fw, cosp, sina, sinb,
        jnp.concatenate([mixh, mixh, mixl]), mixh.T,
    )
    if per > 1:
        od = lax.ppermute(od, "fsdp", [(d, s) for d, s in enumerate(source)])
    own = gv.reshape(8, nf, -1)
    own = lax.dynamic_index_in_dim(own, lax.axis_index("fsdp"), 1, keepdims=False)
    return (
        output, input_grad,
        unturn(oq, 128).astype(F32), od.astype(F32), unturn(ou, unit).astype(F32), ow.astype(F32),
        own[0], own[1], own[2], own[3], own[4],
    )


def solution(mesh):
    nf, nz = mesh.shape["fsdp"], mesh.shape["inner"]
    rows, mat, vec = P(("fsdp", "inner"), None), P("fsdp", "inner"), P("fsdp")
    in_specs = (rows, P(("fsdp", "inner"))) + (mat,) * 4 + (vec,) * 5 + (rows,)
    out_specs = (rows, rows) + (mat,) * 4 + (vec,) * 5
    return jax.shard_map(partial(body, nf, nz), mesh=mesh, in_specs=in_specs, out_specs=out_specs, check_vma=False)
```

```python
from functools import partial
import math
from statistics import NormalDist

import jax
import jax.numpy as jnp
import numpy as np
from jax import lax
from jax.experimental import pallas as pl
from jax.experimental.pallas import tpu as pltpu
from jax.sharding import PartitionSpec as P

MESH = pl.DeviceIdType.MESH
BF16 = jnp.bfloat16
F32 = jnp.float32


HEAD = 64
ROT = 16
FEATS = 64
SEQ_LEN = 1024

class Place:
    def __init__(self, nf, nz):
        self.nf, self.nz = nf, nz
        self.nbits = (nf // 2).bit_length() - 1
        self.f = lax.axis_index("fsdp")
        self.z = lax.axis_index("inner")
        self.core = lax.rem(self.f, 2)
        self.bits = [lax.rem(lax.div(self.f, 2 << b), 2) for b in range(self.nbits)]

    def partner(self):
        return (self.f + 1 - 2 * self.core, self.z)

    def across(self, b):
        return (self.f + (1 - 2 * self.bits[b]) * (2 << b), self.z)

    def along(self, step):
        return (self.f, self.z + step)

    def slot(self, done, flip=None):
        index = []
        for b in reversed(range(self.nbits)):
            if b in done:
                index.append(slice(None))
            elif b == flip:
                index.append(1 - self.bits[b])
            else:
                index.append(self.bits[b])
        return tuple(index)

    def columns(self, buf, zsel):
        if zsel is None:
            return slice(None)
        width = buf.shape[-1] // self.nz
        return pl.ds(pl.multiple_of(zsel * width, width), width)

    def greet(self, far=False):
        bar = pltpu.get_barrier_semaphore()
        z, nz = self.z, self.nz
        fixed = [self.partner()] + [self.across(b) for b in range(self.nbits)]
        for peer in fixed:
            pl.semaphore_signal(bar, inc=1, device_id=peer, device_id_type=MESH)

        @pl.when(z > 0)
        def _():
            pl.semaphore_signal(bar, inc=1, device_id=self.along(-1), device_id_type=MESH)

        @pl.when(z < nz - 1)
        def _():
            pl.semaphore_signal(bar, inc=1, device_id=self.along(1), device_id_type=MESH)

        count = len(fixed)
        if far and nz > 2:
            step = 2
            while step < nz:
                pl.semaphore_signal(
                    bar, inc=1, device_id=self.fold(step), device_id_type=MESH
                )
                count += 1
                step *= 2
        inner = (z > 0).astype(jnp.int32) + (z < nz - 1).astype(jnp.int32)
        pl.semaphore_wait(bar, count + inner)

    def fold(self, step):
        bit = lax.rem(lax.div(self.z, step), 2)
        return (self.f, self.z + (1 - 2 * bit) * step)


class Sems:
    def __init__(self, send, recv):
        self.send, self.recv, self.count = send, recv, 0

    def take(self):
        self.count += 1
        return self.count - 1

    def copy(self, src, dst, i, peer):
        return pltpu.make_async_remote_copy(
            src_ref=src,
            dst_ref=dst,
            send_sem=self.send.at[i],
            recv_sem=self.recv.at[i],
            device_id=peer,
            device_id_type=MESH,
        )


def streams_of(rows, nbits, cuts=1):
    up, down = list(range(nbits)), list(reversed(range(nbits)))
    parts = [(3, ["z"] + up), (3, ["z"] + down)] * cuts + [(2, up + ["z"]), (2, down + ["z"])][:cuts]
    whole, units, at, streams = sum(n for n, _ in parts), rows // 16, 0, []
    for k, (_, order) in enumerate(parts):
        end = round(units * sum(n for n, _ in parts[:k + 1]) / whole)
        if end > at:
            streams.append((at * 16, (end - at) * 16, order))
        at = end
    return streams


def copies_of(nz, nbits):
    return nbits + 2 * (nz - 1)


def gather_stream(at, sems, buf, start, size, order):
    rows = pl.ds(start, size)
    rounds = []
    done, zdone = (), False

    def along(k, done):
        ids = (sems.take(), sems.take())

        def right(zsel):
            ref = buf.at[at.slot(done) + (rows, at.columns(buf, zsel))]
            return sems.copy(ref, ref, ids[0], at.along(1))

        def left(zsel):
            ref = buf.at[at.slot(done) + (rows, at.columns(buf, zsel))]
            return sems.copy(ref, ref, ids[1], at.along(-1))

        z, nz = at.z, at.nz
        goes_right = (z < nz - 1) & (z - k + 1 >= 0)
        goes_left = (z > 0) & (z + k - 1 <= nz - 1)

        def send():
            pl.when(goes_right)(lambda: right(z - k + 1).start())
            pl.when(goes_left)(lambda: left(z + k - 1).start())

        def arrive():
            pl.when(z - k >= 0)(lambda: right(z - k).wait_recv())
            pl.when(z + k <= nz - 1)(lambda: left(z + k).wait_recv())

        def leave():
            pl.when(goes_right)(lambda: right(z - k + 1).wait_send())
            pl.when(goes_left)(lambda: left(z + k - 1).wait_send())

        return send, arrive, leave

    def across(b, done, zsel):
        i = sems.take()
        mine = buf.at[at.slot(done) + (rows, at.columns(buf, zsel))]
        theirs = buf.at[at.slot(done, flip=b) + (rows, at.columns(buf, zsel))]
        out = sems.copy(mine, mine, i, at.across(b))
        back = sems.copy(theirs, theirs, i, at.across(b))
        return out.start, back.wait_recv, out.wait_send

    piece = size * (buf.shape[-1] // at.nz) * 2
    for dim in order:
        if dim == "z":
            rounds += [along(k, done) + ("z", piece << len(done)) for k in range(1, at.nz)]
            zdone = True
        else:
            nbytes = (piece << len(done)) * (at.nz if zdone else 1)
            rounds.append(across(dim, done, None if zdone else at.z) + (dim, nbytes))
            done = done + (dim,)
    return rounds


def scatter_stream(at, sems, acc, holds, start, size, order):
    rows = pl.ds(start, size)
    rounds = []
    left_bits, zleft = set(range(at.nbits)), True

    def along(k, remaining, hold):
        ids = (sems.take(), sems.take())
        z, nz = at.z, at.nz

        def part(zsel):
            return acc.at[at.slot(remaining) + (rows, at.columns(acc, zsel))]

        def right(zsel):
            return sems.copy(part(zsel), hold.at[2 * k - 2], ids[0], at.along(1))

        def left(zsel):
            return sems.copy(part(zsel), hold.at[2 * k - 1], ids[1], at.along(-1))

        goes_right = z + k <= nz - 1
        goes_left = z - k >= 0

        def send():
            pl.when(goes_right)(lambda: right(z + k).start())
            pl.when(goes_left)(lambda: left(z - k).start())

        def arrive():
            @pl.when((z >= 1) & (z - 1 + k <= nz - 1))
            def _():
                right(z - 1 + k).wait_recv()
                ref = part(z - 1 + k)
                ref[...] += hold[2 * k - 2]

            @pl.when((z <= nz - 2) & (z + 1 - k >= 0))
            def _():
                left(z + 1 - k).wait_recv()
                ref = part(z + 1 - k)
                ref[...] += hold[2 * k - 1]

        def leave():
            pl.when(goes_right)(lambda: right(z + k).wait_send())
            pl.when(goes_left)(lambda: left(z - k).wait_send())

        return send, arrive, leave

    def across(b, remaining, zsel, hold):
        i = sems.take()
        out = sems.copy(
            acc.at[at.slot(remaining, flip=b) + (rows, at.columns(acc, zsel))], hold, i, at.across(b)
        )

        def arrive():
            out.wait_recv()
            ref = acc.at[at.slot(remaining) + (rows, at.columns(acc, zsel))]
            ref[...] += hold[...]

        return out.start, arrive, out.wait_send

    piece = size * (acc.shape[-1] // at.nz) * 2
    holds = iter(holds)
    for dim in reversed(order):
        if dim == "z":
            hold = next(holds)
            rounds += [
                along(k, tuple(left_bits), hold) + ("z", piece << len(left_bits))
                for k in range(at.nz - 1, 0, -1)
            ]
            zleft = False
        else:
            left_bits = left_bits - {dim}
            nbytes = (piece << len(left_bits)) * (at.nz if zleft else 1)
            rounds.append(across(dim, tuple(left_bits), None if zleft else at.z, next(holds)) + (dim, nbytes))
    return rounds


def hold_shapes(nz, nbits, size, width, order):
    shapes, bits, zleft = [], nbits, True
    for dim in reversed(order):
        if dim == "z":
            shapes.append((2 * (nz - 1),) + (2,) * bits + (size, width // nz))
            zleft = False
        else:
            bits -= 1
            shapes.append((2,) * bits + (size, width if zleft else width // nz))
    return shapes


LINK_RATE = 48000.0


class Agenda:
    def __init__(self, hop):
        self.hop, self.events, self.now, self.free = hop, [], 0.0, {}

    def add(self, streams, ready, rank=None):
        rank = rank or [0] * len(streams)
        took = [[rounds[r][4] / LINK_RATE for r in range(len(rounds))] for rounds in streams]
        left = [[sum(t[r:]) + self.hop * (len(t) - r) for r in range(len(t) + 1)] for t in took]
        state = [[0, t] for t, _ in ready]
        while True:
            best = None
            for i, rounds in enumerate(streams):
                r, t = state[i]
                if r < len(rounds):
                    begin = max(t, self.free.get(rounds[r][3], 0.0))
                    key = (begin, rank[i], -left[i][r], i)
                    best = key if best is None or key < best else best
            if best is None:
                break
            begin, i = best[0], best[3]
            r = state[i][0]
            rounds = streams[i]
            wait = ready[i][1] if r == 0 else rounds[r - 1][1]

            def act(wait=wait, send=rounds[r][0]):
                if wait is not None:
                    wait()
                send()

            self.events.append((begin, act))
            self.free[rounds[r][3]] = begin + took[i][r]
            state[i] = [r + 1, begin + took[i][r] + self.hop]
            if r + 1 == len(rounds):
                self.events.append((state[i][1], rounds[r][1]))
        self.events.sort(key=lambda e: e[0])
        return [t for _, t in state]

    def at(self, time, act):
        self.events.append((time, act))
        self.events.sort(key=lambda e: e[0])

    def until(self, time):
        while self.events and self.events[0][0] <= time:
            self.events.pop(0)[1]()
        self.now = max(self.now, time)

    def loop(self, n, body, took):
        due = [[] for _ in range(n)]
        while self.events:
            step = max(0, math.ceil((self.events[0][0] - self.now) / took - 0.5))
            if step >= n:
                break
            due[step].append(self.events.pop(0)[1])
        self.now += n * took

        def step(i, carry):
            for u, acts in enumerate(due):
                if acts:

                    @pl.when(i == u)
                    def _(acts=acts):
                        for act in acts:
                            act()

            body(i)
            return carry

        lax.fori_loop(0, n, step, 0)


def once(acts):
    done = []

    def run():
        if not done:
            for act in acts:
                act()
            done.append(1)

    return run


class Copies:
    def __init__(self, at, sems, local):
        self.at, self.sems, self.local, self.count, self.sent = at, sems, local, 0, []

    def put(self, src, dst):
        cp = pltpu.make_async_copy(src, dst, self.local.at[self.count])
        self.count += 1
        cp.start()
        return cp

    def swap(self, src, dst, arrives):
        i = self.sems.take()
        cp = self.sems.copy(src, dst, i, self.at.partner())
        cp.start()
        self.sent.append(cp)
        return self.sems.copy(src, arrives, i, self.at.partner()).wait_recv

    def leave(self):
        for cp in self.sent:
            cp.wait_send()


CH = 256

def dot(a, b):
    return jnp.dot(a, b, preferred_element_type=F32)

def dot_nt(a, b):
    return lax.dot_general(a, b, (((1,), (1,)), ((), ())), preferred_element_type=F32)

def dot_tn(a, b):
    return lax.dot_general(a, b, (((0,), (0,)), ((), ())), preferred_element_type=F32)

def tile(i, n):
    return pl.ds(pl.multiple_of(i * n, n), n)

def lanes(width):
    return lax.broadcasted_iota(jnp.int32, (1, width), 1)

def normed(x):
    center = x - jnp.mean(x, axis=-1, keepdims=True)
    spread = jnp.mean(center * center, axis=-1, keepdims=True)
    rstd = lax.rsqrt(spread + 1e-05)
    return center * rstd, rstd

def gelu_pair(x):
    e = jnp.exp2((-0.5 * math.log2(math.e)) * (x * x))
    d = 1.0 + (0.3275911 / math.sqrt(2.0)) * jnp.abs(x)
    t = 1.0 / d
    poly = t * (0.127414796 + t * (-0.142248368 + t * (0.7107068705 + t * (-0.7265760135 + t * 0.5307027145))))
    tail = poly * e
    phi = jnp.where(x >= 0, 1.0 - tail, tail)
    return x * phi, phi + x * e * (1.0 / math.sqrt(2.0 * math.pi))


def tables(seq, rot, head, feats):
    half = rot // 2
    angles = np.arange(seq)[:, None] / 10000.0 ** (np.arange(0, rot, 2) / rot)[None, :]
    cosp, sina, sinb = np.ones((seq, 128)), np.zeros((seq, 128)), np.zeros((seq, 128))
    for base in range(0, 128, head):
        cosp[:, base:base + half] = np.cos(angles)
        cosp[:, base + half:base + rot] = np.cos(angles)
        sina[:, base + half:base + rot] = np.sin(angles)
        sinb[:, base:base + half] = -np.sin(angles)
    k, i = np.arange(head)[:, None], np.arange(head)[None, :]
    cosine = np.where(k == 0, math.sqrt(1.0 / head), math.sqrt(2.0 / head)) * np.cos(math.pi * (i + 0.5) * k / head)
    j = np.arange(feats)[None, :]
    level = (((j * (2 * k + 1) + k) % feats) + 0.5) / feats
    normals = np.vectorize(NormalDist().inv_cdf)(level)
    mixing = cosine.T @ normals / math.sqrt(head)
    mix = np.zeros((128, 128), np.float32)
    for base in range(0, 128, head):
        mix[base:base + head, base:base + feats] = mixing
    return cosp.astype(np.float32), sina.astype(np.float32), sinb.astype(np.float32), mix


def feed_kernel(nf, nz, unit, tok, cot, vec1, wq1, wd1, wu1, ww1,
                attn_in, cot2, bq, bd, gu2, gw2, out2, out2in, dy2, dy2in, vec, fw,
                tok_v, mlp_v, cot_v, wu, ww, h, pre, gu, gw, vecs, send, recv, local):
    at = Place(nf, nz)
    nb = at.nbits
    sems = Sems(send, recv)
    copies = Copies(at, sems, local)
    put, swap = copies.put, copies.swap
    c, p = at.core, 1 - at.core
    S, D = tok.shape
    T = 2 * S
    FH = h.shape[1]
    RT, FB = 512, 512
    every = (slice(None),) * nb
    me = at.slot(())
    own_rows, other_rows = tile(c, S), tile(p, S)
    at.greet()

    def halves(w, buf, block):
        r, n = w.shape
        here, there = [], []
        for t in range(n // (2 * block)):
            def part(core, t=t):
                return w.at[:, pl.ds(pl.multiple_of((2 * t + core) * block, block), block)]

            def place(core, t=t):
                cols = pl.ds(pl.multiple_of(at.z * (n // 2) + t * block, 128), block)
                return buf.at[me + (tile(core, r), cols)]

            there.append(swap(part(p), place(c), place(p)))
            here.append(put(part(c), place(c)).wait)
        return there + here

    z = lambda b: at.columns(b, at.z)
    in_u = halves(wu1, wu, unit)
    in_vec = [swap(vec1, vecs.at[me + (c,)], vecs.at[me + (p,)]), put(vec1, vecs.at[me + (c,)]).wait]
    in_tok = [put(tok, tok_v.at[own_rows]).wait, swap(tok, tok_v.at[own_rows], tok_v.at[other_rows])]
    in_w = [put(ww1, ww.at[me + (slice(None), z(ww))]).wait]
    in_q = halves(wq1, bq, 128)
    in_d = [put(wd1, bd.at[me + (slice(None), z(bd))]).wait]
    in_cot = [put(cot, cot_v.at[own_rows]).wait, swap(cot, cot_v.at[own_rows], cot_v.at[other_rows])]

    agenda = Agenda(4.5)
    streams, ready, rank, ends = [], [], [], []
    for buf, waits, time, r, cuts in (
        (wu, in_u, 2.0, 0, 2), (ww, in_w, 2.0, 1, 1), (bq, in_q, 12.0, 2, 1), (bd, in_d, 4.0, 2, 1)
    ):
        wait = once(waits)
        for start, size, order in streams_of(buf.shape[-2], nb, cuts):
            streams.append(gather_stream(at, sems, buf, start, size, order))
            ready.append((time, wait))
            rank.append(r)
    ends = agenda.add(streams, ready, rank)
    end_u, end_w = (max(e for e, r in zip(ends, rank) if r == k) for k in (0, 1))
    agenda.until(4.0)
    for w in in_vec:
        w()
    done, small = (), []
    for b in range(nb):
        i = sems.take()
        m, t = vecs.at[at.slot(done)], vecs.at[at.slot(done, flip=b)]
        out = sems.copy(m, m, i, at.across(b))
        out.start()
        sems.copy(t, t, i, at.across(b)).wait_recv()
        small.append(out)
        done = done + (b,)
    w = vec1.shape[1]
    for f in range(nf):
        at_f = tuple((f >> (b + 1)) & 1 for b in reversed(range(nb))) + (f & 1,)
        vec[:, f * w:(f + 1) * w] = vecs[at_f]
    for m in range(fw.shape[1] // 128):
        fw[:, m * 128:(m + 1) * 128] = vec[4:5, pl.ds(pl.multiple_of((2 * m + c) * 128, 128), 128)]
    agenda.until(11.0)
    for w in in_tok:
        w()

    def ln(i):
        r = tile(i, CH)
        n, _ = normed(tok_v[r, :].astype(F32))
        tok_v[r, :] = (n * vec[0:1, :] + vec[1:2, :]).astype(BF16)
        mlp_v[r, :] = (n * vec[2:3, :] + vec[3:4, :]).astype(BF16)

    agenda.loop(T // CH, ln, 0.5)
    stores = [put(tok_v, attn_in)]
    agenda.until(end_u)

    top = (FH // FB).bit_length() - 1
    bits_of = lambda m: tuple((m >> b) & 1 for b in reversed(range(top))) + (slice(None),) * (nb - top)
    wu2, ww2 = wu.reshape(D, FH), ww.reshape(FH, D)

    for m in range(FH // FB):
        cols = slice(m * FB, (m + 1) * FB)

        def hidden(i, cols=cols):
            r = tile(i, RT)
            act, slope = gelu_pair(dot(mlp_v[r, :], wu2[:, cols]))
            h[r, cols] = act.astype(BF16)
            pre[r, cols] = slope.astype(BF16)

        agenda.loop(T // RT, hidden, 1.1)
    for w in in_cot:
        w()
    keep_cot = put(cot_v, cot2)
    gu_flat, gw_flat = gu.reshape(D, FH), gw.reshape(FH, D)

    def grad_down(m):
        gw_flat[tile(m, FB), :] = dot_tn(h[:, tile(m, FB)], cot_v[...]).astype(BF16)

    agenda.loop(FH // FB, grad_down, 2.4)
    stores.append(put(gw, gw2))
    agenda.until(end_w)

    for m in range(FH // FB):
        cols = slice(m * FB, (m + 1) * FB)

        def slopes(i, cols=cols, m=m):
            r = tile(i, RT)
            dh = dot_nt(cot_v[r, :], ww2[cols, :])
            pre[r, cols] = (dh * pre[r, cols].astype(F32)).astype(BF16)

        agenda.loop(T // RT, slopes, 0.75)


    def grad_up(m):
        gu_flat[:, tile(m, FB)] = dot_tn(mlp_v[...], pre[:, tile(m, FB)]).astype(BF16)

    agenda.loop(FH // FB, grad_up, 2.5)
    stores.append(put(gu, gu2))

    keep_cot.wait()

    def back(i, rows, into):
        r = tile(i + rows * (S // RT), RT)
        into[tile(i, RT), :] = dot(h[r, :], ww2[...]).astype(BF16)
        into[tile(i + S // RT, RT), :] = dot_nt(pre[r, :], wu2[...]).astype(BF16)

    agenda.loop(S // RT, lambda i: back(i, p, cot_v), 5.0)
    arrive = [
        swap(cot_v.at[pl.ds(0, S)], out2in, out2in),
        swap(cot_v.at[pl.ds(S, S)], dy2in, dy2in),
    ]
    agenda.loop(S // RT, lambda i: back(i, c, mlp_v), 5.0)
    stores += [put(mlp_v.at[pl.ds(0, S)], out2), put(mlp_v.at[pl.ds(S, S)], dy2)]
    agenda.until(1e9)
    for w in arrive:
        w()
    for cp in stores:
        cp.wait()
    copies.leave()
    for cp in small:
        cp.wait_send()
    for s in streams:
        for r in s:
            r[2]()


def feed(nf, nz, unit, tok, cot, vec, wq, wd, wu, ww):
    bits = (2,) * ((nf // 2).bit_length() - 1)
    nb = len(bits)
    S, D = tok.shape
    T, W = 2 * S, D // 2
    sd = jax.ShapeDtypeStruct
    hb, vm = pl.BlockSpec(memory_space=pl.ANY), pl.BlockSpec(memory_space=pltpu.VMEM)
    full_u = bits + (2 * wu.shape[0], nz * wu.shape[1] // 2)
    full_w = bits + (ww.shape[0], nz * ww.shape[1])
    full_q = bits + (2 * wq.shape[0], nz * wq.shape[1] // 2)
    full_d = bits + (wd.shape[0], nz * wd.shape[1])
    FH = full_u[-1]
    outs = [sd((T, D), BF16), sd((T, D), BF16), sd(full_q, BF16), sd(full_d, BF16), sd(full_u, BF16), sd(full_w, BF16)]
    outs += [sd((S, D), BF16)] * 4 + [sd((8, D), F32), sd((1, W), F32)]
    n = 6 + nb + wu.shape[1] // (2 * unit) + wq.shape[1] // 256 + 15 * copies_of(nz, nb)
    v = lambda *shape: pltpu.VMEM(shape, BF16)
    return pl.pallas_call(
        partial(feed_kernel, nf, nz, unit), out_shape=outs,
        in_specs=[hb] * 7, out_specs=[hb] * 10 + [vm] * 2,
        scratch_shapes=[
            v(T, D), v(T, D), v(T, D), v(*full_u), v(*full_w), v(T, FH), v(T, FH), v(*full_u), v(*full_w),
            pltpu.VMEM(bits + (2,) + vec.shape, F32),
            pltpu.SemaphoreType.DMA((n,)), pltpu.SemaphoreType.DMA((n,)), pltpu.SemaphoreType.DMA((24,)),
        ],
        compiler_params=pltpu.CompilerParams(collective_id=0, has_side_effects=True, vmem_limit_bytes=63 << 20),
        name="feed",
    )(tok, cot, vec, wq, wd, wu, ww)


def attend_kernel(nf, nz, head, rot, block_u, nh, *refs):
    (attn_in, cot2, bq2, bd2, gu, gw, out2, out2in, dy2, dy2in, tok, docc1, docr1,
     vec, fw, cosp, sina, sinb, mix, mixt,
     output, input_grad, oq, od, ou, ow, ovec) = refs[:27]
    (attn_v, cot_v, bq, bd, qkv, dd, do, o, st, cur, docc, docr, aq, ad, au, aw) = refs[27:43]
    hold_u, hold_w, hold_d = refs[43:43 + nh[0]], refs[43 + nh[0]:43 + nh[0] + nh[1]], refs[43 + nh[0] + nh[1]:43 + sum(nh)]
    hq, hu, gv, vh, gf, outs, igs, send, recv, local, free_u, free_d = refs[43 + sum(nh):]
    at = Place(nf, nz)
    nb = at.nbits
    sems = Sems(send, recv)
    copies = Copies(at, sems, local)
    put, swap = copies.put, copies.swap
    c, p = at.core, 1 - at.core
    S, D = tok.shape
    T = 2 * S
    width = D // 2
    npair = width // 128
    seq = cosp.shape[0]
    nch = T // CH
    half = rot // 2
    RT, FT = 512, outs.shape[1]
    every = (slice(None),) * nb
    own_rows, other_rows = tile(c, S), tile(p, S)
    at.greet(far=True)

    in_u = once([put(gu, au).wait])
    in_p = [put(attn_in, attn_v), put(bq2, bq)]
    in_w = once([put(gw, aw).wait])
    in_do = [put(cot2, cot_v), put(bd2, bd)]
    n1 = docr1.shape[0]
    in_doc = [
        put(docc1, docc.at[own_rows]).wait, swap(docc1, docc.at[own_rows], docc.at[other_rows]),
        put(docr1, docr.at[tile(c, n1)]).wait, swap(docr1, docr.at[tile(c, n1)], docr.at[tile(p, n1)]),
    ]

    def scatters(acc, holds, like=None):
        streams, it = [], iter(holds)
        for start, size, order in streams_of(acc.shape[-2], nb):
            shapes = hold_shapes(nz, nb, size, acc.shape[-1], order)
            mine = [next(it) for _ in shapes]
            if like is not None:
                mine = [hold.at[(slice(None),) * (len(s) - 1) + (pl.ds(0, s[-1]),)] for hold, s in zip(mine, shapes)]
            streams.append(scatter_stream(at, sems, acc, mine, start, size, order))
        return streams

    def release(free):
        for b in range(nb):
            pl.semaphore_signal(free, inc=1, device_id=at.across(b), device_id_type=MESH)

        @pl.when(at.z > 0)
        def _():
            pl.semaphore_signal(free, inc=1, device_id=at.along(-1), device_id_type=MESH)

        @pl.when(at.z < nz - 1)
        def _():
            pl.semaphore_signal(free, inc=1, device_id=at.along(1), device_id_type=MESH)

    def wait_free(free):
        inner = (at.z > 0).astype(jnp.int32) + (at.z < nz - 1).astype(jnp.int32)
        pl.semaphore_wait(free, nb + inner)

    agenda = Agenda(3.0)
    su, sw = scatters(au, hold_u), scatters(aw, hold_w)
    ends = agenda.add(su + sw, [(1.0, in_u)] * len(su) + [(1.5, in_w)] * len(sw), [0] * len(su) + [1] * len(sw))
    end_u, end_w = max(ends[:len(su)]), max(ends[len(su):])
    agenda.at(end_u + 0.1, lambda: release(free_u))
    for cp in in_p:
        cp.wait()

    wq = bq.reshape(D, 3 * width)
    wd = bd.reshape(width, D)

    def project(i):
        r = tile(i, RT)
        ps = tile(lax.rem(i, seq // RT), RT)
        a = attn_v[r, :]
        for part in range(2):
            x = dot(a, wq[:, part * width:(part + 1) * width])
            for m in range(npair):
                s = slice(m * 128, (m + 1) * 128)
                y = x[:, s]
                y = y * cosp[ps, :] + pltpu.roll(y, half, 1) * sina[ps, :] + pltpu.roll(y, 128 - half, 1) * sinb[ps, :]
                hi = y.astype(BF16)
                lo = (y - hi.astype(F32)).astype(BF16)
                e = dot(jnp.concatenate([hi, lo, hi], axis=1), mix[...])
                qkv[r, part * width + s.start:part * width + s.stop] = (fw[:, s] * jnp.exp(e)).astype(BF16)
        qkv[r, 2 * width:] = dot(a, wq[:, 2 * width:]).astype(BF16)

    agenda.until(1.0)
    agenda.loop(T // RT, project, 3.2)
    for cp in in_do:
        cp.wait()

    def mixed_grad(i):
        r = tile(i, RT)
        do[r, :] = dot_nt(cot_v[r, :], wd[...]).astype(BF16)

    agenda.loop(T // RT, mixed_grad, 0.7)
    for w in in_doc:
        w()

    h0 = (lanes(128) % (2 * head)) < head
    h0w = jnp.concatenate([h0, h0], axis=1)
    rowh = lax.broadcasted_iota(jnp.int32, (128, 1), 0) < head
    block = rowh == h0w
    same = (rowh == h0).astype(BF16)
    one = jnp.ones((CH, 128), BF16)
    zero = jnp.zeros((), BF16)
    place = lanes(128) % head
    causal = lax.broadcasted_iota(jnp.int32, (CH, 1), 0) >= lanes(CH)

    def split(x):
        hi = x.astype(BF16)
        return hi, (x - hi.astype(F32)).astype(BF16)

    def masks(i):
        d = docc[tile(i, CH), :]
        inside = jnp.where(causal & (jnp.concatenate([d, d], axis=1) == docr[i]), 1.0, 0.0)
        start = lax.rem(i, seq // CH) == 0
        before = jnp.where(start, -1, docc[pl.ds(jnp.maximum(i * CH - 1, 0), 1), :])
        last = docc[pl.ds(i * CH + CH - 1, 1), :]
        ones = lambda x: jnp.where(x, 1.0, 0.0)
        return inside, ones(d == before), ones(d == last), ones(before == last)

    twice = lambda x: jnp.concatenate([x, x], axis=1)
    beside = lambda a, b: jnp.concatenate([a, b], axis=1)
    above = lambda a, b: jnp.concatenate([a, b], axis=0)
    same2 = above(same, same)

    def scores(q, k, m):
        s0 = dot_nt(jnp.where(h0, q, zero), k)
        s1 = dot_nt(jnp.where(h0, zero, q), k)
        return (s0 * m).astype(BF16), (s1 * m).astype(BF16)

    cur[...] = jnp.zeros_like(cur)

    def forward(i):
        r = tile(i, CH)
        m, cr, tr, kp = masks(i)
        cw, kpw = twice(cr), twice(kp)
        for j in range(npair):
            s = slice(j * 128, (j + 1) * 128)
            q, k, v = (qkv[r, x * width + s.start:x * width + s.stop] for x in range(3))
            va = jnp.concatenate([v, one], axis=1)
            p0, p1 = scores(q, k, m)
            state = cur[j]
            hi, lo = split(state)
            st[i, j, 0] = hi
            st[i, j, 1] = lo
            res = dot(beside(p0, p1), above(jnp.where(h0w, va, zero), jnp.where(h0w, zero, va))) + cw * dot(twice(q), above(hi, lo))
            rd = 1.0 / res[:, 128:]
            att = res[:, :128] * rd
            o[r, s] = att.astype(BF16)
            dnb = (do[r, s].astype(F32) * rd).astype(BF16)
            do[r, s] = dnb
            hi, lo = split(dnb.astype(F32) * att)
            hi, lo = split(-dot(beside(hi, lo), same2))
            dd[r, s] = jnp.where(place == 0, hi, jnp.where(place == 1, lo, zero))
            kt = (k.astype(F32) * tr).astype(BF16)
            cur[j] = kpw * state + jnp.where(block, dot_tn(kt, va), 0.0)
    agenda.loop(nch, forward, 1.95)

    def grad_dense(i):
        ad[...] = dot_tn(o[...], cot_v[...]).astype(BF16).reshape(ad.shape)

    agenda.loop(1, grad_dense, 3.0)

    cur[...] = jnp.zeros_like(cur)
    gf[...] = jnp.zeros_like(gf)

    def backward(ii):
        i = nch - 1 - ii
        r = tile(i, CH)
        ps = tile(lax.rem(i, seq // CH), CH)
        m, cr, tr, kp = masks(i)
        kpw = twice(kp)
        cos, sa, sb = cosp[ps, :], sina[ps, :], sinb[ps, :]

        def unfeature(d, f, s, base):
            de = d * f.astype(F32)
            gf[:, s] += jnp.sum(de.reshape(CH // 8, 8, 128), axis=0)
            g = dot(de.astype(BF16), mixt[...])
            g = g * cos + pltpu.roll(g * sa, 128 - half, 1) + pltpu.roll(g * sb, half, 1)
            qkv[r, base + s.start:base + s.stop] = g.astype(BF16)

        for j in range(npair):
            s = slice(j * 128, (j + 1) * 128)
            q, k, v = (qkv[r, x * width + s.start:x * width + s.stop] for x in range(3))
            va = jnp.concatenate([v, one], axis=1)
            p0, p1 = scores(q, k, m)
            dnb = do[r, s]
            dy = jnp.concatenate([dnb, dd[r, s]], axis=1)
            ds0 = (dot_nt(dy, jnp.where(h0w, va, zero)) * m).astype(BF16)
            ds1 = (dot_nt(dy, jnp.where(h0w, zero, va)) * m).astype(BF16)
            dst = cur[j]
            dhi, dlo = split(dst)
            dq = dot(beside(ds0, ds1), above(jnp.where(h0, k, zero), jnp.where(h0, zero, k))) + cr * dot_nt(
                twice(dy), beside(st[i, j, 0], st[i, j, 1])
            )
            dk = dot_tn(above(ds0, ds1), above(jnp.where(h0, q, zero), jnp.where(h0, zero, q))) + tr * dot_nt(twice(va), beside(dhi, dlo))
            dv = dot_tn(above(p0, p1), above(jnp.where(h0, dnb, zero), jnp.where(h0, zero, dnb))) + tr * dot(k, dhi[:, :128])
            qc = (q.astype(F32) * cr).astype(BF16)
            cur[j] = kpw * dst + jnp.where(block, dot_tn(qc, dy), 0.0)
            unfeature(dq, q, s, 0)
            unfeature(dk, k, s, width)
            qkv[r, 2 * width + s.start:2 * width + s.stop] = dv.astype(BF16)
    agenda.loop(nch, backward, 3.15)


    pl.semaphore_signal(free_d, inc=1, device_id=at.partner(), device_id_type=MESH)
    st_flat = st.reshape(st.shape[0] * st.shape[1] * 2 * 128, 256)

    def cut(ref, width, at_row=0):
        return [ref.at[pl.ds(at_row + k * S, S)] for k in range(D // width)]

    def fetch(src, parts):
        w = D // len(parts)
        return [put(src.at[:, pl.ds(k * w, w)], part) for k, part in enumerate(parts)]

    fetched = fetch(out2in, cut(st_flat, 256)) + fetch(dy2, cut(st_flat, 256, 4 * S))
    fetched.append(put(dy2in, cot_v.at[other_rows]))

    def grad_qkv(i):
        val = dot_tn(attn_v[...], qkv[:, tile(i, width)]).astype(BF16)
        aq[every + (slice(None), tile(i, width))] = val.reshape(aq.shape[:-1] + (width,))

    agenda.loop(3, grad_qkv, 2.4)
    sq, sdn = scatters(aq, hold_u, au), scatters(ad, hold_d)
    wait_u = once([lambda: wait_free(free_u)])
    ready = [(max(agenda.now, end_u + 2.0), wait_u)] * len(sq) + [(agenda.now, None)] * len(sdn)
    ends = agenda.add(sq + sdn, ready, [0] * len(sq) + [1] * len(sdn))
    end_q, end_d = max(ends[:len(sq)]), max(ends[len(sq):])

    def back_qkv(i, rows):
        r = tile(i + rows * (S // RT), RT)
        attn_v[r, :] = dot_nt(qkv[r, :], wq[...]).astype(BF16)

    def back_dense(i, rows):
        r = tile(i + rows * (S // RT), RT)
        qkv[r, :D] = dot(o[r, :], wd[...]).astype(BF16)

    def send_back(src, dst):
        return [
            swap(src.at[other_rows, pl.ds(k * width, width)], part, part) for k, part in enumerate(cut(dst, width))
        ]

    agenda.loop(S // RT, lambda i: back_qkv(i, p), 1.9)
    pl.semaphore_wait(free_d, 1)
    arrive = send_back(attn_v, do)
    agenda.loop(S // RT, lambda i: back_dense(i, p), 0.7)
    arrive += send_back(qkv, dd)
    agenda.loop(S // RT, lambda i: back_qkv(i, c), 1.9)
    fetched.append(put(out2, wq.at[pl.ds(0, S), pl.ds(0, D)]))
    agenda.loop(S // RT, lambda i: back_dense(i, c), 0.7)
    fetched += fetch(tok, cut(o, width))
    agenda.until(agenda.now)

    gv[0] = jnp.zeros((8, D), F32)
    for m in range(npair):
        s = slice(m * 128, (m + 1) * 128)
        gv[0, 4:5, pl.ds(pl.multiple_of((2 * m + c) * 128, 128), 128)] = jnp.sum(gf[:, s], axis=0, keepdims=True) / fw[:, s]
    for cp in fetched:
        cp.wait()
    for w in arrive:
        w()
    first = copies.count

    def stores(i):
        k, r = lax.rem(i, 2), tile(i, FT)
        return [
            pltpu.make_async_copy(outs.at[k], output.at[r], local.at[first + 2 * k]),
            pltpu.make_async_copy(igs.at[k], input_grad.at[r], local.at[first + 2 * k + 1]),
        ]

    def finish(i):
        k = lax.rem(i, 2)

        @pl.when(i >= 2)
        def _():
            for cp in stores(i - 2):
                cp.wait()

        def rows(t, sums):
            part = tile(t, 32)
            at_row = i * FT + t * 32
            own = pl.ds(pl.multiple_of(at_row + c * S, 32), 32)

            def joined(ref, n, base=0):
                return jnp.concatenate(
                    [ref[pl.ds(pl.multiple_of(at_row + base + q * S, 32), 32), :] for q in range(n)], axis=1
                ).astype(F32)

            here = pl.ds(pl.multiple_of(at_row, 32), 32)
            x = joined(o, D // width)
            n, rstd = normed(x)
            out1 = qkv[own, :D].astype(F32) + joined(dd, D // width)
            outs[k, part, :] = (x + out1 + (wq[here, :D].astype(F32) + joined(st_flat, D // 256))).astype(BF16)
            d1 = attn_v[own, :].astype(F32) + joined(do, D // width)
            d2 = joined(st_flat, D // 256, 4 * S) + cot_v[pl.ds(pl.multiple_of(at_row + p * S, 32), 32), :].astype(F32)
            dn = d1 * vec[0:1, :] + d2 * vec[2:3, :]
            dx = rstd * (dn - jnp.mean(dn, axis=-1, keepdims=True) - n * jnp.mean(dn * n, axis=-1, keepdims=True))
            igs[k, part, :] = cot_v[own, :].astype(F32) + dx
            fold = lambda y: jnp.sum(y.reshape(4, 8, D), axis=0)
            return tuple(a + fold(y) for a, y in zip(sums, (d1 * n, d1, d2 * n, d2)))

        sums = lax.fori_loop(0, FT // 32, rows, (jnp.zeros((8, D), F32),) * 4)
        for q, y in enumerate(sums):
            gv[0, q:q + 1, :] += jnp.sum(y, axis=0, keepdims=True)
        for cp in stores(i):
            cp.start()

    agenda.loop(S // FT, finish, 1.5)
    for i in range(S // FT - 2, S // FT):
        for cp in stores(i):
            cp.wait()

    peers = [at.partner()] + [at.across(b) for b in range(nb)]
    step = 1
    while step < nz:
        peers.append(at.fold(step))
        step *= 2
    rounds = []
    for k, peer in enumerate(peers):
        cp = sems.copy(gv.at[k], vh.at[k], sems.take(), peer)

        def arrive(cp=cp, k=k):
            cp.wait_recv()
            gv[k + 1] = gv[k] + vh[k]

        rounds.append((cp.start, arrive, cp.wait_send, "small", 4.0 * 8 * D))
    agenda.add([rounds], [(agenda.now, None)])
    me = at.slot(())
    sent = []
    for acc, hold, out, end, wide in ((aq, hq, oq, end_q, 128), (au, hu, ou, end_u, block_u)):
        half = hold.shape[0]
        cols = at.columns(acc, at.z)
        cp = sems.copy(acc.at[me + (tile(p, half), cols)], hold, sems.take(), at.partner())

        def place_columns(core, val, out=out, wide=wide):
            for t in range(val.shape[1] // wide):
                out[:, tile(2 * t + core, wide)] = val[:, t * wide:(t + 1) * wide].astype(F32)

        def act(cp=cp, acc=acc, half=half, cols=cols, place_columns=place_columns):
            cp.start()
            place_columns(c, acc[me + (tile(c, half), cols)])

        def arrive(cp=cp, hold=hold, place_columns=place_columns):
            cp.wait_recv()
            place_columns(p, hold[...])

        begin = max(end + 0.1, agenda.now)
        agenda.at(begin, act)
        agenda.at(begin + 4.0, arrive)
        sent.append(cp)

    def keep(acc, out):
        out[...] = acc[me + (slice(None), at.columns(acc, at.z))]

    agenda.at(max(end_d + 0.1, agenda.now), lambda: keep(ad, od))
    agenda.at(end_w + 0.1, lambda: keep(aw, ow))
    agenda.until(1e9)
    ovec[...] = gv[len(peers)]
    copies.leave()
    for cp in sent:
        cp.wait_send()
    for s in su + sw + sdn + sq + [rounds]:
        for r in s:
            r[2]()


def attend(nf, nz, head, rot, block_u, attn_in, cot2, bq, bd, gu, gw, out2, out2in, dy2, dy2in, tok, docc, docr, vec, fw, *tabs):
    sd = jax.ShapeDtypeStruct
    nb = (nf // 2).bit_length() - 1
    S, D = tok.shape
    T, W = 2 * S, D // 2
    own = lambda a: (a.shape[-2], a.shape[-1] // nz)

    def holds(a):
        shapes = []
        for _, size, order in streams_of(a.shape[-2], nb):
            shapes += hold_shapes(nz, nb, size, a.shape[-1], order)
        return shapes

    room = [holds(gu), holds(gw), holds(bd)]
    halves = [(own(a)[0] // 2, own(a)[1]) for a in (bq, gu)]
    nsteps = 1 + nb + nz.bit_length() - 1
    ncopies = 12 * copies_of(nz, nb) + 6 + nsteps + 2
    vm, hb = pl.BlockSpec(memory_space=pltpu.VMEM), pl.BlockSpec(memory_space=pl.ANY)
    v = lambda *shape: pltpu.VMEM(shape, BF16)
    f = lambda *shape: pltpu.VMEM(shape, F32)
    i32 = lambda *shape: pltpu.VMEM(shape, jnp.int32)
    outs = [sd((S, D), BF16), sd((S, D), F32)]
    outs += [sd((halves[0][0], 2 * halves[0][1]), F32), sd(own(bd), BF16), sd((halves[1][0], 2 * halves[1][1]), F32), sd(own(gw), BF16), sd((8, D), F32)]
    return pl.pallas_call(
        partial(attend_kernel, nf, nz, head, rot, block_u, tuple(len(r) for r in room)), out_shape=outs,
        in_specs=[hb] * 13 + [vm] * 7, out_specs=[hb] * 2 + [vm] * 5,
        scratch_shapes=[
            v(T, D), v(T, D), v(*bq.shape), v(*bd.shape), v(T, 3 * W), v(T, W), v(T, W), v(T, W),
            v(T // CH, W // 128, 2, 128, 256), f(W // 128, 128, 256), i32(T, 128), i32(2 * docr.shape[0], 1, CH),
            v(*bq.shape), v(*bd.shape), v(*gu.shape), v(*gw.shape),
        ]
        + [v(*s) for r in room for s in r] + [v(*s) for s in halves]
        + [f(nsteps + 1, 8, D), f(nsteps, 8, D), f(8, W), v(2, 128, D), f(2, 128, D)]
        + [pltpu.SemaphoreType.DMA((ncopies,)), pltpu.SemaphoreType.DMA((ncopies,)), pltpu.SemaphoreType.DMA((28,))]
        + [pltpu.SemaphoreType.REGULAR] * 2,
        compiler_params=pltpu.CompilerParams(collective_id=1, has_side_effects=True, vmem_limit_bytes=63 << 20),
        name="attend",
    )(attn_in, cot2, bq, bd, gu, gw, out2, out2in, dy2, dy2in, tok, docc, docr, vec, fw, *tabs)


def body(nf, nz, tokens, doc_starts, w_qkv, w_dense, w_up, w_down, norm1_gain, norm1_bias, norm2_gain, norm2_bias, feature_weight, cotangent):
    rows, D = tokens.shape
    unit = w_down.shape[0]

    block = unit
    if unit % 128:
        block = w_up.shape[1] // 2
        w_up = w_up.reshape(-1, block // unit, 2, unit).swapaxes(1, 2).reshape(w_up.shape)

    per = 128 // w_dense.shape[0]
    source = [(2 * (k // per) + c) * per + k % per for k in range(nf // 2) for c in range(2)]
    if per > 1:
        w_dense = lax.ppermute(w_dense, "fsdp", [(s, d) for d, s in enumerate(source)])

    doc = jnp.cumsum(doc_starts.reshape(-1, SEQ_LEN), axis=1).astype(jnp.int32).reshape(rows)
    vec = jnp.stack([norm1_gain, norm1_bias, norm2_gain, norm2_bias, feature_weight] + [jnp.zeros_like(norm1_gain)] * 3)
    cosp, sina, sinb, mix = tables(SEQ_LEN, ROT, HEAD, FEATS)
    mix = jnp.asarray(mix)
    mixh = mix.astype(BF16)
    mixl = (mix - mixh.astype(F32)).astype(BF16)
    attn_in, cot2, bq, bd, gu, gw, out2, out2in, dy2, dy2in, vec8, fw = feed(
        nf, nz, block, tokens, cotangent, vec, w_qkv, w_dense, w_up, w_down
    )
    output, input_grad, oq, od, ou, ow, gv = attend(
        nf, nz, HEAD, ROT, block, attn_in, cot2, bq, bd, gu, gw, out2, out2in, dy2, dy2in, tokens,
        jnp.broadcast_to(doc[:, None], (rows, 128)), doc.reshape(-1, 1, CH), vec8, fw, cosp, sina, sinb,
        jnp.concatenate([mixh, mixh, mixl]), mixh.T,
    )
    if per > 1:
        od = lax.ppermute(od, "fsdp", [(d, s) for d, s in enumerate(source)])
    if unit % 128:
        ou = ou.reshape(-1, 2, block // unit, unit).swapaxes(1, 2).reshape(ou.shape)
    own = gv.reshape(8, nf, -1)
    own = lax.dynamic_index_in_dim(own, lax.axis_index("fsdp"), 1, keepdims=False)
    return (
        output, input_grad,
        oq, od.astype(F32), ou, ow.astype(F32),
        own[0], own[1], own[2], own[3], own[4],
    )


def solution(mesh):
    nf, nz = mesh.shape["fsdp"], mesh.shape["inner"]
    rows, mat, vec = P(("fsdp", "inner"), None), P("fsdp", "inner"), P("fsdp")
    in_specs = (rows, P(("fsdp", "inner"))) + (mat,) * 4 + (vec,) * 5 + (rows,)
    out_specs = (rows, rows) + (mat,) * 4 + (vec,) * 5
    return jax.shard_map(partial(body, nf, nz), mesh=mesh, in_specs=in_specs, out_specs=out_specs, check_vma=False)
```
